256 devices in a mesh: uv: 32 (over y_hi, z, core), freq: 8 (over y_lo, x).
Axes of the slice: x: 4, y: 4 (y_hi: 2, y_lo: 2; y = y_hi * 2 + y_lo), z: 8, core: 2. Of those that a mesh axis runs over, the one named last changes fastest.
Arguments:
- visibility: float32 [8, 1024, 8, 128], P('freq', 'uv'), may hold values from -6 to 6
- uv_offset: float32 [8, 1024, 2, 128], P('freq', 'uv'), may hold values from -12 to 12
- w_offset: float32 [8, 1024, 128], P('freq', 'uv'), may hold values from -40 to 40
- taper: float32 [32, 32], replicated, may hold values from 0.2 to 1
- row_count: int32 [8, 1024], P('freq', 'uv'), may hold values from 1 to 128, as said below
- block_owner: int32 [8, 1024, 1], P('freq', 'uv'), may hold values from 0 to 31; in each aligned block of 32 rows (0 to 31, 32 to 63, ..., all dimensions but the last counted through in order) at most 2 rows name the same one
- block_slot: int32 [8, 1024], P('freq', 'uv'), may hold values from 0 to 15
- subgrid_offset: int32 [512, 2], P('uv'), may hold values from 0 to 96
Outputs:
- grid: float32 [4096, 8, 128], P(('uv', 'freq'))
The draws below stay inside these ranges and needn't reach their ends.
Inputs may be any that keep to these rules, and one draw needn't show every extreme that they name: `block_owner`: among the 32 blocks of one device at most 2 name the same owner, a bound that some block reaches of them. `row_count`: some block has all 128 rows live.
All inputs are finite; a program needn't handle non-finite values.
Results may differ from the reference program's by a relative error of at most 0.0003.
Values sent between devices are 32-bit elements; how exact they have to be, the bound alone decides.
A program may use at most 64 MiB of HBM per device.

```python
import math
import jax
import jax.numpy as jnp
import numpy as np
from jax import lax

SUB = 32
BLK = 128
NB_DEV = 32
SUB_DEV = 16
TILE = 128
OWNERS = 32
CAP = 2
NF = 8
NBT = 1024
SUBGRIDS = 512
N_UV = 32


def draw_row_count(key, part):
    counts = jax.random.randint(key, (NF, NBT), 1, BLK + 1, dtype=jnp.int32)
    return counts.at[0, 0].set(BLK)


def plant(values, key, least, top_value):
    shape = values.shape
    index_at = [jax.random.randint(jax.random.fold_in(key, axis), (), 0, shape[axis]) for axis in range(len(shape))]
    values = values.at[tuple(index_at)].set(least)
    longest = shape.index(max(shape))
    index_at[longest] = (index_at[longest] + 1) % shape[longest]
    return values.at[tuple(index_at)].set(top_value)


def shard_levels(key, dims, shards, low, top_value):
    gain, own = 1.0, jax.random.fold_in(key, 6)
    for position, shards_of in shards:
        draws = jnp.exp(jax.random.uniform(jax.random.fold_in(own, position), (shards_of,), jnp.float32, low / len(shards), top_value / len(shards)))
        gain = gain * jnp.repeat(draws, dims[position] // shards_of).reshape([-1 if axis == position else 1 for axis in range(len(dims))])
    return gain


def deal_out(stream_key, own, number, rows, number_of, top, most, slope):
    ranking = jax.random.permutation(stream_key, number_of)
    packed, usual = load_shares(number_of, rows * top, most, slope, True), load_shares(number_of, rows * top, most, slope, False)
    places = jnp.arange(number_of)

    def named(sizes, rotation):
        used = int((sizes > 0).sum())
        fixed = max(1, used // 4)
        passed = fixed + (places - fixed + rotation * (used - fixed)) % max(1, number_of - fixed)
        return jnp.zeros((number_of,), jnp.int32).at[ranking[jnp.where(places < fixed, places, passed)]].set(jnp.asarray(sizes, jnp.int32))

    sizes = jnp.where(number % 4 == 0, named(packed, number // 4), named(usual, number - number // 4 - 1))
    mixed = jax.random.permutation(jax.random.fold_in(own, 3), number_of)
    source_of, receiver = mixed[0:number_of // 2 * 2:2], mixed[1:number_of // 2 * 2:2]
    slack = jnp.minimum(sizes[source_of] - 1, most - sizes[receiver]) // 2
    slack = jnp.where((source_of == ranking[0]) | (receiver == ranking[0]) | (sizes[receiver] == 0), 0, jnp.maximum(slack, 0))
    passed = jax.random.randint(jax.random.fold_in(own, 4), (number_of // 2,), 0, 1 << 20) % (slack + 1)
    sizes = sizes.at[source_of].add(-passed).at[receiver].add(passed)
    members = jnp.searchsorted(jnp.cumsum(sizes), jnp.arange(rows * top), side="right").astype(jnp.int32)
    grid = members.reshape(top, rows).T
    grid = grid[jax.random.permutation(jax.random.fold_in(own, 1), rows)]
    rotation = jax.random.randint(jax.random.fold_in(own, 2), (rows, 1), 0, top)
    return jnp.take_along_axis(grid, (jnp.arange(top)[None, :] + rotation) % top, axis=1)


def load_shares(count, total, bound, slope, full):
    portions = [(1 << 20) // math.isqrt(rank ** slope) + 1 for rank in range(1, count + 1)]
    largest = bound if full else min(bound, max(-(-total // count), total * portions[0] // sum(portions)))
    least = 1 if total - largest >= count - 1 else 0
    holding, surplus = [largest] + [least] * (count - 1), total - largest - least * (count - 1)
    while surplus > 0:
        candidates = [i for i in range(1, count) if holding[i] < largest] or [i for i in range(1, count) if holding[i] < bound]
        whole, remaining = sum([portions[i] for i in candidates]), surplus
        for i in candidates:
            extra = min(bound - holding[i], max(1, remaining * portions[i] // whole), surplus)
            holding[i] = holding[i] + extra
            surplus = surplus - extra
    return np.array(holding)


def noise(stream_key, shape, scale, reach, split=(), kind=jnp.bfloat16):
    array = jax.random.normal(stream_key, shape, jnp.float32) * scale
    if len(split) > 0:
        array = shard_levels(stream_key, shape, split, -0.22, 0.18) * array
    return jnp.clip(array, min=-reach, max=reach).astype(kind)


def setup_inputs(seed: int = 0) -> dict:
    streams_of = jax.random.split(jax.random.key(seed), 9)
    visibility = noise(streams_of[0], (NF, NBT, 8, BLK), 1.0, 6.0, ((0, 8), (1, 32)), jnp.float32)
    uv_offset = jnp.clip(jax.random.uniform(streams_of[1], (NF, NBT, 2, BLK), jnp.float32, -12.0, 12.0) * shard_levels(streams_of[1], (NF, NBT, 2, BLK), ((0, 8), (1, 32)), -0.4, 0.0), -12.0, 12.0)
    w_offset = jnp.clip(jax.random.uniform(streams_of[2], (NF, NBT, BLK), jnp.float32, -40.0, 40.0) * shard_levels(streams_of[2], (NF, NBT, BLK), ((0, 8), (1, 32)), -0.4, 0.0), -40.0, 40.0)
    taper = jnp.clip(jax.random.uniform(streams_of[3], (SUB, SUB), jnp.float32, 0.2, 1.0), 0.2, 1.0)
    row_count = draw_row_count(jax.random.fold_in(streams_of[8], 71), 0)
    block_owner_keys = jax.random.split(jax.random.fold_in(streams_of[5], 1), NF * NBT // NB_DEV)
    block_owner_turns = jax.random.permutation(jax.random.fold_in(streams_of[5], 3), NF * NBT // NB_DEV)
    block_owner = jax.vmap(lambda own, number: deal_out(jax.random.fold_in(streams_of[5], 2), own, number, NB_DEV, OWNERS, 1, CAP, 2))(block_owner_keys, block_owner_turns).reshape((NF, NBT, 1))
    block_slot = plant(jax.random.randint(streams_of[6], (NF, NBT), 0, SUB_DEV), jax.random.fold_in(streams_of[6], 1), 0, SUB_DEV - 1).astype(jnp.int32)
    subgrid_offset = plant(jax.random.randint(streams_of[7], (SUBGRIDS, 2), 0, TILE - SUB + 1), jax.random.fold_in(streams_of[7], 1), 0, TILE - SUB).astype(jnp.int32)
    return dict(visibility=visibility, uv_offset=uv_offset, w_offset=w_offset, taper=taper, row_count=row_count, block_owner=block_owner, block_slot=block_slot, subgrid_offset=subgrid_offset)


field_width = 0.5

def phase_images(data, counts, taper):
    blk = data.shape[2]
    sub = taper.shape[0]
    pix = sub * sub
    index = jnp.arange(pix, dtype=jnp.int32)
    xs = (index % sub).astype(jnp.float32)
    ys = (index // sub).astype(jnp.float32)
    lpos = field_width * (xs - sub / 2) / sub
    mpos = field_width * (ys - sub / 2) / sub
    npos = 1.0 - jnp.sqrt(1.0 - lpos * lpos - mpos * mpos)
    live = (jnp.arange(blk, dtype=jnp.int32)[None, :] < counts[:, None]).astype(jnp.float32)
    theta = 2.0 * math.pi * (data[:, 8, :, None] * lpos + data[:, 9, :, None] * mpos + data[:, 10, :, None] * npos)
    real_part = data[:, 0:4] * live[:, None, :]
    imag_part = data[:, 4:8] * live[:, None, :]
    left = jnp.concatenate([jnp.concatenate([real_part, imag_part], 2), jnp.concatenate([imag_part, -real_part], 2)], 1)
    right = jnp.concatenate([jnp.cos(theta), jnp.sin(theta)], 1)
    images = jnp.einsum('gak,gkp->gap', left, right, precision=lax.Precision.HIGHEST)
    return images * (taper.reshape(pix) * (1.0 / math.sqrt(blk)))

def reference(visibility, uv_offset, w_offset, taper, row_count, block_owner, block_slot, subgrid_offset):
    blocks = NF * NBT
    data = jnp.concatenate([visibility, uv_offset, w_offset[:, :, None, :]], 2).reshape(blocks, 11, BLK)
    counts = row_count.reshape(blocks)
    group = math.gcd(blocks, 64)

    def one_group(pieces):
        return phase_images(pieces[0], pieces[1], taper)
    images = lax.map(one_group, (data.reshape(blocks // group, group, 11, BLK), counts.reshape(blocks // group, group)))
    images = images.reshape(blocks, 8, SUB, SUB)
    spectrum = jnp.fft.fft2(images[:, 0:4] + 1j * images[:, 4:8]) / SUB
    grids = jnp.concatenate([jnp.real(spectrum), jnp.imag(spectrum)], 1).astype(jnp.float32)
    owner = block_owner.reshape(blocks).astype(jnp.int32)
    subgrid = owner * SUB_DEV + block_slot.reshape(blocks).astype(jnp.int32)
    corner_row = subgrid_offset[subgrid, 0]
    corner_col = subgrid_offset[subgrid, 1]
    steps = jnp.arange(SUB, dtype=jnp.int32)
    rows = corner_row[:, None, None] + steps[None, :, None]
    cols = corner_col[:, None, None] + steps[None, None, :]
    flat = ((owner[:, None, None] * TILE + rows) * TILE + cols).reshape(-1).astype(jnp.int32)
    values = jnp.transpose(grids, (0, 2, 3, 1)).reshape(-1, 8)
    summed = jax.ops.segment_sum(values, flat, num_segments=N_UV * TILE * TILE)
    return jnp.transpose(summed.reshape(N_UV * TILE, TILE, 8), (0, 2, 1))
```

```python
import functools
import math

import jax
import jax.numpy as jnp
from jax import lax
from jax.experimental import pallas as pl
from jax.experimental.pallas import tpu as pltpu
from jax.sharding import PartitionSpec as P

SUB = 32
BLK = 128
TILE = 128
OWNERS = 32
GROUPS = 8
OWNED = 16
SLOTS = 64
ROWS = 24
MAX_GROUPS = 82

SIN_POLY = (
    6.283185302511503,
    -41.34170040531769,
    81.60513138580204,
    -76.7030153539128,
    42.02592698618416,
    -14.899846668691637,
    3.238137510515757,
)
COS_POLY = (
    0.9999999890590228,
    -19.739204499454026,
    64.93911745990036,
    -85.45013953095037,
    60.16763095136588,
    -25.96759924965491,
    6.528658162567069,
)


def sincos_turns(turns):
    f = turns - jnp.round(turns)
    z = f * f
    s = jnp.full_like(z, SIN_POLY[-1])
    c = jnp.full_like(z, COS_POLY[-1])
    for a, b in zip(SIN_POLY[-2::-1], COS_POLY[-2::-1]):
        s = s * z + a
        c = c * z + b
    return s * f, c


def split(x):
    hi = x.astype(jnp.bfloat16)
    lo = (x - hi.astype(jnp.float32)).astype(jnp.bfloat16)
    return hi, lo


def dot_nt(a, b):
    return lax.dot_general(a, b, (((1,), (1,)), ((), ())), preferred_element_type=jnp.float32)


def dot_nn(a, b):
    return lax.dot_general(a, b, (((1,), (0,)), ((), ())), preferred_element_type=jnp.float32)


def iota(shape, axis):
    return lax.broadcasted_iota(jnp.int32, shape, axis)


def exchange_kernel(
    inv, slot, count, vis, uvo, wo, got, info, send, recv, send_sem, recv_sem
):
    me = lax.axis_index("uv")
    barrier = pltpu.get_barrier_semaphore()

    def greet(k, carry):
        peer = lax.rem(me + k, OWNERS)
        pl.semaphore_signal(
            barrier, inc=1, device_id={"uv": peer}, device_id_type=pl.DeviceIdType.MESH
        )
        return carry

    lax.fori_loop(1, OWNERS, greet, 0)

    lane = iota((1, BLK), 1)

    def pack(o, carry):
        others = []
        for rank in range(2):
            entry = inv[2 * o + rank]
            used = entry > 0
            j = jnp.maximum(entry - 1, 0)
            send[pl.ds(o * ROWS + 8 * rank, 8), :] = jnp.where(used, vis[j], 0.0)
            live = jnp.where(used, count[j], 0)
            facts = jnp.where(lane == 0, slot[j], live).astype(jnp.float32)
            others += [uvo[j], wo[pl.ds(j, 1), :], facts]
        send[pl.ds(o * ROWS + 16, 8), :] = jnp.concatenate(others, 0)
        return carry

    lax.fori_loop(0, OWNERS, pack, 0)
    pl.semaphore_wait(barrier, OWNERS - 1)

    def copy_to(k):
        peer = lax.rem(me + k, OWNERS)
        return pltpu.make_async_remote_copy(
            src_ref=send.at[pl.ds(pl.multiple_of(peer * ROWS, 8), ROWS)],
            dst_ref=recv.at[pl.ds(pl.multiple_of(me * ROWS, 8), ROWS)],
            send_sem=send_sem.at[k],
            recv_sem=recv_sem.at[k],
            device_id={"uv": peer},
            device_id_type=pl.DeviceIdType.MESH,
        )

    def start(k, carry):
        copy_to(k).start()
        return carry

    lax.fori_loop(1, OWNERS, start, 0)
    own = pl.ds(pl.multiple_of(me * ROWS, 8), ROWS)
    recv[own, :] = send[own, :]

    def finish(k, carry):
        source = lax.rem(me + OWNERS - k, OWNERS)
        pltpu.make_async_remote_copy(
            src_ref=send.at[pl.ds(pl.multiple_of(source * ROWS, 8), ROWS)],
            dst_ref=recv.at[pl.ds(pl.multiple_of(source * ROWS, 8), ROWS)],
            send_sem=send_sem.at[k],
            recv_sem=recv_sem.at[k],
            device_id={"uv": source},
            device_id_type=pl.DeviceIdType.MESH,
        ).wait_recv()
        return carry

    lax.fori_loop(1, OWNERS, finish, 0)
    got[...] = recv[...]
    info[0:OWNERS, :] = recv[pl.ds(19, OWNERS, stride=ROWS), :].astype(jnp.int32)
    info[OWNERS:, :] = recv[pl.ds(23, OWNERS, stride=ROWS), :].astype(jnp.int32)

    def drain(k, carry):
        copy_to(k).wait_send()
        return carry

    lax.fori_loop(1, OWNERS, drain, 0)


def exchange(inv, slot, count, vis, uvo, wo):
    smem = pl.BlockSpec(memory_space=pltpu.SMEM)
    vmem = pl.BlockSpec(memory_space=pltpu.VMEM)
    return pl.pallas_call(
        exchange_kernel,
        out_shape=(
            jax.ShapeDtypeStruct((OWNERS * ROWS, BLK), jnp.float32),
            jax.ShapeDtypeStruct((SLOTS, BLK), jnp.int32),
        ),
        in_specs=[smem] * 3 + [vmem] * 3,
        out_specs=(vmem, vmem),
        scratch_shapes=[
            pltpu.VMEM((OWNERS * ROWS, BLK), jnp.float32),
            pltpu.VMEM((OWNERS * ROWS, BLK), jnp.float32),
            pltpu.SemaphoreType.DMA((OWNERS,)),
            pltpu.SemaphoreType.DMA((OWNERS,)),
        ],
        compiler_params=pltpu.CompilerParams(collective_id=0, has_side_effects=True),
        name="exchange",
    )(inv, slot, count, vis, uvo, wo)


N_PHASE = 216
ROW_B = 64
ROW_C = 192
ROW_M = 208
ROW_U = 216
ROW_V = 232
N_TRIG = 248


def grid_kernel(
    info,
    offset,
    taper,
    got,
    tile,
    total,
    base,
    slot_of,
    buf,
    ntab,
    sines,
    cosines,
    c_hi,
    c_lo,
    d_hi,
    d_lo,
    acc,
    acc_edge,
    spread,
):
    def clear_total(s, carry):
        total[s] = 0
        return carry

    lax.fori_loop(0, OWNED, clear_total, 0)

    def add_total(b, carry):
        s = info[b, 0]
        total[s] = total[s] + info[b, 1]
        return carry

    lax.fori_loop(0, SLOTS, add_total, 0)

    def place_slot(s, first):
        number = lax.div(total[s] + (BLK - 1), BLK)
        base[s] = first * BLK

        def name_group(i, carry):
            slot_of[first + i] = s
            return carry

        lax.fori_loop(0, number, name_group, 0)
        return first + number

    groups = lax.fori_loop(0, OWNED, place_slot, 0)

    def clear_group(g, carry):
        buf[g] = jnp.zeros((16, BLK), jnp.float32)
        return carry

    lax.fori_loop(0, groups + 2, clear_group, 0)
    lane8 = iota((8, BLK), 1)

    def compact(i, carry):
        others = got[pl.ds(i * ROWS + 16, 8), :]
        for rank in range(2):
            b = i + OWNERS * rank
            s = info[b, 0]
            n = info[b, 1]
            at = base[s]
            base[s] = at + n
            g = lax.div(at, BLK)
            shift = at - g * BLK
            vis = pltpu.roll(got[pl.ds(i * ROWS + 8 * rank, 8), :], shift, 1)
            rest = pltpu.roll(others if rank == 0 else pltpu.roll(others, 4, 0), shift, 1)
            here = (lane8 >= shift) & (lane8 < shift + n)
            after = lane8 < shift + n - BLK
            buf[g, 0:8, :] = jnp.where(here, vis, buf[g, 0:8, :])
            buf[g, 8:16, :] = jnp.where(here, rest, buf[g, 8:16, :])
            buf[g + 1, 0:8, :] = jnp.where(after, vis, buf[g + 1, 0:8, :])
            buf[g + 1, 8:16, :] = jnp.where(after, rest, buf[g + 1, 8:16, :])
        return carry

    lax.fori_loop(0, OWNERS, compact, 0)

    def n_of(a, b):
        l = b * (0.5 / SUB)
        m = a * (0.5 / SUB)
        return 1.0 - jnp.sqrt(1.0 - l * l - m * m)

    row = iota((8, BLK), 0).astype(jnp.float32)
    for a in range(8):
        ntab[a * 8 : a * 8 + 8, :] = n_of(float(a), row)
    for a in range(8, 17):
        for h in range(2):
            at = ROW_B + (a - 8) * 16 + 8 * h
            ntab[at : at + 8, :] = n_of(float(a), row + 8.0 * h)
    ntab[ROW_M : ROW_M + 8, :] = jnp.where(
        row < 2.0, 16 * 0.5 / SUB, n_of(16.0, jnp.full((8, BLK), 16.0, jnp.float32))
    )
    step0 = row * (0.5 / SUB)
    step1 = (row + 8.0) * (0.5 / SUB)

    for s in range(OWNED):
        acc[s] = jnp.zeros((2, BLK, 2 * BLK), jnp.float32)
        acc_edge[s] = jnp.zeros((16, BLK), jnp.float32)

    first_row = iota((8, BLK), 0) == 0
    halves = jnp.where(iota((8, BLK), 0) < 4, 1.0, -1.0)

    def one_group(g, carry):
        u = buf[g, 8:9, :]
        v = buf[g, 9:10, :]
        w = buf[g, 10:11, :]

        def keep(at, turns):
            s, c = sincos_turns(turns)
            sines[at : at + 8, :] = s
            cosines[at : at + 8, :] = c

        for at in range(0, ROW_M, 8):
            keep(at, w * ntab[at : at + 8, :])
        sub = iota((8, BLK), 0)
        keep(ROW_M, jnp.where(sub == 0, u, jnp.where(sub == 1, v, w)) * ntab[ROW_M : ROW_M + 8, :])
        keep(ROW_U, u * step0)
        keep(ROW_U + 8, u * step1)
        keep(ROW_V, v * step0)
        keep(ROW_V + 8, v * step1)

        cu0 = cosines[ROW_U : ROW_U + 8, :]
        cu1 = cosines[ROW_U + 8 : ROW_U + 16, :]
        su0 = sines[ROW_U : ROW_U + 8, :]
        su1 = sines[ROW_U + 8 : ROW_U + 16, :]
        cu2 = jnp.where(first_row, cosines[ROW_M : ROW_M + 1, :], cu0)
        su2 = jnp.where(first_row, sines[ROW_M : ROW_M + 1, :], su0)

        for a in range(17):
            if a < 8:
                p0 = slice(a * 8, a * 8 + 8)
                p1 = pl.ds(ROW_B + a, 8, stride=16)
                edge = slice(ROW_C + a, ROW_C + a + 1)
            elif a < 16:
                p0 = slice(ROW_B + (a - 8) * 16, ROW_B + (a - 8) * 16 + 8)
                p1 = slice(ROW_B + (a - 8) * 16 + 8, ROW_B + (a - 8) * 16 + 16)
                edge = slice(ROW_C + a, ROW_C + a + 1)
            else:
                p0 = slice(ROW_C, ROW_C + 8)
                p1 = slice(ROW_C + 8, ROW_C + 16)
                edge = slice(ROW_M + 2, ROW_M + 3)
            cw0, sw0 = cosines[p0, :], sines[p0, :]
            cw1, sw1 = cosines[p1, :], sines[p1, :]
            cw2 = jnp.where(first_row, cosines[edge, :], cw0)
            sw2 = jnp.where(first_row, sines[edge, :], sw0)
            cc, ss, sc, cs = cw1 * cu1, sw1 * su1, sw1 * cu1, cw1 * su1
            cos_rows = [cw0 * cu0 - sw0 * su0, cc - ss, cw2 * cu2 + sw2 * su2, cc + ss]
            sin_rows = [sw0 * cu0 + cw0 * su0, sc + cs, sw2 * cu2 - cw2 * su2, sc - cs]
            for part, rows in enumerate((cos_rows, sin_rows)):
                hi, lo = split(jnp.concatenate(rows, 0))
                c_hi[a * 32 : a * 32 + 32, part * BLK : part * BLK + BLK] = hi
                c_lo[a * 32 : a * 32 + 32, part * BLK : part * BLK + BLK] = lo

        vis = buf[g, 0:8, :]
        swapped = pltpu.roll(vis, 4, 0) * halves
        for a in range(17):
            if a < 16:
                cv = cosines[ROW_V + a : ROW_V + a + 1, :]
                sv = sines[ROW_V + a : ROW_V + a + 1, :]
                left = jnp.concatenate([vis * cv, swapped * sv], 0)
                right = jnp.concatenate([swapped * cv, vis * -sv], 0)
            else:
                cv = cosines[ROW_M + 1 : ROW_M + 2, :]
                sv = sines[ROW_M + 1 : ROW_M + 2, :]
                nothing = jnp.zeros((8, BLK), jnp.float32)
                left = jnp.concatenate([vis * cv - swapped * sv, nothing], 0)
                right = jnp.concatenate([swapped * cv + vis * sv, nothing], 0)
            for part, rows in enumerate((left, right)):
                hi, lo = split(rows)
                d_hi[a * 16 : a * 16 + 16, part * BLK : part * BLK + BLK] = hi
                d_lo[a * 16 : a * 16 + 16, part * BLK : part * BLK + BLK] = lo

        s = slot_of[g]
        for t in range(2):
            dh = d_hi[t * 128 : t * 128 + 128, :]
            dl = d_lo[t * 128 : t * 128 + 128, :]
            ch = c_hi[t * 256 : t * 256 + 256, :]
            cl = c_lo[t * 256 : t * 256 + 256, :]
            acc[s, t] += dot_nt(dh, ch) + dot_nt(dl, ch) + dot_nt(dh, cl)
        dh, dl = d_hi[256:272, :], d_lo[256:272, :]
        ch, cl = c_hi[512:544, :], c_lo[512:544, :]
        acc_edge[s, :, 0:32] += dot_nt(dh, ch) + dot_nt(dl, ch) + dot_nt(dh, cl)
        return carry

    lax.fori_loop(0, groups, one_group, 0)

    col = iota((SUB, 2 * BLK), 1) % SUB
    col = jnp.where(col < 16, col + 16, jnp.where(col == 16, 0, 32 - col))
    pick = (iota((SUB, 2 * BLK), 0) == col).astype(jnp.float32)
    wide = lax.dot_general(
        taper[...], pick, (((1,), (0,)), ((), ())), precision=lax.Precision.HIGHEST,
        preferred_element_type=jnp.float32,
    ) * (1.0 / math.sqrt(BLK))
    place = lax.div(iota((1, 2 * BLK), 1), SUB)

    xr = iota((SUB, BLK), 0)
    xr = jnp.where(xr < 16, xr + 16, jnp.where(xr == 16, 0, 32 - xr))
    kx = iota((SUB, BLK), 1)
    sx, cx = sincos_turns((xr * kx % SUB).astype(jnp.float32) * (1.0 / SUB))
    table_re = jnp.where(kx < SUB, cx * (1.0 / SUB), 0.0)
    table_im = jnp.where(kx < SUB, sx * (-1.0 / SUB), 0.0)

    for s in range(OWNED):
        pieces = []
        for y in range(SUB):
            a = abs(y - 16)
            if a == 16:
                x = jnp.concatenate([acc_edge[s, 0:8, :], jnp.zeros((8, BLK), jnp.float32)], 1)
            else:
                even = acc[s, a // 8, (a % 8) * 16 : (a % 8) * 16 + 8, :]
                odd = acc[s, a // 8, (a % 8) * 16 + 8 : (a % 8) * 16 + 16, :]
                x = even + odd if y >= 16 else even - odd
            pieces.append(x * jnp.where(place == a % 8, wide[y : y + 1, :], 0.0))
        x_hi, x_lo = split(jnp.concatenate(pieces, 0))
        right = offset[s, 1]
        spun = jnp.concatenate(
            [pltpu.roll(table_re, right, 1), pltpu.roll(table_im, right, 1)], 1
        )
        t_hi, t_lo = split(spun)
        t_hi = jnp.concatenate([t_hi] * 8, 0)
        t_lo = jnp.concatenate([t_lo] * 8, 0)
        z = dot_nn(x_hi, t_hi) + dot_nn(x_lo, t_hi) + dot_nn(x_hi, t_lo)
        z_re = z[:, 0:BLK].reshape(SUB, 8, BLK)
        z_im = z[:, BLK:].reshape(SUB, 8, BLK)
        for y in range(SUB):
            spread[s * 256 + y * 8 : s * 256 + y * 8 + 8, :] = (
                z_re[y] - pltpu.roll(z_im[y], 4, 0) * halves
            )

    lane = iota((1, OWNED * SUB), 1)
    corner = jnp.zeros((1, OWNED * SUB), jnp.int32)
    for s in range(OWNED):
        corner = jnp.where(lax.div(lane, SUB) == s, offset[s, 0], corner)
    ky = iota((TILE, OWNED * SUB), 0) - corner
    yy = iota((TILE, OWNED * SUB), 1) % SUB
    sy, cy = sincos_turns(((ky * yy) & (SUB - 1)).astype(jnp.float32) * (1.0 / SUB))
    inside = (ky >= 0) & (ky < SUB)
    h = jnp.concatenate([jnp.where(inside, cy, 0.0), jnp.where(inside, -sy, 0.0)], 0)
    h_hi, h_lo = split(h)
    for p in range(4):
        both = jnp.concatenate(
            [
                spread[pl.ds(p, OWNED * SUB, stride=8), :],
                spread[pl.ds(p + 4, OWNED * SUB, stride=8), :],
            ],
            1,
        )
        b_hi, b_lo = split(both)
        o = dot_nn(h_hi, b_hi) + dot_nn(h_hi, b_lo) + dot_nn(h_lo, b_hi)
        tile[:, p, :] = o[0:TILE, 0:BLK] - o[TILE:, BLK:]
        tile[:, p + 4, :] = o[0:TILE, BLK:] + o[TILE:, 0:BLK]


def grid_tile(info, offset, taper, got):
    smem = pl.BlockSpec(memory_space=pltpu.SMEM)
    vmem = pl.BlockSpec(memory_space=pltpu.VMEM)
    f32, bf16 = jnp.float32, jnp.bfloat16
    return pl.pallas_call(
        grid_kernel,
        out_shape=jax.ShapeDtypeStruct((TILE, 8, TILE), f32),
        in_specs=[smem, smem, vmem, vmem],
        out_specs=vmem,
        scratch_shapes=[
            pltpu.SMEM((OWNED,), jnp.int32),
            pltpu.SMEM((OWNED,), jnp.int32),
            pltpu.SMEM((MAX_GROUPS,), jnp.int32),
            pltpu.VMEM((MAX_GROUPS, 16, BLK), f32),
            pltpu.VMEM((N_PHASE, BLK), f32),
            pltpu.VMEM((N_TRIG, BLK), f32),
            pltpu.VMEM((N_TRIG, BLK), f32),
            pltpu.VMEM((544, 2 * BLK), bf16),
            pltpu.VMEM((544, 2 * BLK), bf16),
            pltpu.VMEM((272, 2 * BLK), bf16),
            pltpu.VMEM((272, 2 * BLK), bf16),
            pltpu.VMEM((OWNED, 2, BLK, 2 * BLK), f32),
            pltpu.VMEM((OWNED, 16, BLK), f32),
            pltpu.VMEM((OWNED * SUB * 8, BLK), f32),
        ],
        compiler_params=pltpu.CompilerParams(vmem_limit_bytes=48 * 1024 * 1024),
        name="grid_tile",
    )(info, offset, taper, got)


def sum_kernel(tile, out, recv, send_sem, recv_sem):
    me = lax.axis_index("freq")
    barrier = pltpu.get_barrier_semaphore()
    for k in range(1, GROUPS):
        pl.semaphore_signal(
            barrier,
            inc=1,
            device_id={"freq": lax.rem(me + k, GROUPS)},
            device_id_type=pl.DeviceIdType.MESH,
        )
    pl.semaphore_wait(barrier, GROUPS - 1)
    strip = TILE // GROUPS
    copies = []
    for k in range(1, GROUPS):
        peer = lax.rem(me + k, GROUPS)
        copy = pltpu.make_async_remote_copy(
            src_ref=tile.at[pl.ds(peer * strip, strip)],
            dst_ref=recv.at[k],
            send_sem=send_sem.at[k],
            recv_sem=recv_sem.at[k],
            device_id={"freq": peer},
            device_id_type=pl.DeviceIdType.MESH,
        )
        copy.start()
        copies.append(copy)
    value = tile[pl.ds(me * strip, strip)]
    for k in range(1, GROUPS):
        copies[k - 1].wait_recv()
        value = value + recv[k]
    out[...] = value
    for copy in copies:
        copy.wait_send()


def sum_over_freq(tile):
    vmem = pl.BlockSpec(memory_space=pltpu.VMEM)
    strip = TILE // GROUPS
    return pl.pallas_call(
        sum_kernel,
        out_shape=jax.ShapeDtypeStruct((strip, 8, TILE), jnp.float32),
        in_specs=[vmem],
        out_specs=vmem,
        scratch_shapes=[
            pltpu.VMEM((GROUPS, strip, 8, TILE), jnp.float32),
            pltpu.SemaphoreType.DMA((GROUPS,)),
            pltpu.SemaphoreType.DMA((GROUPS,)),
        ],
        compiler_params=pltpu.CompilerParams(collective_id=1, has_side_effects=True),
        name="sum_over_freq",
    )(tile)


def shards(
    visibility, uv_offset, w_offset, taper, row_count, block_owner, block_slot, subgrid_offset
):
    owner = block_owner[0, :, 0]
    blocks = owner.shape[0]
    index = jnp.arange(blocks, dtype=jnp.int32)
    same = (owner[:, None] == owner[None, :]) & (index[None, :] < index[:, None])
    target = 2 * owner + jnp.sum(same.astype(jnp.int32), axis=1)
    inv = jnp.sum(
        jnp.where(
            target[None, :] == jnp.arange(SLOTS, dtype=jnp.int32)[:, None], index[None, :] + 1, 0
        ),
        axis=1,
    )
    got, info = exchange(
        inv, block_slot[0], row_count[0], visibility[0], uv_offset[0], w_offset[0]
    )
    return sum_over_freq(grid_tile(info, subgrid_offset, taper, got))


def solution(mesh):
    placed = (
        P("freq", "uv", None, None),
        P("freq", "uv", None, None),
        P("freq", "uv", None),
        P(),
        P("freq", "uv"),
        P("freq", "uv", None),
        P("freq", "uv"),
        P("uv", None),
    )
    return jax.shard_map(
        shards, mesh=mesh, in_specs=placed, out_specs=P(("uv", "freq"), None, None), check_vma=False
    )
```

```python
import functools
import math

import jax
import jax.numpy as jnp
from jax import lax
from jax.experimental import pallas as pl
from jax.experimental.pallas import tpu as pltpu
from jax.sharding import PartitionSpec as P

SUB = 32
BLK = 128
TILE = 128
OWNERS = 32
GROUPS = 8
OWNED = 16
SLOTS = 64
ROWS = 24
MAX_GROUPS = 82

SIN_POLY = (
    4.442882919124345,
    -7.308245686509104,
    3.6063542184332804,
    -0.8461116503752865,
    0.10982451642699691,
)
COS_POLY = (
    1.4142135620618328,
    -6.97886410988463,
    5.7398815391730755,
    -1.8882749233647587,
    0.3322515355413188,
    -0.03450161282339655,
)


def horner(z, coefficients):
    value = z * coefficients[-1] + coefficients[-2]
    for c in coefficients[-3::-1]:
        value = value * z + c
    return value


def sincos_turns(turns):
    f = turns - jnp.round(turns)
    z = f * f
    s = horner(z, SIN_POLY) * f
    c = horner(z, COS_POLY)
    return s * c, 1.0 - s * s


def split(x):
    hi = x.astype(jnp.bfloat16)
    lo = (x - hi.astype(jnp.float32)).astype(jnp.bfloat16)
    return hi, lo


def dot_nt(a, b):
    return lax.dot_general(a, b, (((1,), (1,)), ((), ())), preferred_element_type=jnp.float32)


def dot_nn(a, b):
    return lax.dot_general(a, b, (((1,), (0,)), ((), ())), preferred_element_type=jnp.float32)


def iota(shape, axis):
    return lax.broadcasted_iota(jnp.int32, shape, axis)


def exchange_kernel(
    inv, slot, count, vis, uvo, wo, got, info, send, recv, send_sem, recv_sem
):
    me = lax.axis_index("uv")
    barrier = pltpu.get_barrier_semaphore()

    def greet(k, carry):
        peer = lax.rem(me + k, OWNERS)
        pl.semaphore_signal(
            barrier, inc=1, device_id={"uv": peer}, device_id_type=pl.DeviceIdType.MESH
        )
        return carry

    lax.fori_loop(1, OWNERS, greet, 0)

    lane = iota((1, BLK), 1)

    def pack(o, carry):
        others = []
        for rank in range(2):
            entry = inv[2 * o + rank]
            used = entry > 0
            j = jnp.maximum(entry - 1, 0)
            send[pl.ds(o * ROWS + 8 * rank, 8), :] = jnp.where(used, vis[j], 0.0)
            live = jnp.where(used, count[j], 0)
            facts = jnp.where(lane == 0, slot[j], live).astype(jnp.float32)
            others += [uvo[j], wo[pl.ds(j, 1), :], facts]
        send[pl.ds(o * ROWS + 16, 8), :] = jnp.concatenate(others, 0)
        return carry

    lax.fori_loop(0, OWNERS, pack, 0)
    pl.semaphore_wait(barrier, OWNERS - 1)

    def copy_to(k):
        peer = lax.rem(me + k, OWNERS)
        return pltpu.make_async_remote_copy(
            src_ref=send.at[pl.ds(pl.multiple_of(peer * ROWS, 8), ROWS)],
            dst_ref=recv.at[pl.ds(pl.multiple_of(me * ROWS, 8), ROWS)],
            send_sem=send_sem.at[k],
            recv_sem=recv_sem.at[k],
            device_id={"uv": peer},
            device_id_type=pl.DeviceIdType.MESH,
        )

    def start(k, carry):
        copy_to(k).start()
        return carry

    lax.fori_loop(1, OWNERS, start, 0)
    own = pl.ds(pl.multiple_of(me * ROWS, 8), ROWS)
    recv[own, :] = send[own, :]

    def finish(k, carry):
        source = lax.rem(me + OWNERS - k, OWNERS)
        pltpu.make_async_remote_copy(
            src_ref=send.at[pl.ds(pl.multiple_of(source * ROWS, 8), ROWS)],
            dst_ref=recv.at[pl.ds(pl.multiple_of(source * ROWS, 8), ROWS)],
            send_sem=send_sem.at[k],
            recv_sem=recv_sem.at[k],
            device_id={"uv": source},
            device_id_type=pl.DeviceIdType.MESH,
        ).wait_recv()
        return carry

    lax.fori_loop(1, OWNERS, finish, 0)
    got[...] = recv[...]
    info[0:OWNERS, :] = recv[pl.ds(19, OWNERS, stride=ROWS), :].astype(jnp.int32)
    info[OWNERS:, :] = recv[pl.ds(23, OWNERS, stride=ROWS), :].astype(jnp.int32)

    def drain(k, carry):
        copy_to(k).wait_send()
        return carry

    lax.fori_loop(1, OWNERS, drain, 0)


def exchange(inv, slot, count, vis, uvo, wo):
    smem = pl.BlockSpec(memory_space=pltpu.SMEM)
    vmem = pl.BlockSpec(memory_space=pltpu.VMEM)
    return pl.pallas_call(
        exchange_kernel,
        out_shape=(
            jax.ShapeDtypeStruct((OWNERS * ROWS, BLK), jnp.float32),
            jax.ShapeDtypeStruct((SLOTS, BLK), jnp.int32),
        ),
        in_specs=[smem] * 3 + [vmem] * 3,
        out_specs=(vmem, vmem),
        scratch_shapes=[
            pltpu.VMEM((OWNERS * ROWS, BLK), jnp.float32),
            pltpu.VMEM((OWNERS * ROWS, BLK), jnp.float32),
            pltpu.SemaphoreType.DMA((OWNERS,)),
            pltpu.SemaphoreType.DMA((OWNERS,)),
        ],
        compiler_params=pltpu.CompilerParams(collective_id=0, has_side_effects=True),
        name="exchange",
    )(inv, slot, count, vis, uvo, wo)


N_PHASE = 216
ROW_B = 64
ROW_C = 192
ROW_M = 208
ROW_U = 216
ROW_V = 232
N_TRIG = 248
TILE_A = (tuple(range(8)) + (16,), tuple(range(8, 16)))
C_ROWS = (0, 9 * 32, 17 * 32)


def phases(g, buf, ntab, sines, cosines, c_part, d_part):
    u = buf[g, 8:9, :]
    v = buf[g, 9:10, :]
    w = buf[g, 10:11, :]
    sub = iota((8, BLK), 0)
    row = sub.astype(jnp.float32)
    first_row = sub == 0
    halves = jnp.where(sub < 4, 1.0, -1.0)
    step0 = row * (0.5 / SUB)
    step1 = (row + 8.0) * (0.5 / SUB)

    def keep(at, turns):
        s, c = sincos_turns(turns)
        sines[at : at + 8, :] = s
        cosines[at : at + 8, :] = c

    keep(ROW_M, jnp.where(sub == 0, u, jnp.where(sub == 1, v, w)) * ntab[ROW_M : ROW_M + 8, :])
    keep(ROW_U, u * step0)
    keep(ROW_U + 8, u * step1)
    keep(ROW_V, v * step0)
    keep(ROW_V + 8, v * step1)
    for at in range(0, ROW_M, 8):
        keep(at, w * ntab[at : at + 8, :])

    vis = buf[g, 0:8, :]
    swapped = pltpu.roll(vis, 4, 0) * halves
    for t in range(2):
        cv = cosines[ROW_V + 8 * t : ROW_V + 8 * t + 8, :]
        sv = sines[ROW_V + 8 * t : ROW_V + 8 * t + 8, :]
        if t == 0:
            c16 = jnp.where(first_row, cosines[ROW_M + 1 : ROW_M + 2, :], 0.0)
            sv = jnp.where(first_row, -sines[ROW_M + 1 : ROW_M + 2, :], sv)
        for c in range(8):
            one = jnp.broadcast_to(vis[c : c + 1, :], (8, BLK))
            two = jnp.broadcast_to(swapped[c : c + 1, :], (8, BLK))
            at = t * 128 + c * 16
            left, right = two * sv, -(one * sv)
            if t == 0:
                left, right = left + one * c16, right + two * c16
            d_part[at : at + 8, 0:BLK] = one * cv
            d_part[at : at + 8, BLK:] = two * cv
            d_part[at + 8 : at + 16, 0:BLK] = left
            d_part[at + 8 : at + 16, BLK:] = right

    cu0 = cosines[ROW_U : ROW_U + 8, :]
    cu1 = cosines[ROW_U + 8 : ROW_U + 16, :]
    su0 = sines[ROW_U : ROW_U + 8, :]
    su1 = sines[ROW_U + 8 : ROW_U + 16, :]
    cu2 = jnp.where(first_row, cosines[ROW_M : ROW_M + 1, :], cu0)
    su2 = jnp.where(first_row, sines[ROW_M : ROW_M + 1, :], su0)
    for t in range(2):
        for i, a in enumerate(TILE_A[t]):
            if a < 8:
                p0 = slice(a * 8, a * 8 + 8)
                p1 = pl.ds(ROW_B + a, 8, stride=16)
                edge = slice(ROW_C + a, ROW_C + a + 1)
            elif a < 16:
                p0 = slice(ROW_B + (a - 8) * 16, ROW_B + (a - 8) * 16 + 8)
                p1 = slice(ROW_B + (a - 8) * 16 + 8, ROW_B + (a - 8) * 16 + 16)
                edge = slice(ROW_C + a, ROW_C + a + 1)
            else:
                p0 = slice(ROW_C, ROW_C + 8)
                p1 = slice(ROW_C + 8, ROW_C + 16)
                edge = slice(ROW_M + 2, ROW_M + 3)
            cw0, sw0 = cosines[p0, :], sines[p0, :]
            cw1, sw1 = cosines[p1, :], sines[p1, :]
            cw2 = jnp.where(first_row, cosines[edge, :], cw0)
            sw2 = jnp.where(first_row, sines[edge, :], sw0)
            cc, ss, sc, cs = cw1 * cu1, sw1 * su1, sw1 * cu1, cw1 * su1
            cos_rows = [cw0 * cu0 - sw0 * su0, cc - ss, cw2 * cu2 + sw2 * su2, cc + ss]
            sin_rows = [sw0 * cu0 + cw0 * su0, sc + cs, sw2 * cu2 - cw2 * su2, sc - cs]
            at = C_ROWS[t] + i * 32
            for part, rows in enumerate((cos_rows, sin_rows)):
                for k in range(4):
                    c_part[at + 8 * k : at + 8 * k + 8, part * BLK : part * BLK + BLK] = rows[k]


def add_images(s, c_part, d_part, acc):
    lane = iota((SUB, BLK), 1)
    for t in range(2):
        d_both = jnp.concatenate(split(d_part[t * 128 : t * 128 + 128, :]), 0)
        c_hi, c_lo = split(c_part[C_ROWS[t] : C_ROWS[t + 1], :])
        o_hi = dot_nt(c_hi, d_both)
        o_lo = dot_nt(c_lo, d_both)
        total = None
        for i, a in enumerate(TILE_A[t]):
            hi = o_hi[i * 32 : i * 32 + 32, :]
            lo = o_lo[i * 32 : i * 32 + 32, 0:BLK]
            value = hi[:, 0:BLK] + hi[:, BLK:] + lo
            if total is None:
                total = value
            elif a == 16:
                total = jnp.where((lane & 15) == 8, value, total)
            else:
                total = jnp.where((lane & 7) == i, value, total)
        acc[s, t] += total


def grid_kernel(
    info,
    offset,
    taper,
    got,
    tile,
    total,
    base,
    slot_of,
    buf,
    ntab,
    sines_0,
    cosines_0,
    c_0,
    d_0,
    sines_1,
    cosines_1,
    c_1,
    d_1,
    acc,
    spread,
):
    def clear_total(s, carry):
        total[s] = 0
        return carry

    lax.fori_loop(0, OWNED, clear_total, 0)

    def add_total(b, carry):
        s = info[b, 0]
        total[s] = total[s] + info[b, 1]
        return carry

    lax.fori_loop(0, SLOTS, add_total, 0)
    slot_of[0] = OWNED

    def place_slot(s, first):
        number = lax.div(total[s] + (BLK - 1), BLK)
        base[s] = first * BLK

        def name_group(i, carry):
            slot_of[first + i + 1] = s
            return carry

        lax.fori_loop(0, number, name_group, 0)
        return first + number

    groups = lax.fori_loop(0, OWNED, place_slot, 0)
    slot_of[groups + 1] = OWNED

    def clear_group(g, carry):
        buf[g] = jnp.zeros((16, BLK), jnp.float32)
        return carry

    lax.fori_loop(0, groups + 2, clear_group, 0)
    lane8 = iota((8, BLK), 1)

    def compact(k, carry):
        moved = []
        for i4 in range(4):
            i = k * 4 + i4
            others = got[pl.ds(i * ROWS + 16, 8), :]
            for rank in range(2):
                b = i + OWNERS * rank
                s = info[b, 0]
                n = info[b, 1]
                at = base[s]
                base[s] = at + n
                g = lax.shift_right_logical(at, 7)
                shift = at & (BLK - 1)
                vis = pltpu.roll(got[pl.ds(i * ROWS + 8 * rank, 8), :], shift, 1)
                rest = pltpu.roll(others if rank == 0 else pltpu.roll(others, 4, 0), shift, 1)
                here = (lane8 >= shift) & (lane8 < shift + n)
                after = lane8 < shift + n - BLK
                moved.append((g, vis, rest, here, after))
        for g, vis, rest, here, after in moved:
            buf[g, 0:8, :] = jnp.where(here, vis, buf[g, 0:8, :])
            buf[g, 8:16, :] = jnp.where(here, rest, buf[g, 8:16, :])
            buf[g + 1, 0:8, :] = jnp.where(after, vis, buf[g + 1, 0:8, :])
            buf[g + 1, 8:16, :] = jnp.where(after, rest, buf[g + 1, 8:16, :])
        return carry

    lax.fori_loop(0, OWNERS // 4, compact, 0)

    def n_of(a, b):
        l = b * (0.5 / SUB)
        m = a * (0.5 / SUB)
        return 1.0 - jnp.sqrt(1.0 - l * l - m * m)

    row = iota((8, BLK), 0).astype(jnp.float32)
    for a in range(8):
        ntab[a * 8 : a * 8 + 8, :] = n_of(float(a), row)
    for a in range(8, 17):
        for h in range(2):
            at = ROW_B + (a - 8) * 16 + 8 * h
            ntab[at : at + 8, :] = n_of(float(a), row + 8.0 * h)
    ntab[ROW_M : ROW_M + 8, :] = jnp.where(
        row < 2.0, 16 * 0.5 / SUB, n_of(16.0, jnp.full((8, BLK), 16.0, jnp.float32))
    )

    for s in range(OWNED):
        acc[s] = jnp.zeros((2, SUB, BLK), jnp.float32)

    def two_groups(i, carry):
        g = 2 * i
        phases(g, buf, ntab, sines_0, cosines_0, c_0, d_0)
        add_images(slot_of[g], c_1, d_1, acc)
        phases(g + 1, buf, ntab, sines_1, cosines_1, c_1, d_1)
        add_images(slot_of[g + 1], c_0, d_0, acc)
        return carry

    steps = lax.div(groups + 1, 2)
    lax.fori_loop(0, steps, two_groups, 0)
    add_images(slot_of[2 * steps], c_1, d_1, acc)

    def y_of(high, sign, low):
        i = high * 8 + low
        return jnp.where(sign == 0, 16 + i, jnp.where(i == 0, 0, 16 - i))

    def x_of(j):
        return jnp.where(j < 16, j + 16, jnp.where(j == 16, 0, 32 - j))

    def exact(a, b, dims):
        return lax.dot_general(
            a, b, (dims, ((), ())), precision=lax.Precision.HIGHEST,
            preferred_element_type=jnp.float32,
        )

    pick_x = (x_of(iota((SUB, SUB), 0)) == iota((SUB, SUB), 1)).astype(jnp.float32)
    place = iota((SUB, 2 * BLK), 1)
    pick_y = (
        y_of(lax.shift_right_logical(place, 7), lax.shift_right_logical(place, 3) & 1, place & 7)
        == iota((SUB, 2 * BLK), 0)
    ).astype(jnp.float32)
    weight = exact(exact(pick_x, taper[...], ((1,), (1,))), pick_y, ((1,), (0,))) * (
        1.0 / math.sqrt(BLK)
    )

    xr = x_of(iota((SUB, BLK), 0))
    kx = iota((SUB, BLK), 1)
    sx, cx = sincos_turns((xr * kx & (SUB - 1)).astype(jnp.float32) * (1.0 / SUB))
    table_re = jnp.where(kx < SUB, cx * (1.0 / SUB), 0.0)
    table_im = jnp.where(kx < SUB, sx * (-1.0 / SUB), 0.0)
    lane = iota((SUB, BLK), 1)
    even_lane = (lane & 8) == 0
    nothing = jnp.zeros((SUB, 2 * BLK), jnp.bfloat16)

    for q in range(OWNED // 4):
        rows = []
        for s in range(4 * q, 4 * q + 4):
            both = []
            for t in range(2):
                a = acc[s, t]
                y = jnp.where(even_lane, a + pltpu.roll(a, BLK - 8, 1), pltpu.roll(a, 8, 1) - a)
                if t == 0:
                    y = jnp.where((lane & 7) == 0, a, y)
                both.append(y)
            rows.append(jnp.concatenate(both, 1) * weight)
        image = jnp.transpose(jnp.concatenate(rows, 0))
        x_hi, x_lo = split(image)
        x_both = jnp.concatenate([x_hi, x_lo], 1)
        for j in range(4):
            s = 4 * q + j
            right = offset[s, 1]
            t_hi, t_lo = split(
                jnp.concatenate(
                    [pltpu.roll(table_re, right, 1), pltpu.roll(table_im, right, 1)], 1
                )
            )
            w_hi = jnp.concatenate([nothing] * j + [t_hi] + [nothing] * (3 - j), 0)
            w_lo = jnp.concatenate([nothing] * j + [t_lo] + [nothing] * (3 - j), 0)
            z = dot_nn(x_both, jnp.concatenate([w_hi, w_hi], 0)) + dot_nn(x_hi, w_lo)
            for t in range(2):
                for p in range(4):
                    re = z[t * 128 + p * 16 : t * 128 + p * 16 + 16, :]
                    im = z[t * 128 + p * 16 + 64 : t * 128 + p * 16 + 80, :]
                    at = s * SUB + t * 16
                    spread[p, at : at + 16, 0:BLK] = re[:, 0:BLK] - im[:, BLK:]
                    spread[p, at : at + 16, BLK:] = re[:, BLK:] + im[:, 0:BLK]

    lane = iota((1, OWNED * SUB), 1)
    corner = jnp.zeros((1, OWNED * SUB), jnp.int32)
    for s in range(OWNED):
        corner = jnp.where(lax.shift_right_logical(lane, 5) == s, offset[s, 0], corner)
    ky = iota((TILE, OWNED * SUB), 0) - corner
    yy = y_of(lax.shift_right_logical(lane, 4) & 1, lax.shift_right_logical(lane, 3) & 1, lane & 7)
    sy, cy = sincos_turns(((ky * yy) & (SUB - 1)).astype(jnp.float32) * (1.0 / SUB))
    inside = (ky >= 0) & (ky < SUB)
    h = jnp.concatenate([jnp.where(inside, cy, 0.0), jnp.where(inside, -sy, 0.0)], 0)
    h_hi, h_lo = split(h)
    for p in range(4):
        b_hi, b_lo = split(spread[p])
        o = dot_nn(h_hi, b_hi) + dot_nn(h_hi, b_lo) + dot_nn(h_lo, b_hi)
        tile[p] = o[0:TILE, 0:BLK] - o[TILE:, BLK:]
        tile[p + 4] = o[0:TILE, BLK:] + o[TILE:, 0:BLK]


def grid_tile(info, offset, taper, got):
    smem = pl.BlockSpec(memory_space=pltpu.SMEM)
    vmem = pl.BlockSpec(memory_space=pltpu.VMEM)
    f32 = jnp.float32
    factors = [
        pltpu.VMEM((N_TRIG, BLK), f32),
        pltpu.VMEM((N_TRIG, BLK), f32),
        pltpu.VMEM((C_ROWS[2], 2 * BLK), f32),
        pltpu.VMEM((256, 2 * BLK), f32),
    ]
    return pl.pallas_call(
        grid_kernel,
        out_shape=jax.ShapeDtypeStruct((8, TILE, TILE), f32),
        in_specs=[smem, smem, vmem, vmem],
        out_specs=vmem,
        scratch_shapes=[
            pltpu.SMEM((OWNED,), jnp.int32),
            pltpu.SMEM((OWNED,), jnp.int32),
            pltpu.SMEM((MAX_GROUPS + 2,), jnp.int32),
            pltpu.VMEM((MAX_GROUPS, 16, BLK), f32),
            pltpu.VMEM((N_PHASE, BLK), f32),
            *factors,
            *factors,
            pltpu.VMEM((OWNED + 1, 2, SUB, BLK), f32),
            pltpu.VMEM((4, OWNED * SUB, 2 * BLK), f32),
        ],
        compiler_params=pltpu.CompilerParams(vmem_limit_bytes=62 * 1024 * 1024),
        name="grid_tile",
    )(info, offset, taper, got)


def sum_kernel(tile, out, recv, send_sem, recv_sem):
    me = lax.axis_index("freq")
    barrier = pltpu.get_barrier_semaphore()
    for k in range(1, GROUPS):
        pl.semaphore_signal(
            barrier,
            inc=1,
            device_id={"freq": lax.rem(me + k, GROUPS)},
            device_id_type=pl.DeviceIdType.MESH,
        )
    pl.semaphore_wait(barrier, GROUPS - 1)
    strip = TILE // GROUPS
    copies = []
    for k in range(1, GROUPS):
        peer = lax.rem(me + k, GROUPS)
        copy = pltpu.make_async_remote_copy(
            src_ref=tile.at[:, pl.ds(pl.multiple_of(peer * strip, 8), strip)],
            dst_ref=recv.at[k],
            send_sem=send_sem.at[k],
            recv_sem=recv_sem.at[k],
            device_id={"freq": peer},
            device_id_type=pl.DeviceIdType.MESH,
        )
        copy.start()
        copies.append(copy)
    value = tile[:, pl.ds(pl.multiple_of(me * strip, 8), strip), :]
    for k in range(1, GROUPS):
        copies[k - 1].wait_recv()
        value = value + recv[k]
    for c in range(8):
        out[:, c, :] = value[c]
    for copy in copies:
        copy.wait_send()


def sum_over_freq(tile):
    vmem = pl.BlockSpec(memory_space=pltpu.VMEM)
    strip = TILE // GROUPS
    return pl.pallas_call(
        sum_kernel,
        out_shape=jax.ShapeDtypeStruct((strip, 8, TILE), jnp.float32),
        in_specs=[vmem],
        out_specs=vmem,
        scratch_shapes=[
            pltpu.VMEM((GROUPS, 8, strip, TILE), jnp.float32),
            pltpu.SemaphoreType.DMA((GROUPS,)),
            pltpu.SemaphoreType.DMA((GROUPS,)),
        ],
        compiler_params=pltpu.CompilerParams(collective_id=1, has_side_effects=True),
        name="sum_over_freq",
    )(tile)


def shards(
    visibility, uv_offset, w_offset, taper, row_count, block_owner, block_slot, subgrid_offset
):
    owner = block_owner[0, :, 0]
    blocks = owner.shape[0]
    index = jnp.arange(blocks, dtype=jnp.int32)
    same = (owner[:, None] == owner[None, :]) & (index[None, :] < index[:, None])
    target = 2 * owner + jnp.sum(same.astype(jnp.int32), axis=1)
    inv = jnp.sum(
        jnp.where(
            target[None, :] == jnp.arange(SLOTS, dtype=jnp.int32)[:, None], index[None, :] + 1, 0
        ),
        axis=1,
    )
    got, info = exchange(
        inv, block_slot[0], row_count[0], visibility[0], uv_offset[0], w_offset[0]
    )
    return sum_over_freq(grid_tile(info, subgrid_offset, taper, got))


def solution(mesh):
    placed = (
        P("freq", "uv", None, None),
        P("freq", "uv", None, None),
        P("freq", "uv", None),
        P(),
        P("freq", "uv"),
        P("freq", "uv", None),
        P("freq", "uv"),
        P("uv", None),
    )
    return jax.shard_map(
        shards, mesh=mesh, in_specs=placed, out_specs=P(("uv", "freq"), None, None), check_vma=False
    )
```

```python
import functools
import math

import jax
import jax.numpy as jnp
from jax import lax
from jax.experimental import pallas as pl
from jax.experimental.pallas import tpu as pltpu
from jax.sharding import PartitionSpec as P

SUB = 32
BLK = 128
TILE = 128
OWNERS = 32
GROUPS = 8
OWNED = 16
SLOTS = 64
ROWS = 24
MAX_GROUPS = 82

SIN_POLY = (
    4.442882919124345,
    -7.308245686509104,
    3.6063542184332804,
    -0.8461116503752865,
    0.10982451642699691,
)
COS_POLY = (
    1.4142134962552289,
    -6.978850948563853,
    5.7394603769076955,
    -1.8835579059892091,
    0.31068802753070307,
)


def horner(z, coefficients):
    value = z * coefficients[-1] + coefficients[-2]
    for c in coefficients[-3::-1]:
        value = value * z + c
    return value


def sincos_turns(turns):
    f = turns - jnp.round(turns)
    z = f * f
    s = horner(z, SIN_POLY) * f
    c = horner(z, COS_POLY)
    return s * c, 1.0 - s * s


def split(x):
    hi = x.astype(jnp.bfloat16)
    lo = (x - hi.astype(jnp.float32)).astype(jnp.bfloat16)
    return hi, lo


def dot_nt(a, b):
    return lax.dot_general(a, b, (((1,), (1,)), ((), ())), preferred_element_type=jnp.float32)


def dot_nn(a, b):
    return lax.dot_general(a, b, (((1,), (0,)), ((), ())), preferred_element_type=jnp.float32)


def iota(shape, axis):
    return lax.broadcasted_iota(jnp.int32, shape, axis)


def partner(me, i, sign):
    j = i // 4
    dz = jnp.where(j % 2 == 0, 4 + j // 2, 4 - (j + 1) // 2)
    dy = 1 - (i % 4) // 2
    dc = 1 - i % 2
    y = (me // 16 + dy) % 2
    z = (me // 2 + 8 + sign * dz) % 8
    return y * 16 + z * 2 + (me + dc) % 2


def exchange_kernel(
    owner, slot, count, vis, uvo, wo, got, info, send, recv, send_sem, recv_sem
):
    me = lax.axis_index("uv")
    barrier = pltpu.get_barrier_semaphore()

    def greet(k, carry):
        peer = partner(me, k, 1)
        pl.semaphore_signal(
            barrier, inc=1, device_id={"uv": peer}, device_id_type=pl.DeviceIdType.MESH
        )
        return carry

    lax.fori_loop(0, OWNERS - 1, greet, 0)

    size = vis.shape[0]
    mine = owner[...].astype(jnp.float32)
    across = jnp.broadcast_to(mine, (size, size))
    row, col = iota((size, size), 0), iota((size, size), 1)
    down = jnp.sum(jnp.where(row == col, across, 0.0), axis=1, keepdims=True)
    earlier = jnp.where((down == across) & (row < col), 1.0, 0.0)
    target = mine + OWNERS * jnp.sum(earlier, axis=0, keepdims=True)
    pick = jnp.where(iota((SLOTS, size), 0).astype(jnp.float32) == target, 1.0, 0.0)
    slots = jnp.sum(pick * slot[...].astype(jnp.float32), axis=1, keepdims=True)
    counts = jnp.sum(pick * count[...].astype(jnp.float32), axis=1, keepdims=True)
    lane = iota((SLOTS, BLK), 1)
    facts = jnp.where(lane == 0, slots, jnp.where(lane == 1, counts, 0.0))
    data = jnp.concatenate(
        [vis[:, c, :] for c in range(8)] + [uvo[:, 0, :], uvo[:, 1, :], wo[...]], 1
    )
    hi = data.astype(jnp.bfloat16)
    rest = data - hi.astype(jnp.float32)
    mid, lo = split(rest)
    pick = pick.astype(jnp.bfloat16)
    moved = dot_nn(jnp.concatenate([pick] * 3, 1), jnp.concatenate([hi, mid, lo], 0))
    for rank in range(2):
        part = slice(rank * OWNERS, rank * OWNERS + OWNERS)
        for c in range(12):
            value = moved[part, c * BLK : c * BLK + BLK] if c < 11 else facts[part, :]
            at = 8 * rank + c if c < 8 else 16 + 4 * rank + c - 8
            send[pl.ds(at, OWNERS, stride=ROWS), :] = value

    pl.semaphore_wait(barrier, OWNERS - 1)

    def copy_to(k):
        peer = partner(me, k, 1)
        return pltpu.make_async_remote_copy(
            src_ref=send.at[pl.ds(pl.multiple_of(peer * ROWS, 8), ROWS)],
            dst_ref=recv.at[pl.ds(pl.multiple_of(me * ROWS, 8), ROWS)],
            send_sem=send_sem.at[k],
            recv_sem=recv_sem.at[k],
            device_id={"uv": peer},
            device_id_type=pl.DeviceIdType.MESH,
        )

    def start(k, carry):
        copy_to(k).start()
        return carry

    lax.fori_loop(0, OWNERS - 1, start, 0)
    own = pl.ds(pl.multiple_of(me * ROWS, 8), ROWS)
    recv[own, :] = send[own, :]

    def finish(k, carry):
        source = partner(me, k, -1)
        pltpu.make_async_remote_copy(
            src_ref=send.at[pl.ds(pl.multiple_of(source * ROWS, 8), ROWS)],
            dst_ref=recv.at[pl.ds(pl.multiple_of(source * ROWS, 8), ROWS)],
            send_sem=send_sem.at[k],
            recv_sem=recv_sem.at[k],
            device_id={"uv": source},
            device_id_type=pl.DeviceIdType.MESH,
        ).wait_recv()
        return carry

    lax.fori_loop(0, OWNERS - 1, finish, 0)
    got[...] = recv[...]
    known = jnp.concatenate(
        [recv[pl.ds(19, OWNERS, stride=ROWS), :], recv[pl.ds(23, OWNERS, stride=ROWS), :]]
        + [jnp.zeros((BLK - SLOTS, BLK), jnp.float32)],
        0,
    )
    info[...] = jnp.transpose(known)[0:8, :].astype(jnp.int32)

    def drain(k, carry):
        copy_to(k).wait_send()
        return carry

    lax.fori_loop(0, OWNERS - 1, drain, 0)


def exchange(owner, slot, count, vis, uvo, wo):
    vmem = pl.BlockSpec(memory_space=pltpu.VMEM)
    return pl.pallas_call(
        exchange_kernel,
        out_shape=(
            jax.ShapeDtypeStruct((OWNERS * ROWS, BLK), jnp.float32),
            jax.ShapeDtypeStruct((8, BLK), jnp.int32),
        ),
        in_specs=[vmem] * 6,
        out_specs=(vmem, vmem),
        scratch_shapes=[
            pltpu.VMEM((OWNERS * ROWS, BLK), jnp.float32),
            pltpu.VMEM((OWNERS * ROWS, BLK), jnp.float32),
            pltpu.SemaphoreType.DMA((OWNERS,)),
            pltpu.SemaphoreType.DMA((OWNERS,)),
        ],
        compiler_params=pltpu.CompilerParams(
            collective_id=0, has_side_effects=True, vmem_limit_bytes=62 * 1024 * 1024
        ),
        name="exchange",
    )(owner, slot, count, vis, uvo, wo)


N_PHASE = 216
ROW_B = 64
ROW_C = 192
ROW_M = 208
ROW_U = 216
ROW_V = 232
ROW_E = 248
N_TRIG = 272
TILE_A = (tuple(range(8)) + (16,), tuple(range(8, 16)))
C_ROWS = (0, 9 * 32, 17 * 32)


def phases(g, buf, ntab, sines, cosines, c_part, d_part):
    u = buf[g, 8:9, :]
    v = buf[g, 9:10, :]
    w = buf[g, 10:11, :]
    sub = iota((8, BLK), 0)
    row = sub.astype(jnp.float32)
    first_row = sub == 0
    halves = jnp.where(sub < 4, 1.0, -1.0)
    step0 = row * (0.5 / SUB)
    step1 = (row + 8.0) * (0.5 / SUB)

    def keep(at, turns):
        s, c = sincos_turns(turns)
        sines[at : at + 8, :] = s
        cosines[at : at + 8, :] = c

    keep(ROW_M, jnp.where(sub == 0, u, jnp.where(sub == 1, v, w)) * ntab[ROW_M : ROW_M + 8, :])
    keep(ROW_U, u * step0)
    keep(ROW_U + 8, u * step1)
    keep(ROW_V, v * step0)
    keep(ROW_V + 8, v * step1)
    for at in range(0, ROW_M, 8):
        keep(at, w * ntab[at : at + 8, :])

    vis = buf[g, 0:8, :]
    swapped = pltpu.roll(vis, 4, 0) * halves
    for t in range(2):
        cv = cosines[ROW_V + 8 * t : ROW_V + 8 * t + 8, :]
        sv = sines[ROW_V + 8 * t : ROW_V + 8 * t + 8, :]
        if t == 0:
            c16 = jnp.where(first_row, cosines[ROW_M + 1 : ROW_M + 2, :], 0.0)
            sv = jnp.where(first_row, -sines[ROW_M + 1 : ROW_M + 2, :], sv)
        less = -sv
        for c in range(8):
            one = jnp.broadcast_to(vis[c : c + 1, :], (8, BLK))
            two = jnp.broadcast_to(swapped[c : c + 1, :], (8, BLK))
            at = t * 128 + c * 16
            left, right = two * sv, one * less
            if t == 0:
                left, right = left + one * c16, right + two * c16
            d_part[at : at + 8, 0:BLK] = one * cv
            d_part[at : at + 8, BLK:] = two * cv
            d_part[at + 8 : at + 16, 0:BLK] = left
            d_part[at + 8 : at + 16, BLK:] = right

    cu0 = cosines[ROW_U : ROW_U + 8, :]
    cu1 = cosines[ROW_U + 8 : ROW_U + 16, :]
    su0 = sines[ROW_U : ROW_U + 8, :]
    su1 = sines[ROW_U + 8 : ROW_U + 16, :]
    c16 = cosines[ROW_M : ROW_M + 1, :]
    s16 = sines[ROW_M : ROW_M + 1, :]
    for at, to in ((ROW_C, ROW_E), (ROW_C + 8, ROW_E + 8), (ROW_M, ROW_E + 16)):
        c, s = cosines[at : at + 8, :], sines[at : at + 8, :]
        cosines[to : to + 8, :] = c * c16 + s * s16
        sines[to : to + 8, :] = s * c16 - c * s16
    for t in range(2):
        for i, a in enumerate(TILE_A[t]):
            edge = slice(ROW_E + a, ROW_E + a + 1)
            if a < 8:
                p0 = slice(a * 8, a * 8 + 8)
                p1 = pl.ds(ROW_B + a, 8, stride=16)
            elif a < 16:
                p0 = slice(ROW_B + (a - 8) * 16, ROW_B + (a - 8) * 16 + 8)
                p1 = slice(ROW_B + (a - 8) * 16 + 8, ROW_B + (a - 8) * 16 + 16)
            else:
                p0 = slice(ROW_C, ROW_C + 8)
                p1 = slice(ROW_C + 8, ROW_C + 16)
                edge = slice(ROW_E + 18, ROW_E + 19)
            cw0, sw0 = cosines[p0, :], sines[p0, :]
            cw1, sw1 = cosines[p1, :], sines[p1, :]
            cc0, ss0, sc0, cs0 = cw0 * cu0, sw0 * su0, sw0 * cu0, cw0 * su0
            cc1, ss1, sc1, cs1 = cw1 * cu1, sw1 * su1, sw1 * cu1, cw1 * su1
            cos_2 = jnp.where(first_row, cosines[edge, :], cc0 + ss0)
            sin_2 = jnp.where(first_row, sines[edge, :], sc0 - cs0)
            cos_rows = [cc0 - ss0, cc1 - ss1, cos_2, cc1 + ss1]
            sin_rows = [sc0 + cs0, sc1 + cs1, sin_2, sc1 - cs1]
            at = C_ROWS[t] + i * 32
            for part, rows in enumerate((cos_rows, sin_rows)):
                for k in range(4):
                    c_part[at + 8 * k : at + 8 * k + 8, part * BLK : part * BLK + BLK] = rows[k]


def add_images(s, c_part, d_part, acc):
    lane = iota((SUB, BLK), 1)
    for t in range(2):
        d_both = jnp.concatenate(split(d_part[t * 128 : t * 128 + 128, :]), 0)
        c_hi, c_lo = split(c_part[C_ROWS[t] : C_ROWS[t + 1], :])
        o_hi = dot_nt(c_hi, d_both)
        o_lo = dot_nt(c_lo, d_both)
        total = None
        for i, a in enumerate(TILE_A[t]):
            hi = o_hi[i * 32 : i * 32 + 32, :]
            lo = o_lo[i * 32 : i * 32 + 32, 0:BLK]
            value = hi[:, 0:BLK] + hi[:, BLK:] + lo
            if total is None:
                total = value
            elif a == 16:
                total = jnp.where((lane & 15) == 8, value, total)
            else:
                total = jnp.where((lane & 7) == i, value, total)
        acc[s, t] += total


def grid_kernel(
    info,
    offset,
    taper,
    got,
    tile,
    total,
    base,
    slot_of,
    buf,
    ntab,
    sines_0,
    cosines_0,
    c_0,
    d_0,
    sines_1,
    cosines_1,
    c_1,
    d_1,
    acc,
    spread,
):
    def clear_total(s, carry):
        total[s] = 0
        return carry

    lax.fori_loop(0, OWNED, clear_total, 0)

    def add_total(b, carry):
        s = info[0, b]
        total[s] = total[s] + info[1, b]
        return carry

    lax.fori_loop(0, SLOTS, add_total, 0)
    slot_of[0] = OWNED

    def place_slot(s, first):
        number = lax.div(total[s] + (BLK - 1), BLK)
        base[s] = first * BLK

        def name_group(i, carry):
            slot_of[first + i + 1] = s
            return carry

        lax.fori_loop(0, number, name_group, 0)
        return first + number

    groups = lax.fori_loop(0, OWNED, place_slot, 0)
    slot_of[groups + 1] = OWNED

    def clear_group(g, carry):
        buf[g] = jnp.zeros((16, BLK), jnp.float32)
        return carry

    lax.fori_loop(0, groups + 2, clear_group, 0)
    lane8 = iota((8, BLK), 1)

    def compact(k, carry):
        moved = []
        for i4 in range(4):
            i = k * 4 + i4
            others = got[pl.ds(i * ROWS + 16, 8), :]
            for rank in range(2):
                b = i + OWNERS * rank
                s = info[0, b]
                n = info[1, b]
                at = base[s]
                base[s] = at + n
                g = lax.shift_right_logical(at, 7)
                shift = at & (BLK - 1)
                vis = pltpu.roll(got[pl.ds(i * ROWS + 8 * rank, 8), :], shift, 1)
                rest = pltpu.roll(others if rank == 0 else pltpu.roll(others, 4, 0), shift, 1)
                here = (lane8 >= shift) & (lane8 < shift + n)
                after = lane8 < shift + n - BLK
                moved.append((g, vis, rest, here, after))
        for g, vis, rest, here, after in moved:
            buf[g, 0:8, :] = jnp.where(here, vis, buf[g, 0:8, :])
            buf[g, 8:16, :] = jnp.where(here, rest, buf[g, 8:16, :])
            buf[g + 1, 0:8, :] = jnp.where(after, vis, buf[g + 1, 0:8, :])
            buf[g + 1, 8:16, :] = jnp.where(after, rest, buf[g + 1, 8:16, :])
        return carry

    lax.fori_loop(0, OWNERS // 4, compact, 0)

    def n_of(a, b):
        l = b * (0.5 / SUB)
        m = a * (0.5 / SUB)
        return 1.0 - jnp.sqrt(1.0 - l * l - m * m)

    row = iota((8, BLK), 0).astype(jnp.float32)
    for a in range(8):
        ntab[a * 8 : a * 8 + 8, :] = n_of(float(a), row)
    for a in range(8, 17):
        for h in range(2):
            at = ROW_B + (a - 8) * 16 + 8 * h
            ntab[at : at + 8, :] = n_of(float(a), row + 8.0 * h)
    ntab[ROW_M : ROW_M + 8, :] = jnp.where(
        row < 2.0, 16 * 0.5 / SUB, n_of(16.0, jnp.full((8, BLK), 16.0, jnp.float32))
    )

    for s in range(OWNED):
        acc[s] = jnp.zeros((2, SUB, BLK), jnp.float32)

    def two_groups(i, carry):
        g = 2 * i
        phases(g, buf, ntab, sines_0, cosines_0, c_0, d_0)
        add_images(slot_of[g], c_1, d_1, acc)
        phases(g + 1, buf, ntab, sines_1, cosines_1, c_1, d_1)
        add_images(slot_of[g + 1], c_0, d_0, acc)
        return carry

    steps = lax.div(groups + 1, 2)
    lax.fori_loop(0, steps, two_groups, 0)
    add_images(slot_of[2 * steps], c_1, d_1, acc)

    def y_of(high, sign, low):
        i = high * 8 + low
        return jnp.where(sign == 0, 16 + i, jnp.where(i == 0, 0, 16 - i))

    def x_of(j):
        return jnp.where(j < 16, j + 16, jnp.where(j == 16, 0, 32 - j))

    def exact(a, b, dims):
        return lax.dot_general(
            a, b, (dims, ((), ())), precision=lax.Precision.HIGHEST,
            preferred_element_type=jnp.float32,
        )

    pick_x = (x_of(iota((SUB, SUB), 0)) == iota((SUB, SUB), 1)).astype(jnp.float32)
    place = iota((SUB, 2 * BLK), 1)
    pick_y = (
        y_of(lax.shift_right_logical(place, 7), lax.shift_right_logical(place, 3) & 1, place & 7)
        == iota((SUB, 2 * BLK), 0)
    ).astype(jnp.float32)
    weight = exact(exact(pick_x, taper[...], ((1,), (1,))), pick_y, ((1,), (0,))) * (
        1.0 / math.sqrt(BLK)
    )

    row, col = iota((BLK, BLK), 0), iota((BLK, BLK), 1)
    turn = (x_of(row & (SUB - 1)) * (col & (SUB - 1))) & (SUB - 1)
    sx, cx = sincos_turns(turn.astype(jnp.float32) * (1.0 / SUB))
    same = lax.shift_right_logical(row, 5) == lax.shift_right_logical(col, 5)
    w_hi, w_lo = split(
        jnp.concatenate(
            [jnp.where(same, cx * (1.0 / SUB), 0.0), jnp.where(same, sx * (-1.0 / SUB), 0.0)], 1
        )
    )
    w_all = jnp.concatenate([w_hi, w_hi, w_lo], 0)
    lane = iota((SUB, BLK), 1)
    even_lane = (lane & 8) == 0
    lane16 = iota((16, BLK), 1)

    for q in range(OWNED // 4):
        rows = []
        for s in range(4 * q, 4 * q + 4):
            both = []
            for t in range(2):
                a = acc[s, t]
                y = jnp.where(even_lane, a + pltpu.roll(a, BLK - 8, 1), pltpu.roll(a, 8, 1) - a)
                if t == 0:
                    y = jnp.where((lane & 7) == 0, a, y)
                both.append(y)
            rows.append(jnp.concatenate(both, 1) * weight)
        x_hi, x_lo = split(jnp.transpose(jnp.concatenate(rows, 0)))
        z = dot_nn(jnp.concatenate([x_hi, x_lo, x_hi], 1), w_all)
        rights = [offset[1, 4 * q + j] for j in range(4)]
        inside = [(lane16 >= right) & (lane16 < right + SUB) for right in rights]
        for t in range(2):
            for p in range(4):
                re = z[t * 128 + p * 16 : t * 128 + p * 16 + 16, :]
                im = z[t * 128 + p * 16 + 64 : t * 128 + p * 16 + 80, :]
                joined = (re[:, 0:BLK] - im[:, BLK:], re[:, BLK:] + im[:, 0:BLK])
                for j in range(4):
                    at = (4 * q + j) * SUB + t * 16
                    shift = (rights[j] + (BLK - SUB * j)) & (BLK - 1)
                    for part in range(2):
                        spread[p, at : at + 16, part * BLK : part * BLK + BLK] = jnp.where(
                            inside[j], pltpu.roll(joined[part], shift, 1), 0.0
                        )

    lane = iota((1, OWNED * SUB), 1)
    corner = jnp.zeros((1, OWNED * SUB), jnp.int32)
    for s in range(OWNED):
        corner = jnp.where(lax.shift_right_logical(lane, 5) == s, offset[0, s], corner)
    ky = iota((TILE, OWNED * SUB), 0) - corner
    yy = y_of(lax.shift_right_logical(lane, 4) & 1, lax.shift_right_logical(lane, 3) & 1, lane & 7)
    sy, cy = sincos_turns(((ky * yy) & (SUB - 1)).astype(jnp.float32) * (1.0 / SUB))
    inside = (ky >= 0) & (ky < SUB)
    h = jnp.concatenate([jnp.where(inside, cy, 0.0), jnp.where(inside, -sy, 0.0)], 0)
    h_hi, h_lo = split(h)
    h_all = jnp.concatenate([h_hi, h_hi, h_lo], 1)
    for p in range(4):
        b_hi, b_lo = split(spread[p])
        o = dot_nn(h_all, jnp.concatenate([b_hi, b_lo, b_hi], 0))
        tile[p] = o[0:TILE, 0:BLK] - o[TILE:, BLK:]
        tile[p + 4] = o[0:TILE, BLK:] + o[TILE:, 0:BLK]


def grid_tile(info, offset, taper, got):
    smem = pl.BlockSpec(memory_space=pltpu.SMEM)
    vmem = pl.BlockSpec(memory_space=pltpu.VMEM)
    f32 = jnp.float32
    factors = [
        pltpu.VMEM((N_TRIG, BLK), f32),
        pltpu.VMEM((N_TRIG, BLK), f32),
        pltpu.VMEM((C_ROWS[2], 2 * BLK), f32),
        pltpu.VMEM((256, 2 * BLK), f32),
    ]
    return pl.pallas_call(
        grid_kernel,
        out_shape=jax.ShapeDtypeStruct((8, TILE, TILE), f32),
        in_specs=[smem, smem, vmem, vmem],
        out_specs=vmem,
        scratch_shapes=[
            pltpu.SMEM((OWNED,), jnp.int32),
            pltpu.SMEM((OWNED,), jnp.int32),
            pltpu.SMEM((MAX_GROUPS + 2,), jnp.int32),
            pltpu.VMEM((MAX_GROUPS, 16, BLK), f32),
            pltpu.VMEM((N_PHASE, BLK), f32),
            *factors,
            *factors,
            pltpu.VMEM((OWNED + 1, 2, SUB, BLK), f32),
            pltpu.VMEM((4, OWNED * SUB, 2 * BLK), f32),
        ],
        compiler_params=pltpu.CompilerParams(vmem_limit_bytes=62 * 1024 * 1024),
        name="grid_tile",
    )(info, offset, taper, got)


FAR_FIRST = (6, 5, 7, 2, 4, 1, 3)


def near(me, k, sign):
    return (me // 4 + k // 4) % 2 * 4 + (me + 4 + sign * (k % 4)) % 4


def sum_kernel(tile, out, recv, send_sem, recv_sem):
    me = lax.axis_index("freq")
    barrier = pltpu.get_barrier_semaphore()
    for k in FAR_FIRST:
        pl.semaphore_signal(
            barrier,
            inc=1,
            device_id={"freq": near(me, k, 1)},
            device_id_type=pl.DeviceIdType.MESH,
        )
    pl.semaphore_wait(barrier, GROUPS - 1)
    strip = TILE // GROUPS
    copies = []
    for k in FAR_FIRST:
        peer = near(me, k, 1)
        copy = pltpu.make_async_remote_copy(
            src_ref=tile.at[:, pl.ds(pl.multiple_of(peer * strip, 8), strip)],
            dst_ref=recv.at[k],
            send_sem=send_sem.at[k],
            recv_sem=recv_sem.at[k],
            device_id={"freq": peer},
            device_id_type=pl.DeviceIdType.MESH,
        )
        copy.start()
        copies.append(copy)
    value = tile[:, pl.ds(pl.multiple_of(me * strip, 8), strip), :]
    for k, copy in zip(FAR_FIRST, copies):
        copy.wait_recv()
        value = value + recv[k]
    for c in range(8):
        out[:, c, :] = value[c]
    for copy in copies:
        copy.wait_send()


def sum_over_freq(tile):
    vmem = pl.BlockSpec(memory_space=pltpu.VMEM)
    strip = TILE // GROUPS
    return pl.pallas_call(
        sum_kernel,
        out_shape=jax.ShapeDtypeStruct((strip, 8, TILE), jnp.float32),
        in_specs=[vmem],
        out_specs=vmem,
        scratch_shapes=[
            pltpu.VMEM((GROUPS, 8, strip, TILE), jnp.float32),
            pltpu.SemaphoreType.DMA((GROUPS,)),
            pltpu.SemaphoreType.DMA((GROUPS,)),
        ],
        compiler_params=pltpu.CompilerParams(
            collective_id=1, has_side_effects=True, vmem_limit_bytes=62 * 1024 * 1024
        ),
        name="sum_over_freq",
    )(tile)


def shards(
    visibility, uv_offset, w_offset, taper, row_count, block_owner, block_slot, subgrid_offset
):
    got, info = exchange(
        block_owner[:, :, 0], block_slot, row_count, visibility[0], uv_offset[0], w_offset[0]
    )
    return sum_over_freq(grid_tile(info, subgrid_offset.T, taper, got))


def solution(mesh):
    placed = (
        P("freq", "uv", None, None),
        P("freq", "uv", None, None),
        P("freq", "uv", None),
        P(),
        P("freq", "uv"),
        P("freq", "uv", None),
        P("freq", "uv"),
        P("uv", None),
    )
    return jax.shard_map(
        shards, mesh=mesh, in_specs=placed, out_specs=P(("uv", "freq"), None, None), check_vma=False
    )
```

```python
import functools
import math

import jax
import jax.numpy as jnp
from jax import lax
from jax.experimental import pallas as pl
from jax.experimental.pallas import tpu as pltpu
from jax.sharding import PartitionSpec as P

SUB = 32
BLK = 128
TILE = 128
OWNERS = 32
GROUPS = 8
OWNED = 16
SLOTS = 64
ROWS = 24
MAX_GROUPS = 82

SIN_POLY = (
    4.442882919124345,
    -7.308245686509104,
    3.6063542184332804,
    -0.8461116503752865,
    0.10982451642699691,
)
COS_POLY = (
    1.4142134962552289,
    -6.978850948563853,
    5.7394603769076955,
    -1.8835579059892091,
    0.31068802753070307,
)


def horner(z, coefficients):
    value = z * coefficients[-1] + coefficients[-2]
    for c in coefficients[-3::-1]:
        value = value * z + c
    return value


def sincos_turns(turns):
    f = turns - jnp.round(turns)
    z = f * f
    s = horner(z, SIN_POLY) * f
    c = horner(z, COS_POLY)
    return s * c, 1.0 - s * s


def split(x):
    hi = x.astype(jnp.bfloat16)
    lo = (x - hi.astype(jnp.float32)).astype(jnp.bfloat16)
    return hi, lo


def dot_nt(a, b):
    return lax.dot_general(a, b, (((1,), (1,)), ((), ())), preferred_element_type=jnp.float32)


def dot_nn(a, b):
    return lax.dot_general(a, b, (((1,), (0,)), ((), ())), preferred_element_type=jnp.float32)


def iota(shape, axis):
    return lax.broadcasted_iota(jnp.int32, shape, axis)


def partner(me, i, sign):
    j = i // 4
    dz = jnp.where(j % 2 == 0, 4 + j // 2, 4 - (j + 1) // 2)
    dy = 1 - (i % 4) // 2
    dc = 1 - i % 2
    y = (me // 16 + dy) % 2
    z = (me // 2 + 8 + sign * dz) % 8
    return y * 16 + z * 2 + (me + dc) % 2


def exchange_kernel(
    owner, slot, count, vis, uvo, wo, got, info, send, recv, send_sem, recv_sem
):
    me = lax.axis_index("uv")
    barrier = pltpu.get_barrier_semaphore()

    def greet(k, carry):
        peer = partner(me, k, 1)
        pl.semaphore_signal(
            barrier, inc=1, device_id={"uv": peer}, device_id_type=pl.DeviceIdType.MESH
        )
        return carry

    lax.fori_loop(0, OWNERS - 1, greet, 0)

    size = vis.shape[0]
    mine = owner[...].astype(jnp.float32)
    across = jnp.broadcast_to(mine, (size, size))
    row, col = iota((size, size), 0), iota((size, size), 1)
    down = jnp.sum(jnp.where(row == col, across, 0.0), axis=1, keepdims=True)
    earlier = jnp.where((down == across) & (row < col), 1.0, 0.0)
    target = mine + OWNERS * jnp.sum(earlier, axis=0, keepdims=True)
    pick = jnp.where(iota((SLOTS, size), 0).astype(jnp.float32) == target, 1.0, 0.0)
    slots = jnp.sum(pick * slot[...].astype(jnp.float32), axis=1, keepdims=True)
    counts = jnp.sum(pick * count[...].astype(jnp.float32), axis=1, keepdims=True)
    lane = iota((SLOTS, BLK), 1)
    facts = jnp.where(lane == 0, slots, jnp.where(lane == 1, counts, 0.0))
    data = jnp.concatenate(
        [vis[:, c, :] for c in range(8)] + [uvo[:, 0, :], uvo[:, 1, :], wo[...]], 1
    )
    hi = data.astype(jnp.bfloat16)
    rest = data - hi.astype(jnp.float32)
    mid, lo = split(rest)
    pick = pick.astype(jnp.bfloat16)
    moved = dot_nn(jnp.concatenate([pick] * 3, 1), jnp.concatenate([hi, mid, lo], 0))
    for rank in range(2):
        part = slice(rank * OWNERS, rank * OWNERS + OWNERS)
        for c in range(12):
            value = moved[part, c * BLK : c * BLK + BLK] if c < 11 else facts[part, :]
            at = 8 * rank + c if c < 8 else 16 + 4 * rank + c - 8
            send[pl.ds(at, OWNERS, stride=ROWS), :] = value

    pl.semaphore_wait(barrier, OWNERS - 1)

    def copy_to(k):
        peer = partner(me, k, 1)
        return pltpu.make_async_remote_copy(
            src_ref=send.at[pl.ds(pl.multiple_of(peer * ROWS, 8), ROWS)],
            dst_ref=recv.at[pl.ds(pl.multiple_of(me * ROWS, 8), ROWS)],
            send_sem=send_sem.at[k],
            recv_sem=recv_sem.at[k],
            device_id={"uv": peer},
            device_id_type=pl.DeviceIdType.MESH,
        )

    def start(k, carry):
        copy_to(k).start()
        return carry

    lax.fori_loop(0, OWNERS - 1, start, 0)
    own = pl.ds(pl.multiple_of(me * ROWS, 8), ROWS)
    recv[own, :] = send[own, :]

    def finish(k, carry):
        source = partner(me, k, -1)
        pltpu.make_async_remote_copy(
            src_ref=send.at[pl.ds(pl.multiple_of(source * ROWS, 8), ROWS)],
            dst_ref=recv.at[pl.ds(pl.multiple_of(source * ROWS, 8), ROWS)],
            send_sem=send_sem.at[k],
            recv_sem=recv_sem.at[k],
            device_id={"uv": source},
            device_id_type=pl.DeviceIdType.MESH,
        ).wait_recv()
        return carry

    lax.fori_loop(0, OWNERS - 1, finish, 0)
    got[...] = recv[...]
    known = jnp.concatenate(
        [recv[pl.ds(19, OWNERS, stride=ROWS), :], recv[pl.ds(23, OWNERS, stride=ROWS), :]]
        + [jnp.zeros((BLK - SLOTS, BLK), jnp.float32)],
        0,
    )
    own_slot = iota((BLK, BLK), 1).astype(jnp.float32) == known[:, 0:1]
    totals = jnp.sum(jnp.where(own_slot, known[:, 1:2], 0.0), axis=0, keepdims=True)
    listed = jnp.transpose(known)[0:8, :]
    info[...] = jnp.where(iota((8, BLK), 0) == 2, totals, listed).astype(jnp.int32)

    def drain(k, carry):
        copy_to(k).wait_send()
        return carry

    lax.fori_loop(0, OWNERS - 1, drain, 0)


def exchange(owner, slot, count, vis, uvo, wo):
    vmem = pl.BlockSpec(memory_space=pltpu.VMEM)
    return pl.pallas_call(
        exchange_kernel,
        out_shape=(
            jax.ShapeDtypeStruct((OWNERS * ROWS, BLK), jnp.float32),
            jax.ShapeDtypeStruct((8, BLK), jnp.int32),
        ),
        in_specs=[vmem] * 6,
        out_specs=(vmem, vmem),
        scratch_shapes=[
            pltpu.VMEM((OWNERS * ROWS, BLK), jnp.float32),
            pltpu.VMEM((OWNERS * ROWS, BLK), jnp.float32),
            pltpu.SemaphoreType.DMA((OWNERS,)),
            pltpu.SemaphoreType.DMA((OWNERS,)),
        ],
        compiler_params=pltpu.CompilerParams(
            collective_id=0, has_side_effects=True, vmem_limit_bytes=62 * 1024 * 1024
        ),
        name="exchange",
    )(owner, slot, count, vis, uvo, wo)


ROW_L = 0
ROW_B = 64
ROW_H = 128
ROW_C = 192
ROW_M = 208
ROW_U = 216
ROW_V = 232
ROW_E = 248
N_TRIG = 272
N_ONCE = 72
N_PHASE = 160


def once(k):
    if k < 6:
        base, k = (ROW_L, ROW_H)[k // 3], k % 3 + 1
        return ((0, 8 - k, base, 8 - k, 0), (8 - k, k, base, k, 0))
    if k == 6:
        return ((0, 4, ROW_L, 4, 0), (4, 4, ROW_H, 4, 0))
    return ((0, 8, (ROW_L, ROW_H)[k - 7], 0, 1),)


TILE_A = (tuple(range(8)) + (16,), tuple(range(8, 16)))
C_ROWS = (0, 9 * 32, 17 * 32)


def phases(g, buf, ntab, sines, cosines, c_part, d_part):
    u = buf[g, 8:9, :]
    v = buf[g, 9:10, :]
    w = buf[g, 10:11, :]
    sub = iota((8, BLK), 0)
    row = sub.astype(jnp.float32)
    first_row = sub == 0
    halves = jnp.where(sub < 4, 1.0, -1.0)
    step0 = row * (0.5 / SUB)
    step1 = (row + 8.0) * (0.5 / SUB)

    def keep(at, turns):
        s, c = sincos_turns(turns)
        sines[at : at + 8, :] = s
        cosines[at : at + 8, :] = c

    keep(ROW_M, jnp.where(sub == 0, u, jnp.where(sub == 1, v, w)) * ntab[152:160, :])
    keep(ROW_U, u * step0)
    keep(ROW_U + 8, u * step1)
    keep(ROW_V, v * step0)
    keep(ROW_V + 8, v * step1)
    for k in range(N_ONCE // 8):
        s, c = sincos_turns(w * ntab[8 * k : 8 * k + 8, :])
        for first, size, base, a, diagonal in once(k):
            for table, value in ((sines, s), (cosines, c)):
                part = value[first : first + size, :]
                if diagonal:
                    table[pl.ds(base, size, stride=9), :] = part
                else:
                    table[base + a * 8 : base + a * 8 + size, :] = part
                    table[pl.ds(base + a, size, stride=8), :] = part
    for k in range(8):
        keep(ROW_B + 8 * k, w * ntab[N_ONCE + 8 * k : N_ONCE + 8 * k + 8, :])
    keep(ROW_C, w * ntab[136:144, :])
    keep(ROW_C + 8, w * ntab[144:152, :])

    vis = buf[g, 0:8, :]
    swapped = pltpu.roll(vis, 4, 0) * halves
    for t in range(2):
        cv = cosines[ROW_V + 8 * t : ROW_V + 8 * t + 8, :]
        sv = sines[ROW_V + 8 * t : ROW_V + 8 * t + 8, :]
        if t == 0:
            c16 = jnp.where(first_row, cosines[ROW_M + 1 : ROW_M + 2, :], 0.0)
            sv = jnp.where(first_row, -sines[ROW_M + 1 : ROW_M + 2, :], sv)
        less = -sv
        for c in range(8):
            one = jnp.broadcast_to(vis[c : c + 1, :], (8, BLK))
            two = jnp.broadcast_to(swapped[c : c + 1, :], (8, BLK))
            at = t * 128 + c * 16
            left, right = two * sv, one * less
            if t == 0:
                left, right = left + one * c16, right + two * c16
            d_part[at : at + 8, 0:BLK] = one * cv
            d_part[at : at + 8, BLK:] = two * cv
            d_part[at + 8 : at + 16, 0:BLK] = left
            d_part[at + 8 : at + 16, BLK:] = right

    cu0 = cosines[ROW_U : ROW_U + 8, :]
    cu1 = cosines[ROW_U + 8 : ROW_U + 16, :]
    su0 = sines[ROW_U : ROW_U + 8, :]
    su1 = sines[ROW_U + 8 : ROW_U + 16, :]
    c16 = cosines[ROW_M : ROW_M + 1, :]
    s16 = sines[ROW_M : ROW_M + 1, :]
    for at, to in ((ROW_C, ROW_E), (ROW_C + 8, ROW_E + 8), (ROW_M, ROW_E + 16)):
        c, s = cosines[at : at + 8, :], sines[at : at + 8, :]
        cosines[to : to + 8, :] = c * c16 + s * s16
        sines[to : to + 8, :] = s * c16 - c * s16
    for t in range(2):
        for i, a in enumerate(TILE_A[t]):
            edge = slice(ROW_E + a, ROW_E + a + 1)
            if a < 8:
                p0 = slice(ROW_L + a * 8, ROW_L + a * 8 + 8)
                p1 = pl.ds(ROW_B + a, 8, stride=8)
            elif a < 16:
                p0 = slice(ROW_B + (a - 8) * 8, ROW_B + (a - 8) * 8 + 8)
                p1 = slice(ROW_H + (a - 8) * 8, ROW_H + (a - 8) * 8 + 8)
            else:
                p0 = slice(ROW_C, ROW_C + 8)
                p1 = slice(ROW_C + 8, ROW_C + 16)
                edge = slice(ROW_E + 18, ROW_E + 19)
            cw0, sw0 = cosines[p0, :], sines[p0, :]
            cw1, sw1 = cosines[p1, :], sines[p1, :]
            cos_2 = jnp.where(first_row, cosines[edge, :], cw0 * su0)
            sin_2 = jnp.where(first_row, sines[edge, :], sw0 * su0)
            cos_rows = [cw0 * cu0, cw1 * cu1, cos_2, cw1 * su1]
            sin_rows = [sw0 * cu0, sw1 * cu1, sin_2, sw1 * su1]
            at = C_ROWS[t] + i * 32
            for part, rows in enumerate((cos_rows, sin_rows)):
                for k in range(4):
                    c_part[at + 8 * k : at + 8 * k + 8, part * BLK : part * BLK + BLK] = rows[k]


def add_images(s, c_part, d_part, acc):
    lane = iota((SUB, BLK), 1)
    for t in range(2):
        d_both = jnp.concatenate(split(d_part[t * 128 : t * 128 + 128, :]), 0)
        c_hi, c_lo = split(c_part[C_ROWS[t] : C_ROWS[t + 1], :])
        o_hi = dot_nt(c_hi, d_both)
        o_lo = dot_nt(c_lo, d_both)
        total = None
        for i, a in enumerate(TILE_A[t]):
            hi = o_hi[i * 32 : i * 32 + 32, :]
            lo = o_lo[i * 32 : i * 32 + 32, 0:BLK]
            value = hi[:, 0:BLK] + hi[:, BLK:] + lo
            if total is None:
                total = value
            elif a == 16:
                total = jnp.where((lane & 15) == 8, value, total)
            else:
                total = jnp.where((lane & 7) == i, value, total)
        acc[s, t] += total


def grid_kernel(
    info,
    offset,
    taper,
    got,
    tile,
    base,
    slot_of,
    buf,
    ntab,
    sines_0,
    cosines_0,
    c_0,
    d_0,
    sines_1,
    cosines_1,
    c_1,
    d_1,
    acc,
    spread,
):
    slot_of[0] = OWNED

    def place_slot(s, first):
        number = lax.shift_right_logical(info[2, s] + (BLK - 1), 7)
        base[s] = first * BLK

        def name_group(i, carry):
            slot_of[first + i + 1] = s
            return carry

        lax.fori_loop(0, number, name_group, 0)
        return first + number

    groups = lax.fori_loop(0, OWNED, place_slot, 0)
    slot_of[groups + 1] = OWNED

    def clear_group(g, carry):
        buf[g] = jnp.zeros((16, BLK), jnp.float32)
        return carry

    lax.fori_loop(0, groups + 2, clear_group, 0)
    lane8 = iota((8, BLK), 1)

    def compact(k, carry):
        moved = []
        for i4 in range(4):
            i = k * 4 + i4
            others = got[pl.ds(i * ROWS + 16, 8), :]
            for rank in range(2):
                b = i + OWNERS * rank
                s = info[0, b]
                n = info[1, b]
                at = base[s]
                base[s] = at + n
                g = lax.shift_right_logical(at, 7)
                shift = at & (BLK - 1)
                vis = pltpu.roll(got[pl.ds(i * ROWS + 8 * rank, 8), :], shift, 1)
                rest = pltpu.roll(others if rank == 0 else pltpu.roll(others, 4, 0), shift, 1)
                here = (lane8 >= shift) & (lane8 < shift + n)
                after = lane8 < shift + n - BLK
                moved.append((g, vis, rest, here, after))
        for g, vis, rest, here, after in moved:
            buf[g, 0:8, :] = jnp.where(here, vis, buf[g, 0:8, :])
            buf[g, 8:16, :] = jnp.where(here, rest, buf[g, 8:16, :])
            buf[g + 1, 0:8, :] = jnp.where(after, vis, buf[g + 1, 0:8, :])
            buf[g + 1, 8:16, :] = jnp.where(after, rest, buf[g + 1, 8:16, :])
        return carry

    lax.fori_loop(0, OWNERS // 4, compact, 0)

    def n_of(a, b):
        l = b * (0.5 / SUB)
        m = a * (0.5 / SUB)
        return 1.0 - jnp.sqrt(1.0 - l * l - m * m)

    row = iota((8, BLK), 0).astype(jnp.float32)
    for k in range(N_ONCE // 8):
        a, b = row, row
        for first, size, base, y, diagonal in once(k):
            shift = 0.0 if base == ROW_L else 8.0
            here = row >= float(first)
            a = jnp.where(here, row + shift if diagonal else float(y) + shift, a)
            b = jnp.where(here, row - float(first) + shift, b)
        ntab[8 * k : 8 * k + 8, :] = n_of(a, b)
    for k in range(8):
        ntab[N_ONCE + 8 * k : N_ONCE + 8 * k + 8, :] = n_of(float(8 + k), row)
    ntab[136:144, :] = n_of(16.0, row)
    ntab[144:152, :] = n_of(16.0, row + 8.0)
    ntab[152:160, :] = jnp.where(
        row < 2.0, 16 * 0.5 / SUB, n_of(16.0, jnp.full((8, BLK), 16.0, jnp.float32))
    )

    for s in range(OWNED):
        acc[s] = jnp.zeros((2, SUB, BLK), jnp.float32)

    def two_groups(g):
        phases(g, buf, ntab, sines_0, cosines_0, c_0, d_0)
        add_images(slot_of[g], c_1, d_1, acc)
        phases(g + 1, buf, ntab, sines_1, cosines_1, c_1, d_1)
        add_images(slot_of[g + 1], c_0, d_0, acc)

    def four_groups(i, carry):
        two_groups(4 * i)
        two_groups(4 * i + 2)
        return carry

    def rest(i, carry):
        two_groups(2 * i)
        return carry

    fours = lax.div(groups, 4)
    steps = lax.div(groups + 1, 2)
    lax.fori_loop(0, fours, four_groups, 0)
    lax.fori_loop(2 * fours, steps, rest, 0)
    add_images(slot_of[2 * steps], c_1, d_1, acc)

    def y_of(high, sign, low):
        i = high * 8 + low
        return jnp.where(sign == 0, 16 + i, jnp.where(i == 0, 0, 16 - i))

    def x_of(j):
        return jnp.where(j < 16, j + 16, jnp.where(j == 16, 0, 32 - j))

    def exact(a, b, dims):
        return lax.dot_general(
            a, b, (dims, ((), ())), precision=lax.Precision.HIGHEST,
            preferred_element_type=jnp.float32,
        )

    pick_x = (x_of(iota((SUB, SUB), 0)) == iota((SUB, SUB), 1)).astype(jnp.float32)
    place = iota((SUB, 2 * BLK), 1)
    pick_y = (
        y_of(lax.shift_right_logical(place, 7), lax.shift_right_logical(place, 3) & 1, place & 7)
        == iota((SUB, 2 * BLK), 0)
    ).astype(jnp.float32)
    weight = exact(exact(pick_x, taper[...], ((1,), (1,))), pick_y, ((1,), (0,))) * (
        1.0 / math.sqrt(BLK)
    )

    row, col = iota((BLK, BLK), 0), iota((BLK, BLK), 1)
    turn = (x_of(row & (SUB - 1)) * (col & (SUB - 1))) & (SUB - 1)
    sx, cx = sincos_turns(turn.astype(jnp.float32) * (1.0 / SUB))
    same = lax.shift_right_logical(row, 5) == lax.shift_right_logical(col, 5)
    w_hi, w_lo = split(
        jnp.concatenate(
            [jnp.where(same, cx * (1.0 / SUB), 0.0), jnp.where(same, sx * (-1.0 / SUB), 0.0)], 1
        )
    )
    w_all = jnp.concatenate([w_hi, w_hi, w_lo], 0)
    lane = iota((SUB, BLK), 1)
    even_lane = (lane & 8) == 0
    lane16 = iota((16, BLK), 1)
    turn_sign = jnp.where(lane16 < BLK // 2, 1.0, -1.0)
    edge = iota((16, BLK), 0) == 0

    for q in range(OWNED // 4):
        rows = []
        for s in range(4 * q, 4 * q + 4):
            both = []
            for t in range(2):
                a = acc[s, t]
                y = jnp.where(even_lane, a + pltpu.roll(a, BLK - 8, 1), pltpu.roll(a, 8, 1) - a)
                if t == 0:
                    y = jnp.where((lane & 7) == 0, a, y)
                cos_x, sin_x = y[0:16, :], y[16:32, :]
                turned = pltpu.roll(sin_x, BLK // 2, 1) * turn_sign
                plus = jnp.where(edge, cos_x, cos_x + turned)
                minus = jnp.where(edge, sin_x, cos_x - turned)
                both.append(jnp.concatenate([plus, minus], 0))
            rows.append(jnp.concatenate(both, 1) * weight)
        x_hi, x_lo = split(jnp.transpose(jnp.concatenate(rows, 0)))
        z = dot_nn(jnp.concatenate([x_hi, x_lo, x_hi], 1), w_all)
        rights = [offset[1, 4 * q + j] for j in range(4)]
        inside = [(lane16 >= right) & (lane16 < right + SUB) for right in rights]
        for t in range(2):
            for p in range(4):
                re = z[t * 128 + p * 16 : t * 128 + p * 16 + 16, :]
                im = z[t * 128 + p * 16 + 64 : t * 128 + p * 16 + 80, :]
                joined = (re[:, 0:BLK] - im[:, BLK:], re[:, BLK:] + im[:, 0:BLK])
                for j in range(4):
                    at = (4 * q + j) * SUB + t * 16
                    shift = (rights[j] + (BLK - SUB * j)) & (BLK - 1)
                    for part in range(2):
                        spread[p, at : at + 16, part * BLK : part * BLK + BLK] = jnp.where(
                            inside[j], pltpu.roll(joined[part], shift, 1), 0.0
                        )

    lane = iota((1, OWNED * SUB), 1)
    corner = jnp.zeros((1, OWNED * SUB), jnp.int32)
    for s in range(OWNED):
        corner = jnp.where(lax.shift_right_logical(lane, 5) == s, offset[0, s], corner)
    yy = y_of(lax.shift_right_logical(lane, 4) & 1, lax.shift_right_logical(lane, 3) & 1, lane & 7)

    def turned(at, y):
        return sincos_turns(((at * y) & (SUB - 1)).astype(jnp.float32) * (1.0 / SUB))

    s_at, c_at = turned(iota((TILE, BLK), 0), jnp.broadcast_to(yy[:, 0:BLK], (TILE, BLK)))
    s_at, c_at = jnp.concatenate([s_at] * 4, 1), jnp.concatenate([c_at] * 4, 1)
    s_corner, c_corner = turned(corner, yy)
    cy = c_at * c_corner + s_at * s_corner
    sy = s_at * c_corner - c_at * s_corner
    ky = iota((TILE, OWNED * SUB), 0) - corner
    inside = (ky >= 0) & (ky < SUB)
    h = jnp.concatenate([jnp.where(inside, cy, 0.0), jnp.where(inside, -sy, 0.0)], 0)
    h_hi, h_lo = split(h)
    h_all = jnp.concatenate([h_hi, h_hi, h_lo], 1)
    for p in range(4):
        b_hi, b_lo = split(spread[p])
        o = dot_nn(h_all, jnp.concatenate([b_hi, b_lo, b_hi], 0))
        tile[p] = o[0:TILE, 0:BLK] - o[TILE:, BLK:]
        tile[p + 4] = o[0:TILE, BLK:] + o[TILE:, 0:BLK]


def grid_tile(info, offset, taper, got):
    smem = pl.BlockSpec(memory_space=pltpu.SMEM)
    vmem = pl.BlockSpec(memory_space=pltpu.VMEM)
    f32 = jnp.float32
    factors = [
        pltpu.VMEM((N_TRIG, BLK), f32),
        pltpu.VMEM((N_TRIG, BLK), f32),
        pltpu.VMEM((C_ROWS[2], 2 * BLK), f32),
        pltpu.VMEM((256, 2 * BLK), f32),
    ]
    return pl.pallas_call(
        grid_kernel,
        out_shape=jax.ShapeDtypeStruct((8, TILE, TILE), f32),
        in_specs=[smem, smem, vmem, vmem],
        out_specs=vmem,
        scratch_shapes=[
            pltpu.SMEM((OWNED,), jnp.int32),
            pltpu.SMEM((MAX_GROUPS + 2,), jnp.int32),
            pltpu.VMEM((MAX_GROUPS, 16, BLK), f32),
            pltpu.VMEM((N_PHASE, BLK), f32),
            *factors,
            *factors,
            pltpu.VMEM((OWNED + 1, 2, SUB, BLK), f32),
            pltpu.VMEM((4, OWNED * SUB, 2 * BLK), f32),
        ],
        compiler_params=pltpu.CompilerParams(vmem_limit_bytes=62 * 1024 * 1024),
        name="grid_tile",
    )(info, offset, taper, got)


FAR_FIRST = (6, 5, 7, 2, 4, 1, 3)


def near(me, k, sign):
    return (me // 4 + k // 4) % 2 * 4 + (me + 4 + sign * (k % 4)) % 4


def gather_kernel(tile, recv, send_sem, recv_sem):
    me = lax.axis_index("freq")
    own = pltpu.make_async_copy(
        tile.at[:, pl.ds(pl.multiple_of(me * (TILE // GROUPS), 8), TILE // GROUPS)],
        recv.at[0],
        recv_sem.at[0],
    )
    own.start()
    barrier = pltpu.get_barrier_semaphore()
    for k in FAR_FIRST:
        pl.semaphore_signal(
            barrier,
            inc=1,
            device_id={"freq": near(me, k, 1)},
            device_id_type=pl.DeviceIdType.MESH,
        )
    pl.semaphore_wait(barrier, GROUPS - 1)
    strip = TILE // GROUPS
    copies = []
    for k in FAR_FIRST:
        peer = near(me, k, 1)
        copy = pltpu.make_async_remote_copy(
            src_ref=tile.at[:, pl.ds(pl.multiple_of(peer * strip, 8), strip)],
            dst_ref=recv.at[k],
            send_sem=send_sem.at[k],
            recv_sem=recv_sem.at[k],
            device_id={"freq": peer},
            device_id_type=pl.DeviceIdType.MESH,
        )
        copy.start()
        copies.append(copy)
    own.wait()
    for copy in copies:
        copy.wait_recv()
    for copy in copies:
        copy.wait_send()


def sum_kernel(parts, out):
    value = parts[0]
    for k in range(1, GROUPS):
        value = value + parts[k]
    for c in range(8):
        out[:, c, :] = value[c]


def sum_over_freq(tile):
    strip = TILE // GROUPS
    anywhere = pl.BlockSpec(memory_space=pl.ANY)
    vmem = pl.BlockSpec(memory_space=pltpu.VMEM)
    parts = pl.pallas_call(
        gather_kernel,
        out_shape=jax.ShapeDtypeStruct((GROUPS, 8, strip, TILE), jnp.float32),
        in_specs=[anywhere],
        out_specs=anywhere,
        scratch_shapes=[
            pltpu.SemaphoreType.DMA((GROUPS,)),
            pltpu.SemaphoreType.DMA((GROUPS,)),
        ],
        compiler_params=pltpu.CompilerParams(
            collective_id=1, has_side_effects=True, vmem_limit_bytes=62 * 1024 * 1024
        ),
        name="gather_over_freq",
    )(tile)
    return pl.pallas_call(
        sum_kernel,
        out_shape=jax.ShapeDtypeStruct((strip, 8, TILE), jnp.float32),
        in_specs=[vmem],
        out_specs=vmem,
        compiler_params=pltpu.CompilerParams(vmem_limit_bytes=62 * 1024 * 1024),
        name="sum_over_freq",
    )(parts)


def shards(
    visibility, uv_offset, w_offset, taper, row_count, block_owner, block_slot, subgrid_offset
):
    got, info = exchange(
        block_owner[:, :, 0], block_slot, row_count, visibility[0], uv_offset[0], w_offset[0]
    )
    return sum_over_freq(grid_tile(info, subgrid_offset.T, taper, got))


def solution(mesh):
    placed = (
        P("freq", "uv", None, None),
        P("freq", "uv", None, None),
        P("freq", "uv", None),
        P(),
        P("freq", "uv"),
        P("freq", "uv", None),
        P("freq", "uv"),
        P("uv", None),
    )
    return jax.shard_map(
        shards, mesh=mesh, in_specs=placed, out_specs=P(("uv", "freq"), None, None), check_vma=False
    )
```

```python
import functools
import math

import jax
import jax.numpy as jnp
from jax import lax
from jax.experimental import pallas as pl
from jax.experimental.pallas import tpu as pltpu
from jax.sharding import PartitionSpec as P

SUB = 32
BLK = 128
TILE = 128
OWNERS = 32
GROUPS = 8
OWNED = 16
SLOTS = 64
ROWS = 24
MAX_GROUPS = 82

SIN_POLY = (
    4.442882919124345,
    -7.308245686509104,
    3.6063542184332804,
    -0.8461116503752865,
    0.10982451642699691,
)
COS_POLY = (
    1.4142134962552289,
    -6.978850948563853,
    5.7394603769076955,
    -1.8835579059892091,
    0.31068802753070307,
)


def horner(z, coefficients):
    value = z * coefficients[-1] + coefficients[-2]
    for c in coefficients[-3::-1]:
        value = value * z + c
    return value


def sincos_turns(turns):
    f = turns - jnp.round(turns)
    z = f * f
    s = horner(z, SIN_POLY) * f
    c = horner(z, COS_POLY)
    return s * c, 1.0 - s * s


def split(x):
    hi = x.astype(jnp.bfloat16)
    lo = (x - hi.astype(jnp.float32)).astype(jnp.bfloat16)
    return hi, lo


def dot_nt(a, b):
    return lax.dot_general(a, b, (((1,), (1,)), ((), ())), preferred_element_type=jnp.float32)


def dot_nn(a, b):
    return lax.dot_general(a, b, (((1,), (0,)), ((), ())), preferred_element_type=jnp.float32)


def iota(shape, axis):
    return lax.broadcasted_iota(jnp.int32, shape, axis)


def partner(me, i, sign):
    j = i // 4
    dz = jnp.where(j % 2 == 0, 4 + j // 2, 4 - (j + 1) // 2)
    dy = 1 - (i % 4) // 2
    dc = 1 - i % 2
    y = (me // 16 + dy) % 2
    z = (me // 2 + 8 + sign * dz) % 8
    return y * 16 + z * 2 + (me + dc) % 2


def exchange_kernel(
    owner, slot, count, vis, uvo, wo, got, info, send, recv, send_sem, recv_sem
):
    me = lax.axis_index("uv")
    barrier = pltpu.get_barrier_semaphore()

    def greet(k, carry):
        peer = partner(me, k, 1)
        pl.semaphore_signal(
            barrier, inc=1, device_id={"uv": peer}, device_id_type=pl.DeviceIdType.MESH
        )
        return carry

    lax.fori_loop(0, OWNERS - 1, greet, 0)

    size = vis.shape[0]
    mine = owner[...].astype(jnp.float32)
    across = jnp.broadcast_to(mine, (size, size))
    row, col = iota((size, size), 0), iota((size, size), 1)
    down = jnp.sum(jnp.where(row == col, across, 0.0), axis=1, keepdims=True)
    earlier = jnp.where((down == across) & (row < col), 1.0, 0.0)
    target = mine + OWNERS * jnp.sum(earlier, axis=0, keepdims=True)
    pick = jnp.where(iota((SLOTS, size), 0).astype(jnp.float32) == target, 1.0, 0.0)
    slots = jnp.sum(pick * slot[...].astype(jnp.float32), axis=1, keepdims=True)
    counts = jnp.sum(pick * count[...].astype(jnp.float32), axis=1, keepdims=True)
    lane = iota((SLOTS, BLK), 1)
    facts = jnp.where(lane == 0, slots, jnp.where(lane == 1, counts, 0.0))
    data = jnp.concatenate(
        [vis[:, c, :] for c in range(8)] + [uvo[:, 0, :], uvo[:, 1, :], wo[...]], 1
    )
    hi = data.astype(jnp.bfloat16)
    rest = data - hi.astype(jnp.float32)
    mid, lo = split(rest)
    pick = pick.astype(jnp.bfloat16)
    moved = dot_nn(jnp.concatenate([pick] * 3, 1), jnp.concatenate([hi, mid, lo], 0))
    for rank in range(2):
        part = slice(rank * OWNERS, rank * OWNERS + OWNERS)
        for c in range(12):
            value = moved[part, c * BLK : c * BLK + BLK] if c < 11 else facts[part, :]
            at = 8 * rank + c if c < 8 else 16 + 4 * rank + c - 8
            send[pl.ds(at, OWNERS, stride=ROWS), :] = value

    pl.semaphore_wait(barrier, OWNERS - 1)

    def copy_to(k):
        peer = partner(me, k, 1)
        return pltpu.make_async_remote_copy(
            src_ref=send.at[pl.ds(pl.multiple_of(peer * ROWS, 8), ROWS)],
            dst_ref=recv.at[pl.ds(pl.multiple_of(me * ROWS, 8), ROWS)],
            send_sem=send_sem.at[k],
            recv_sem=recv_sem.at[k],
            device_id={"uv": peer},
            device_id_type=pl.DeviceIdType.MESH,
        )

    def start(k, carry):
        copy_to(k).start()
        return carry

    lax.fori_loop(0, OWNERS - 1, start, 0)
    own = pl.ds(pl.multiple_of(me * ROWS, 8), ROWS)
    recv[own, :] = send[own, :]

    def finish(k, carry):
        source = partner(me, k, -1)
        pltpu.make_async_remote_copy(
            src_ref=send.at[pl.ds(pl.multiple_of(source * ROWS, 8), ROWS)],
            dst_ref=recv.at[pl.ds(pl.multiple_of(source * ROWS, 8), ROWS)],
            send_sem=send_sem.at[k],
            recv_sem=recv_sem.at[k],
            device_id={"uv": source},
            device_id_type=pl.DeviceIdType.MESH,
        ).wait_recv()
        return carry

    lax.fori_loop(0, OWNERS - 1, finish, 0)
    got[...] = recv[...]
    known = jnp.concatenate(
        [recv[pl.ds(19, OWNERS, stride=ROWS), :], recv[pl.ds(23, OWNERS, stride=ROWS), :]]
        + [jnp.zeros((BLK - SLOTS, BLK), jnp.float32)],
        0,
    )
    own_slot = iota((BLK, BLK), 1).astype(jnp.float32) == known[:, 0:1]
    totals = jnp.sum(jnp.where(own_slot, known[:, 1:2], 0.0), axis=0, keepdims=True)
    listed = jnp.transpose(known)[0:8, :]
    info[...] = jnp.where(iota((8, BLK), 0) == 2, totals, listed).astype(jnp.int32)

    def drain(k, carry):
        copy_to(k).wait_send()
        return carry

    lax.fori_loop(0, OWNERS - 1, drain, 0)


def exchange(owner, slot, count, vis, uvo, wo):
    vmem = pl.BlockSpec(memory_space=pltpu.VMEM)
    return pl.pallas_call(
        exchange_kernel,
        out_shape=(
            jax.ShapeDtypeStruct((OWNERS * ROWS, BLK), jnp.float32),
            jax.ShapeDtypeStruct((8, BLK), jnp.int32),
        ),
        in_specs=[vmem] * 6,
        out_specs=(vmem, vmem),
        scratch_shapes=[
            pltpu.VMEM((OWNERS * ROWS, BLK), jnp.float32),
            pltpu.VMEM((OWNERS * ROWS, BLK), jnp.float32),
            pltpu.SemaphoreType.DMA((OWNERS,)),
            pltpu.SemaphoreType.DMA((OWNERS,)),
        ],
        compiler_params=pltpu.CompilerParams(
            collective_id=0, has_side_effects=True, vmem_limit_bytes=62 * 1024 * 1024
        ),
        name="exchange",
    )(owner, slot, count, vis, uvo, wo)


ROW_L = 0
ROW_B = 64
ROW_H = 128
ROW_C = 192
ROW_M = 208
ROW_U = 216
ROW_V = 232
ROW_E = 248
N_TRIG = 272
N_ONCE = 72
N_PHASE = 160


def once(k):
    if k < 6:
        base, k = (ROW_L, ROW_H)[k // 3], k % 3 + 1
        return ((0, 8 - k, base, 8 - k, 0), (8 - k, k, base, k, 0))
    if k == 6:
        return ((0, 4, ROW_L, 4, 0), (4, 4, ROW_H, 4, 0))
    return ((0, 8, (ROW_L, ROW_H)[k - 7], 0, 1),)


TILE_A = (tuple(range(8)) + (16,), tuple(range(8, 16)))
C_ROWS = (0, 9 * 32, 17 * 32)


def phases(g, buf, ntab, sines, cosines, c_part, d_part):
    u = buf[g, 8:9, :]
    v = buf[g, 9:10, :]
    w = buf[g, 10:11, :]
    sub = iota((8, BLK), 0)
    row = sub.astype(jnp.float32)
    first_row = sub == 0
    halves = jnp.where(sub < 4, 1.0, -1.0)
    step0 = row * (0.5 / SUB)
    step1 = (row + 8.0) * (0.5 / SUB)

    def keep(at, turns):
        s, c = sincos_turns(turns)
        sines[at : at + 8, :] = s
        cosines[at : at + 8, :] = c

    keep(ROW_M, jnp.where(sub == 0, u, jnp.where(sub == 1, v, w)) * ntab[152:160, :])
    keep(ROW_U, u * step0)
    keep(ROW_U + 8, u * step1)
    keep(ROW_V, v * step0)
    keep(ROW_V + 8, v * step1)
    for k in range(N_ONCE // 8):
        s, c = sincos_turns(w * ntab[8 * k : 8 * k + 8, :])
        for first, size, base, a, diagonal in once(k):
            for table, value in ((sines, s), (cosines, c)):
                part = value[first : first + size, :]
                if diagonal:
                    table[pl.ds(base, size, stride=9), :] = part
                else:
                    table[base + a * 8 : base + a * 8 + size, :] = part
                    table[pl.ds(base + a, size, stride=8), :] = part
    for k in range(8):
        keep(ROW_B + 8 * k, w * ntab[N_ONCE + 8 * k : N_ONCE + 8 * k + 8, :])
    keep(ROW_C, w * ntab[136:144, :])
    keep(ROW_C + 8, w * ntab[144:152, :])

    vis = buf[g, 0:8, :]
    swapped = pltpu.roll(vis, 4, 0) * halves
    for t in range(2):
        cv = cosines[ROW_V + 8 * t : ROW_V + 8 * t + 8, :]
        sv = sines[ROW_V + 8 * t : ROW_V + 8 * t + 8, :]
        if t == 0:
            c16 = jnp.where(first_row, cosines[ROW_M + 1 : ROW_M + 2, :], 0.0)
            sv = jnp.where(first_row, -sines[ROW_M + 1 : ROW_M + 2, :], sv)
        for c in range(8):
            one = jnp.broadcast_to(vis[c : c + 1, :], (8, BLK))
            two = jnp.broadcast_to(swapped[c : c + 1, :], (8, BLK))
            at = t * 128 + c * 16
            odd = two * sv
            if t == 0:
                odd = odd + one * c16
            d_part[at : at + 8, :] = one * cv
            d_part[at + 8 : at + 16, :] = odd

    cu0 = cosines[ROW_U : ROW_U + 8, :]
    cu1 = cosines[ROW_U + 8 : ROW_U + 16, :]
    su0 = sines[ROW_U : ROW_U + 8, :]
    su1 = sines[ROW_U + 8 : ROW_U + 16, :]
    c16 = cosines[ROW_M : ROW_M + 1, :]
    s16 = sines[ROW_M : ROW_M + 1, :]
    for at, to in ((ROW_C, ROW_E), (ROW_C + 8, ROW_E + 8), (ROW_M, ROW_E + 16)):
        c, s = cosines[at : at + 8, :], sines[at : at + 8, :]
        cosines[to : to + 8, :] = c * c16 + s * s16
        sines[to : to + 8, :] = s * c16 - c * s16
    for t in range(2):
        for i, a in enumerate(TILE_A[t]):
            edge = slice(ROW_E + a, ROW_E + a + 1)
            if a < 8:
                p0 = slice(ROW_L + a * 8, ROW_L + a * 8 + 8)
                p1 = pl.ds(ROW_B + a, 8, stride=8)
            elif a < 16:
                p0 = slice(ROW_B + (a - 8) * 8, ROW_B + (a - 8) * 8 + 8)
                p1 = slice(ROW_H + (a - 8) * 8, ROW_H + (a - 8) * 8 + 8)
            else:
                p0 = slice(ROW_C, ROW_C + 8)
                p1 = slice(ROW_C + 8, ROW_C + 16)
                edge = slice(ROW_E + 18, ROW_E + 19)
            cw0, sw0 = cosines[p0, :], sines[p0, :]
            cw1, sw1 = cosines[p1, :], sines[p1, :]
            cos_2 = jnp.where(first_row, cosines[edge, :], cw0 * su0)
            sin_2 = jnp.where(first_row, sines[edge, :], sw0 * su0)
            cos_rows = [cw0 * cu0, cw1 * cu1, cos_2, cw1 * su1]
            sin_rows = [sw0 * cu0, sw1 * cu1, sin_2, sw1 * su1]
            at = C_ROWS[t] + i * 32
            for part, rows in enumerate((cos_rows, sin_rows)):
                for k in range(4):
                    c_part[at + 8 * k : at + 8 * k + 8, part * BLK : part * BLK + BLK] = rows[k]


def add_images(s, c_part, d_part, acc):
    lane = iota((SUB, BLK), 1)
    for t in range(2):
        d_both = jnp.concatenate(
            [
                jnp.concatenate([d, jnp.concatenate([d[64:, :], -d[:64, :]], 0)], 1)
                for d in split(d_part[t * 128 : t * 128 + 128, :])
            ],
            0,
        )
        c_hi, c_lo = split(c_part[C_ROWS[t] : C_ROWS[t + 1], :])
        o_hi = dot_nt(c_hi, d_both)
        o_lo = dot_nt(c_lo, d_both)
        total = None
        for i, a in enumerate(TILE_A[t]):
            hi = o_hi[i * 32 : i * 32 + 32, :]
            lo = o_lo[i * 32 : i * 32 + 32, 0:BLK]
            value = hi[:, 0:BLK] + hi[:, BLK:] + lo
            if total is None:
                total = value
            elif a == 16:
                total = jnp.where((lane & 15) == 8, value, total)
            else:
                total = jnp.where((lane & 7) == i, value, total)
        acc[s, t] += total


def grid_kernel(
    info,
    offset,
    taper,
    got,
    tile,
    base,
    slot_of,
    buf,
    ntab,
    sines_0,
    cosines_0,
    c_0,
    d_0,
    sines_1,
    cosines_1,
    c_1,
    d_1,
    acc,
    spread,
):
    slot_of[0] = OWNED

    def place_slot(s, first):
        number = lax.shift_right_logical(info[2, s] + (BLK - 1), 7)
        base[s] = first * BLK

        def name_group(i, carry):
            slot_of[first + i + 1] = s
            return carry

        lax.fori_loop(0, number, name_group, 0)
        return first + number

    groups = lax.fori_loop(0, OWNED, place_slot, 0)
    slot_of[groups + 1] = OWNED

    def clear_group(g, carry):
        buf[g] = jnp.zeros((16, BLK), jnp.float32)
        return carry

    lax.fori_loop(0, groups + 2, clear_group, 0)
    lane8 = iota((8, BLK), 1)

    def compact(k, carry):
        moved = []
        for i4 in range(4):
            i = k * 4 + i4
            others = got[pl.ds(i * ROWS + 16, 8), :]
            for rank in range(2):
                b = i + OWNERS * rank
                s = info[0, b]
                n = info[1, b]
                at = base[s]
                base[s] = at + n
                g = lax.shift_right_logical(at, 7)
                shift = at & (BLK - 1)
                vis = pltpu.roll(got[pl.ds(i * ROWS + 8 * rank, 8), :], shift, 1)
                rest = pltpu.roll(others if rank == 0 else pltpu.roll(others, 4, 0), shift, 1)
                here = (lane8 >= shift) & (lane8 < shift + n)
                after = lane8 < shift + n - BLK
                moved.append((g, vis, rest, here, after))
        for g, vis, rest, here, after in moved:
            pltpu.store(buf.at[g, 0:8, :], vis, mask=here)
            pltpu.store(buf.at[g, 8:16, :], rest, mask=here)
            pltpu.store(buf.at[g + 1, 0:8, :], vis, mask=after)
            pltpu.store(buf.at[g + 1, 8:16, :], rest, mask=after)
        return carry

    lax.fori_loop(0, OWNERS // 4, compact, 0)

    def n_of(a, b):
        l = b * (0.5 / SUB)
        m = a * (0.5 / SUB)
        return 1.0 - jnp.sqrt(1.0 - l * l - m * m)

    row = iota((8, BLK), 0).astype(jnp.float32)
    for k in range(N_ONCE // 8):
        a, b = row, row
        for first, size, base, y, diagonal in once(k):
            shift = 0.0 if base == ROW_L else 8.0
            here = row >= float(first)
            a = jnp.where(here, row + shift if diagonal else float(y) + shift, a)
            b = jnp.where(here, row - float(first) + shift, b)
        ntab[8 * k : 8 * k + 8, :] = n_of(a, b)
    for k in range(8):
        ntab[N_ONCE + 8 * k : N_ONCE + 8 * k + 8, :] = n_of(float(8 + k), row)
    ntab[136:144, :] = n_of(16.0, row)
    ntab[144:152, :] = n_of(16.0, row + 8.0)
    ntab[152:160, :] = jnp.where(
        row < 2.0, 16 * 0.5 / SUB, n_of(16.0, jnp.full((8, BLK), 16.0, jnp.float32))
    )

    for s in range(OWNED):
        acc[s] = jnp.zeros((2, SUB, BLK), jnp.float32)

    def two_groups(g):
        phases(g, buf, ntab, sines_0, cosines_0, c_0, d_0)
        add_images(slot_of[g], c_1, d_1, acc)
        phases(g + 1, buf, ntab, sines_1, cosines_1, c_1, d_1)
        add_images(slot_of[g + 1], c_0, d_0, acc)

    def four_groups(i, carry):
        two_groups(4 * i)
        two_groups(4 * i + 2)
        return carry

    def rest(i, carry):
        two_groups(2 * i)
        return carry

    fours = lax.div(groups, 4)
    steps = lax.div(groups + 1, 2)
    lax.fori_loop(0, fours, four_groups, 0)
    lax.fori_loop(2 * fours, steps, rest, 0)
    add_images(slot_of[2 * steps], c_1, d_1, acc)

    def y_of(high, sign, low):
        i = high * 8 + low
        return jnp.where(sign == 0, 16 + i, jnp.where(i == 0, 0, 16 - i))

    def x_of(j):
        return jnp.where(j < 16, j + 16, jnp.where(j == 16, 0, 32 - j))

    def exact(a, b, dims):
        return lax.dot_general(
            a, b, (dims, ((), ())), precision=lax.Precision.HIGHEST,
            preferred_element_type=jnp.float32,
        )

    pick_x = (x_of(iota((SUB, SUB), 0)) == iota((SUB, SUB), 1)).astype(jnp.float32)
    place = iota((SUB, 2 * BLK), 1)
    pick_y = (
        y_of(lax.shift_right_logical(place, 7), lax.shift_right_logical(place, 3) & 1, place & 7)
        == iota((SUB, 2 * BLK), 0)
    ).astype(jnp.float32)
    weight = exact(exact(pick_x, taper[...], ((1,), (1,))), pick_y, ((1,), (0,))) * (
        1.0 / math.sqrt(BLK)
    )

    row, col = iota((BLK, BLK), 0), iota((BLK, BLK), 1)
    turn = (x_of(row & (SUB - 1)) * (col & (SUB - 1))) & (SUB - 1)
    sx, cx = sincos_turns(turn.astype(jnp.float32) * (1.0 / SUB))
    same = lax.shift_right_logical(row, 5) == lax.shift_right_logical(col, 5)
    w_hi, w_lo = split(
        jnp.concatenate(
            [jnp.where(same, cx * (1.0 / SUB), 0.0), jnp.where(same, sx * (-1.0 / SUB), 0.0)], 1
        )
    )
    w_all = jnp.concatenate([w_hi, w_hi, w_lo], 0)
    lane = iota((SUB, BLK), 1)
    even_lane = (lane & 8) == 0
    lane16 = iota((16, BLK), 1)
    turn_sign = jnp.where(lane16 < BLK // 2, 1.0, -1.0)
    edge = iota((16, BLK), 0) == 0

    for q in range(OWNED // 4):
        rows = []
        for s in range(4 * q, 4 * q + 4):
            both = []
            for t in range(2):
                a = acc[s, t]
                y = jnp.where(even_lane, a + pltpu.roll(a, BLK - 8, 1), pltpu.roll(a, 8, 1) - a)
                if t == 0:
                    y = jnp.where((lane & 7) == 0, a, y)
                cos_x, sin_x = y[0:16, :], y[16:32, :]
                turned = pltpu.roll(sin_x, BLK // 2, 1) * turn_sign
                plus = jnp.where(edge, cos_x, cos_x + turned)
                minus = jnp.where(edge, sin_x, cos_x - turned)
                both.append(jnp.concatenate([plus, minus], 0))
            rows.append(jnp.concatenate(both, 1) * weight)
        x_hi, x_lo = split(jnp.transpose(jnp.concatenate(rows, 0)))
        z = dot_nn(jnp.concatenate([x_hi, x_lo, x_hi], 1), w_all)
        rights = [offset[1, 4 * q + j] for j in range(4)]
        inside = [(lane16 >= right) & (lane16 < right + SUB) for right in rights]
        for t in range(2):
            for p in range(4):
                re = z[t * 128 + p * 16 : t * 128 + p * 16 + 16, :]
                im = z[t * 128 + p * 16 + 64 : t * 128 + p * 16 + 80, :]
                joined = (re[:, 0:BLK] - im[:, BLK:], re[:, BLK:] + im[:, 0:BLK])
                for j in range(4):
                    at = (4 * q + j) * SUB + t * 16
                    shift = (rights[j] + (BLK - SUB * j)) & (BLK - 1)
                    for part in range(2):
                        spread[p, at : at + 16, part * BLK : part * BLK + BLK] = jnp.where(
                            inside[j], pltpu.roll(joined[part], shift, 1), 0.0
                        )

    lane = iota((1, OWNED * SUB), 1)
    corner = jnp.zeros((1, OWNED * SUB), jnp.int32)
    for s in range(OWNED):
        corner = jnp.where(lax.shift_right_logical(lane, 5) == s, offset[0, s], corner)
    yy = y_of(lax.shift_right_logical(lane, 4) & 1, lax.shift_right_logical(lane, 3) & 1, lane & 7)

    def turned(at, y):
        return sincos_turns(((at * y) & (SUB - 1)).astype(jnp.float32) * (1.0 / SUB))

    s_at, c_at = turned(iota((TILE, BLK), 0), jnp.broadcast_to(yy[:, 0:BLK], (TILE, BLK)))
    s_at, c_at = jnp.concatenate([s_at] * 4, 1), jnp.concatenate([c_at] * 4, 1)
    s_corner, c_corner = turned(corner, yy)
    cy = c_at * c_corner + s_at * s_corner
    sy = s_at * c_corner - c_at * s_corner
    ky = iota((TILE, OWNED * SUB), 0) - corner
    inside = (ky >= 0) & (ky < SUB)
    h = jnp.concatenate([jnp.where(inside, cy, 0.0), jnp.where(inside, -sy, 0.0)], 0)
    h_hi, h_lo = split(h)
    h_all = jnp.concatenate([h_hi, h_hi, h_lo], 1)
    for p in range(4):
        b_hi, b_lo = split(spread[p])
        o = dot_nn(h_all, jnp.concatenate([b_hi, b_lo, b_hi], 0))
        tile[p] = o[0:TILE, 0:BLK] - o[TILE:, BLK:]
        tile[p + 4] = o[0:TILE, BLK:] + o[TILE:, 0:BLK]


def grid_tile(info, offset, taper, got):
    smem = pl.BlockSpec(memory_space=pltpu.SMEM)
    vmem = pl.BlockSpec(memory_space=pltpu.VMEM)
    f32 = jnp.float32
    factors = [
        pltpu.VMEM((N_TRIG, BLK), f32),
        pltpu.VMEM((N_TRIG, BLK), f32),
        pltpu.VMEM((C_ROWS[2], 2 * BLK), f32),
        pltpu.VMEM((256, BLK), f32),
    ]
    return pl.pallas_call(
        grid_kernel,
        out_shape=jax.ShapeDtypeStruct((8, TILE, TILE), f32),
        in_specs=[smem, smem, vmem, vmem],
        out_specs=vmem,
        scratch_shapes=[
            pltpu.SMEM((OWNED,), jnp.int32),
            pltpu.SMEM((MAX_GROUPS + 2,), jnp.int32),
            pltpu.VMEM((MAX_GROUPS, 16, BLK), f32),
            pltpu.VMEM((N_PHASE, BLK), f32),
            *factors,
            *factors,
            pltpu.VMEM((OWNED + 1, 2, SUB, BLK), f32),
            pltpu.VMEM((4, OWNED * SUB, 2 * BLK), f32),
        ],
        compiler_params=pltpu.CompilerParams(vmem_limit_bytes=62 * 1024 * 1024),
        name="grid_tile",
    )(info, offset, taper, got)


FAR_FIRST = (6, 5, 7, 2, 4, 1, 3)


def near(me, k, sign):
    return (me // 4 + k // 4) % 2 * 4 + (me + 4 + sign * (k % 4)) % 4


def gather_kernel(tile, recv, send_sem, recv_sem):
    me = lax.axis_index("freq")
    own = pltpu.make_async_copy(
        tile.at[:, pl.ds(pl.multiple_of(me * (TILE // GROUPS), 8), TILE // GROUPS)],
        recv.at[0],
        recv_sem.at[0],
    )
    own.start()
    barrier = pltpu.get_barrier_semaphore()
    for k in FAR_FIRST:
        pl.semaphore_signal(
            barrier,
            inc=1,
            device_id={"freq": near(me, k, 1)},
            device_id_type=pl.DeviceIdType.MESH,
        )
    pl.semaphore_wait(barrier, GROUPS - 1)
    strip = TILE // GROUPS
    copies = []
    for k in FAR_FIRST:
        peer = near(me, k, 1)
        copy = pltpu.make_async_remote_copy(
            src_ref=tile.at[:, pl.ds(pl.multiple_of(peer * strip, 8), strip)],
            dst_ref=recv.at[k],
            send_sem=send_sem.at[k],
            recv_sem=recv_sem.at[k],
            device_id={"freq": peer},
            device_id_type=pl.DeviceIdType.MESH,
        )
        copy.start()
        copies.append(copy)
    own.wait()
    for copy in copies:
        copy.wait_recv()
    for copy in copies:
        copy.wait_send()


def sum_kernel(parts, out):
    value = parts[0]
    for k in range(1, GROUPS):
        value = value + parts[k]
    for c in range(8):
        out[:, c, :] = value[c]


def sum_over_freq(tile):
    strip = TILE // GROUPS
    anywhere = pl.BlockSpec(memory_space=pl.ANY)
    vmem = pl.BlockSpec(memory_space=pltpu.VMEM)
    parts = pl.pallas_call(
        gather_kernel,
        out_shape=jax.ShapeDtypeStruct((GROUPS, 8, strip, TILE), jnp.float32),
        in_specs=[anywhere],
        out_specs=anywhere,
        scratch_shapes=[
            pltpu.SemaphoreType.DMA((GROUPS,)),
            pltpu.SemaphoreType.DMA((GROUPS,)),
        ],
        compiler_params=pltpu.CompilerParams(
            collective_id=1, has_side_effects=True, vmem_limit_bytes=62 * 1024 * 1024
        ),
        name="gather_over_freq",
    )(tile)
    return pl.pallas_call(
        sum_kernel,
        out_shape=jax.ShapeDtypeStruct((strip, 8, TILE), jnp.float32),
        in_specs=[vmem],
        out_specs=vmem,
        compiler_params=pltpu.CompilerParams(vmem_limit_bytes=62 * 1024 * 1024),
        name="sum_over_freq",
    )(parts)


def shards(
    visibility, uv_offset, w_offset, taper, row_count, block_owner, block_slot, subgrid_offset
):
    got, info = exchange(
        block_owner[:, :, 0], block_slot, row_count, visibility[0], uv_offset[0], w_offset[0]
    )
    return sum_over_freq(grid_tile(info, subgrid_offset.T, taper, got))


def solution(mesh):
    placed = (
        P("freq", "uv", None, None),
        P("freq", "uv", None, None),
        P("freq", "uv", None),
        P(),
        P("freq", "uv"),
        P("freq", "uv", None),
        P("freq", "uv"),
        P("uv", None),
    )
    return jax.shard_map(
        shards, mesh=mesh, in_specs=placed, out_specs=P(("uv", "freq"), None, None), check_vma=False
    )
```

```python
import functools
import math

import jax
import jax.numpy as jnp
from jax import lax
from jax.experimental import pallas as pl
from jax.experimental.pallas import tpu as pltpu
from jax.sharding import PartitionSpec as P

SUB = 32
BLK = 128
TILE = 128
OWNERS = 32
GROUPS = 8
OWNED = 16
SLOTS = 64
ROWS = 24
MAX_GROUPS = 82

SIN_POLY = (
    4.442882919124345,
    -7.308245686509104,
    3.6063542184332804,
    -0.8461116503752865,
    0.10982451642699691,
)
COS_POLY = (
    1.4142134962552289,
    -6.978850948563853,
    5.7394603769076955,
    -1.8835579059892091,
    0.31068802753070307,
)


def horner(z, coefficients):
    value = z * coefficients[-1] + coefficients[-2]
    for c in coefficients[-3::-1]:
        value = value * z + c
    return value


def sincos_turns(turns):
    f = turns - jnp.round(turns)
    z = f * f
    s = horner(z, SIN_POLY) * f
    c = horner(z, COS_POLY)
    return s * c, 1.0 - s * s


def split(x):
    hi = x.astype(jnp.bfloat16)
    lo = (x - hi.astype(jnp.float32)).astype(jnp.bfloat16)
    return hi, lo


def dot_nt(a, b):
    return lax.dot_general(a, b, (((1,), (1,)), ((), ())), preferred_element_type=jnp.float32)


def dot_nn(a, b):
    return lax.dot_general(a, b, (((1,), (0,)), ((), ())), preferred_element_type=jnp.float32)


def iota(shape, axis):
    return lax.broadcasted_iota(jnp.int32, shape, axis)


def partner(me, i, sign):
    j = i // 4
    dz = jnp.where(j % 2 == 0, 4 + j // 2, 4 - (j + 1) // 2)
    dy = 1 - (i % 4) // 2
    dc = 1 - i % 2
    y = (me // 16 + dy) % 2
    z = (me // 2 + 8 + sign * dz) % 8
    return y * 16 + z * 2 + (me + dc) % 2


def exchange_kernel(
    owner, slot, count, vis, uvo, wo, got, info, send, recv, send_sem, recv_sem
):
    me = lax.axis_index("uv")
    barrier = pltpu.get_barrier_semaphore()

    def greet(k, carry):
        peer = partner(me, k, 1)
        pl.semaphore_signal(
            barrier, inc=1, device_id={"uv": peer}, device_id_type=pl.DeviceIdType.MESH
        )
        return carry

    lax.fori_loop(0, OWNERS - 1, greet, 0)

    size = vis.shape[0]
    mine = owner[...].astype(jnp.float32)
    across = jnp.broadcast_to(mine, (size, size))
    row, col = iota((size, size), 0), iota((size, size), 1)
    down = jnp.sum(jnp.where(row == col, across, 0.0), axis=1, keepdims=True)
    earlier = jnp.where((down == across) & (row < col), 1.0, 0.0)
    target = mine + OWNERS * jnp.sum(earlier, axis=0, keepdims=True)
    pick = jnp.where(iota((SLOTS, size), 0).astype(jnp.float32) == target, 1.0, 0.0)
    slots = jnp.sum(pick * slot[...].astype(jnp.float32), axis=1, keepdims=True)
    counts = jnp.sum(pick * count[...].astype(jnp.float32), axis=1, keepdims=True)
    lane = iota((SLOTS, BLK), 1)
    facts = jnp.where(lane == 0, slots, jnp.where(lane == 1, counts, 0.0))
    data = jnp.concatenate(
        [vis[:, c, :] for c in range(8)] + [uvo[:, 0, :], uvo[:, 1, :], wo[...]], 1
    )
    hi = data.astype(jnp.bfloat16)
    rest = data - hi.astype(jnp.float32)
    mid, lo = split(rest)
    pick = pick.astype(jnp.bfloat16)
    moved = dot_nn(jnp.concatenate([pick] * 3, 1), jnp.concatenate([hi, mid, lo], 0))
    for rank in range(2):
        part = slice(rank * OWNERS, rank * OWNERS + OWNERS)
        for c in range(12):
            value = moved[part, c * BLK : c * BLK + BLK] if c < 11 else facts[part, :]
            at = 8 * rank + c if c < 8 else 16 + 4 * rank + c - 8
            send[pl.ds(at, OWNERS, stride=ROWS), :] = value

    pl.semaphore_wait(barrier, OWNERS - 1)

    def copy_to(k):
        peer = partner(me, k, 1)
        return pltpu.make_async_remote_copy(
            src_ref=send.at[pl.ds(pl.multiple_of(peer * ROWS, 8), ROWS)],
            dst_ref=recv.at[pl.ds(pl.multiple_of(me * ROWS, 8), ROWS)],
            send_sem=send_sem.at[k],
            recv_sem=recv_sem.at[k],
            device_id={"uv": peer},
            device_id_type=pl.DeviceIdType.MESH,
        )

    def start(k, carry):
        copy_to(k).start()
        return carry

    lax.fori_loop(0, OWNERS - 1, start, 0)
    own = pl.ds(pl.multiple_of(me * ROWS, 8), ROWS)
    recv[own, :] = send[own, :]

    def finish(k, carry):
        source = partner(me, k, -1)
        pltpu.make_async_remote_copy(
            src_ref=send.at[pl.ds(pl.multiple_of(source * ROWS, 8), ROWS)],
            dst_ref=recv.at[pl.ds(pl.multiple_of(source * ROWS, 8), ROWS)],
            send_sem=send_sem.at[k],
            recv_sem=recv_sem.at[k],
            device_id={"uv": source},
            device_id_type=pl.DeviceIdType.MESH,
        ).wait_recv()
        return carry

    lax.fori_loop(0, OWNERS - 1, finish, 0)
    got[...] = recv[...]
    known = jnp.concatenate(
        [recv[pl.ds(19, OWNERS, stride=ROWS), :], recv[pl.ds(23, OWNERS, stride=ROWS), :]]
        + [jnp.zeros((BLK - SLOTS, BLK), jnp.float32)],
        0,
    )
    own_slot = iota((BLK, BLK), 1).astype(jnp.float32) == known[:, 0:1]
    totals = jnp.sum(jnp.where(own_slot, known[:, 1:2], 0.0), axis=0, keepdims=True)
    listed = jnp.transpose(known)[0:8, :]
    info[...] = jnp.where(iota((8, BLK), 0) == 2, totals, listed).astype(jnp.int32)

    def drain(k, carry):
        copy_to(k).wait_send()
        return carry

    lax.fori_loop(0, OWNERS - 1, drain, 0)


def exchange(owner, slot, count, vis, uvo, wo):
    vmem = pl.BlockSpec(memory_space=pltpu.VMEM)
    return pl.pallas_call(
        exchange_kernel,
        out_shape=(
            jax.ShapeDtypeStruct((OWNERS * ROWS, BLK), jnp.float32),
            jax.ShapeDtypeStruct((8, BLK), jnp.int32),
        ),
        in_specs=[vmem] * 6,
        out_specs=(vmem, vmem),
        scratch_shapes=[
            pltpu.VMEM((OWNERS * ROWS, BLK), jnp.float32),
            pltpu.VMEM((OWNERS * ROWS, BLK), jnp.float32),
            pltpu.SemaphoreType.DMA((OWNERS,)),
            pltpu.SemaphoreType.DMA((OWNERS,)),
        ],
        compiler_params=pltpu.CompilerParams(
            collective_id=0, has_side_effects=True, vmem_limit_bytes=62 * 1024 * 1024
        ),
        name="exchange",
    )(owner, slot, count, vis, uvo, wo)


ROW_L = 0
ROW_B = 64
ROW_H = 128
ROW_C = 192
ROW_M = 208
ROW_U = 216
ROW_V = 232
ROW_E = 248
N_TRIG = 272
N_ONCE = 72
N_PHASE = 160


def once(k):
    if k < 6:
        base, k = (ROW_L, ROW_H)[k // 3], k % 3 + 1
        return ((0, 8 - k, base, 8 - k, 0), (8 - k, k, base, k, 0))
    if k == 6:
        return ((0, 4, ROW_L, 4, 0), (4, 4, ROW_H, 4, 0))
    return ((0, 8, (ROW_L, ROW_H)[k - 7], 0, 1),)


STEP = 8
TILE_A = (tuple(range(8)) + (16,), tuple(range(8, 16)))
C_ROWS = (0, 9 * 32, 17 * 32)


def phases(g, buf, ntab, sines, cosines, c_part, d_part):
    u = buf[g, 8:9, :]
    v = buf[g, 9:10, :]
    w = buf[g, 10:11, :]
    sub = iota((8, BLK), 0)
    row = sub.astype(jnp.float32)
    first_row = sub == 0
    halves = jnp.where(sub < 4, 1.0, -1.0)
    step0 = row * (0.5 / SUB)
    step1 = (row + 8.0) * (0.5 / SUB)

    def keep(at, turns):
        s, c = sincos_turns(turns)
        sines[at : at + 8, :] = s
        cosines[at : at + 8, :] = c

    keep(ROW_M, jnp.where(sub == 0, u, jnp.where(sub == 1, v, w)) * ntab[152:160, :])
    keep(ROW_U, u * step0)
    keep(ROW_U + 8, u * step1)
    keep(ROW_V, v * step0)
    keep(ROW_V + 8, v * step1)
    for k in range(N_ONCE // 8):
        s, c = sincos_turns(w * ntab[8 * k : 8 * k + 8, :])
        for first, size, base, a, diagonal in once(k):
            for table, value in ((sines, s), (cosines, c)):
                part = value[first : first + size, :]
                if diagonal:
                    table[pl.ds(base, size, stride=9), :] = part
                else:
                    table[base + a * 8 : base + a * 8 + size, :] = part
                    table[pl.ds(base + a, size, stride=8), :] = part
    for k in range(8):
        keep(ROW_B + 8 * k, w * ntab[N_ONCE + 8 * k : N_ONCE + 8 * k + 8, :])
    keep(ROW_C, w * ntab[136:144, :])
    keep(ROW_C + 8, w * ntab[144:152, :])

    vis = buf[g, 0:8, :]
    swapped = pltpu.roll(vis, 4, 0) * halves
    for t in range(2):
        cv = cosines[ROW_V + 8 * t : ROW_V + 8 * t + 8, :]
        sv = sines[ROW_V + 8 * t : ROW_V + 8 * t + 8, :]
        if t == 0:
            c16 = jnp.where(first_row, cosines[ROW_M + 1 : ROW_M + 2, :], 0.0)
            sv = jnp.where(first_row, -sines[ROW_M + 1 : ROW_M + 2, :], sv)
        for c in range(8):
            one = jnp.broadcast_to(vis[c : c + 1, :], (8, BLK))
            two = jnp.broadcast_to(swapped[c : c + 1, :], (8, BLK))
            at = t * 128 + c * 16
            odd = two * sv
            if t == 0:
                odd = odd + one * c16
            d_part[at : at + 8, :] = one * cv
            d_part[at + 8 : at + 16, :] = odd

    cu0 = cosines[ROW_U : ROW_U + 8, :]
    cu1 = cosines[ROW_U + 8 : ROW_U + 16, :]
    su0 = sines[ROW_U : ROW_U + 8, :]
    su1 = sines[ROW_U + 8 : ROW_U + 16, :]
    c16 = cosines[ROW_M : ROW_M + 1, :]
    s16 = sines[ROW_M : ROW_M + 1, :]
    for at, to in ((ROW_C, ROW_E), (ROW_C + 8, ROW_E + 8), (ROW_M, ROW_E + 16)):
        c, s = cosines[at : at + 8, :], sines[at : at + 8, :]
        cosines[to : to + 8, :] = c * c16 + s * s16
        sines[to : to + 8, :] = s * c16 - c * s16
    for t in range(2):
        for i, a in enumerate(TILE_A[t]):
            edge = slice(ROW_E + a, ROW_E + a + 1)
            if a < 8:
                p0 = slice(ROW_L + a * 8, ROW_L + a * 8 + 8)
                p1 = pl.ds(ROW_B + a, 8, stride=8)
            elif a < 16:
                p0 = slice(ROW_B + (a - 8) * 8, ROW_B + (a - 8) * 8 + 8)
                p1 = slice(ROW_H + (a - 8) * 8, ROW_H + (a - 8) * 8 + 8)
            else:
                p0 = slice(ROW_C, ROW_C + 8)
                p1 = slice(ROW_C + 8, ROW_C + 16)
                edge = slice(ROW_E + 18, ROW_E + 19)
            cw0, sw0 = cosines[p0, :], sines[p0, :]
            cw1, sw1 = cosines[p1, :], sines[p1, :]
            cos_2 = jnp.where(first_row, cosines[edge, :], cw0 * su0)
            sin_2 = jnp.where(first_row, sines[edge, :], sw0 * su0)
            cos_rows = [cw0 * cu0, cw1 * cu1, cos_2, cw1 * su1]
            sin_rows = [sw0 * cu0, sw1 * cu1, sin_2, sw1 * su1]
            at = C_ROWS[t] + i * 32
            for part, rows in enumerate((cos_rows, sin_rows)):
                for k in range(4):
                    c_part[at + 8 * k : at + 8 * k + 8, part * BLK : part * BLK + BLK] = rows[k]


def add_images(s, c_part, d_part, acc):
    lane = iota((SUB, BLK), 1)
    for t in range(2):
        d_both = jnp.concatenate(
            [
                jnp.concatenate([d, jnp.concatenate([d[64:, :], -d[:64, :]], 0)], 1)
                for d in split(d_part[t * 128 : t * 128 + 128, :])
            ],
            0,
        )
        c_hi, c_lo = split(c_part[C_ROWS[t] : C_ROWS[t + 1], :])
        o_hi = dot_nt(c_hi, d_both)
        o_lo = dot_nt(c_lo, d_both)
        total = None
        for i, a in enumerate(TILE_A[t]):
            hi = o_hi[i * 32 : i * 32 + 32, :]
            lo = o_lo[i * 32 : i * 32 + 32, 0:BLK]
            value = hi[:, 0:BLK] + hi[:, BLK:] + lo
            if total is None:
                total = value
            elif a == 16:
                total = jnp.where((lane & 15) == 8, value, total)
            else:
                total = jnp.where((lane & 7) == i, value, total)
        acc[s, t] += total


def grid_kernel(
    info,
    offset,
    taper,
    got,
    tile,
    base,
    slot_of,
    buf,
    ntab,
    sines_0,
    cosines_0,
    c_0,
    d_0,
    sines_1,
    cosines_1,
    c_1,
    d_1,
    acc,
    spread,
):
    slot_of[0] = OWNED

    def place_slot(s, first):
        number = lax.shift_right_logical(info[2, s] + (BLK - 1), 7)
        base[s] = first * BLK

        def name_group(i, carry):
            slot_of[first + i + 1] = s
            return carry

        lax.fori_loop(0, number, name_group, 0)
        return first + number

    groups = lax.fori_loop(0, OWNED, place_slot, 0)
    slot_of[groups + 1] = OWNED

    def clear_group(g, carry):
        buf[g] = jnp.zeros((16, BLK), jnp.float32)
        return carry

    lax.fori_loop(0, groups + 2, clear_group, 0)
    lane8 = iota((8, BLK), 1)

    def compact(k, carry):
        moved = []
        for i4 in range(4):
            i = k * 4 + i4
            others = got[pl.ds(i * ROWS + 16, 8), :]
            for rank in range(2):
                b = i + OWNERS * rank
                s = info[0, b]
                n = info[1, b]
                at = base[s]
                base[s] = at + n
                g = lax.shift_right_logical(at, 7)
                shift = at & (BLK - 1)
                vis = pltpu.roll(got[pl.ds(i * ROWS + 8 * rank, 8), :], shift, 1)
                rest = pltpu.roll(others if rank == 0 else pltpu.roll(others, 4, 0), shift, 1)
                here = (lane8 >= shift) & (lane8 < shift + n)
                after = lane8 < shift + n - BLK
                moved.append((g, vis, rest, here, after))
        for g, vis, rest, here, after in moved:
            pltpu.store(buf.at[g, 0:8, :], vis, mask=here)
            pltpu.store(buf.at[g, 8:16, :], rest, mask=here)
            pltpu.store(buf.at[g + 1, 0:8, :], vis, mask=after)
            pltpu.store(buf.at[g + 1, 8:16, :], rest, mask=after)
        return carry

    lax.fori_loop(0, OWNERS // 4, compact, 0)

    def n_of(a, b):
        l = b * (0.5 / SUB)
        m = a * (0.5 / SUB)
        return 1.0 - jnp.sqrt(1.0 - l * l - m * m)

    row = iota((8, BLK), 0).astype(jnp.float32)
    for k in range(N_ONCE // 8):
        a, b = row, row
        for first, size, base, y, diagonal in once(k):
            shift = 0.0 if base == ROW_L else 8.0
            here = row >= float(first)
            a = jnp.where(here, row + shift if diagonal else float(y) + shift, a)
            b = jnp.where(here, row - float(first) + shift, b)
        ntab[8 * k : 8 * k + 8, :] = n_of(a, b)
    for k in range(8):
        ntab[N_ONCE + 8 * k : N_ONCE + 8 * k + 8, :] = n_of(float(8 + k), row)
    ntab[136:144, :] = n_of(16.0, row)
    ntab[144:152, :] = n_of(16.0, row + 8.0)
    ntab[152:160, :] = jnp.where(
        row < 2.0, 16 * 0.5 / SUB, n_of(16.0, jnp.full((8, BLK), 16.0, jnp.float32))
    )

    for s in range(OWNED):
        acc[s] = jnp.zeros((2, SUB, BLK), jnp.float32)

    def two_groups(g):
        phases(g, buf, ntab, sines_0, cosines_0, c_0, d_0)
        add_images(slot_of[g], c_1, d_1, acc)
        phases(g + 1, buf, ntab, sines_1, cosines_1, c_1, d_1)
        add_images(slot_of[g + 1], c_0, d_0, acc)

    def more_groups(i, carry):
        for k in range(0, STEP, 2):
            two_groups(STEP * i + k)
        return carry

    def rest(i, carry):
        two_groups(2 * i)
        return carry

    whole = lax.div(groups, STEP)
    steps = lax.div(groups + 1, 2)
    lax.fori_loop(0, whole, more_groups, 0)
    lax.fori_loop(STEP // 2 * whole, steps, rest, 0)
    add_images(slot_of[2 * steps], c_1, d_1, acc)

    def y_of(high, sign, low):
        i = high * 8 + low
        return jnp.where(sign == 0, 16 + i, jnp.where(i == 0, 0, 16 - i))

    def x_of(j):
        return jnp.where(j < 16, j + 16, jnp.where(j == 16, 0, 32 - j))

    def exact(a, b, dims):
        return lax.dot_general(
            a, b, (dims, ((), ())), precision=lax.Precision.HIGHEST,
            preferred_element_type=jnp.float32,
        )

    pick_x = (x_of(iota((SUB, SUB), 0)) == iota((SUB, SUB), 1)).astype(jnp.float32)
    place = iota((SUB, 2 * BLK), 1)
    pick_y = (
        y_of(lax.shift_right_logical(place, 7), lax.shift_right_logical(place, 3) & 1, place & 7)
        == iota((SUB, 2 * BLK), 0)
    ).astype(jnp.float32)
    weight = exact(exact(pick_x, taper[...], ((1,), (1,))), pick_y, ((1,), (0,))) * (
        1.0 / math.sqrt(BLK)
    )

    row, col = iota((BLK, BLK), 0), iota((BLK, BLK), 1)
    turn = (x_of(row & (SUB - 1)) * (col & (SUB - 1))) & (SUB - 1)
    sx, cx = sincos_turns(turn.astype(jnp.float32) * (1.0 / SUB))
    same = lax.shift_right_logical(row, 5) == lax.shift_right_logical(col, 5)
    w_hi, w_lo = split(
        jnp.concatenate(
            [jnp.where(same, cx * (1.0 / SUB), 0.0), jnp.where(same, sx * (-1.0 / SUB), 0.0)], 1
        )
    )
    w_all = jnp.concatenate([w_hi, w_hi, w_lo], 0)
    lane = iota((SUB, BLK), 1)
    even_lane = (lane & 8) == 0
    lane16 = iota((16, BLK), 1)
    first_row = iota((8, BLK), 0) == 0
    turn_sign = jnp.where(lane16 < BLK // 2, 1.0, -1.0)
    edge = iota((16, BLK), 0) == 0

    for q in range(OWNED // 4):
        rows = []
        for s in range(4 * q, 4 * q + 4):
            both = []
            for t in range(2):
                a = acc[s, t]
                y = jnp.where(even_lane, a + pltpu.roll(a, BLK - 8, 1), pltpu.roll(a, 8, 1) - a)
                if t == 0:
                    y = jnp.where((lane & 7) == 0, a, y)
                cos_x, sin_x = y[0:16, :], y[16:32, :]
                turned = pltpu.roll(sin_x, BLK // 2, 1) * turn_sign
                plus = jnp.where(edge, cos_x, cos_x + turned)
                minus = jnp.where(edge, sin_x, cos_x - turned)
                both.append(jnp.concatenate([plus, minus], 0))
            rows.append(jnp.concatenate(both, 1) * weight)
        x_hi, x_lo = split(jnp.transpose(jnp.concatenate(rows, 0)))
        z = dot_nn(jnp.concatenate([x_hi, x_lo, x_hi], 1), w_all)
        rights = [offset[1, 4 * q + j] for j in range(4)]
        inside = [(lane16 >= right) & (lane16 < right + SUB) for right in rights]
        for t in range(2):
            for p in range(4):
                re = z[t * 128 + p * 16 : t * 128 + p * 16 + 16, :]
                im = z[t * 128 + p * 16 + 64 : t * 128 + p * 16 + 80, :]
                re, im = re[:, 0:BLK] - im[:, BLK:], re[:, BLK:] + im[:, 0:BLK]
                up, down = (re[:8], im[:8]), (re[8:], im[8:])
                tops = [up[0] + down[0], up[1] + down[1]]
                lows = [up[1] - down[1], down[0] - up[0]]
                if t == 0:
                    tops = [jnp.where(first_row, x, y) for x, y in zip(up, tops)]
                    lows = [jnp.where(first_row, x, y) for x, y in zip(down, lows)]
                joined = [jnp.concatenate(pair, 0) for pair in zip(tops, lows)]
                for j in range(4):
                    at = (4 * q + j) * SUB + t * 16
                    shift = (rights[j] + (BLK - SUB * j)) & (BLK - 1)
                    for part in range(2):
                        spread[p, at : at + 16, part * BLK : part * BLK + BLK] = jnp.where(
                            inside[j], pltpu.roll(joined[part], shift, 1), 0.0
                        )

    lane = iota((1, OWNED * SUB), 1)
    corner = jnp.zeros((1, OWNED * SUB), jnp.int32)
    for s in range(OWNED):
        corner = jnp.where(lax.shift_right_logical(lane, 5) == s, offset[0, s], corner)
    high = (lax.shift_right_logical(lane, 4) & 1) * 8 + (lane & 7)
    low_half = (lane & 8) == 0
    yy = jnp.where(low_half | (high > 0), 16 + high, 0)
    use_cos = low_half | (high == 0)

    def turned(at, y):
        return sincos_turns(((at * y) & (SUB - 1)).astype(jnp.float32) * (1.0 / SUB))

    s_at, c_at = turned(iota((TILE, BLK), 0), jnp.broadcast_to(yy[:, 0:BLK], (TILE, BLK)))
    use_cos = jnp.broadcast_to(use_cos[:, 0:BLK], (TILE, BLK))
    first = jnp.concatenate([jnp.where(use_cos, c_at, s_at)] * 4, 1)
    second = jnp.concatenate([jnp.where(use_cos, s_at, -c_at)] * 4, 1)
    s_corner, c_corner = turned(corner, yy)
    ky = iota((TILE, OWNED * SUB), 0) - corner
    inside = (ky >= 0) & (ky < SUB)
    h_hi, h_lo = split(jnp.where(inside, first * c_corner + second * s_corner, 0.0))
    h_both = jnp.concatenate([h_hi, h_lo], 0)
    for p in range(4):
        b_hi, b_lo = split(spread[p])
        o = dot_nn(h_both, b_hi)
        o = o[0:TILE, :] + o[TILE:, :] + dot_nn(h_hi, b_lo)
        tile[p] = o[:, 0:BLK]
        tile[p + 4] = o[:, BLK:]


def grid_tile(info, offset, taper, got):
    smem = pl.BlockSpec(memory_space=pltpu.SMEM)
    vmem = pl.BlockSpec(memory_space=pltpu.VMEM)
    f32 = jnp.float32
    factors = [
        pltpu.VMEM((N_TRIG, BLK), f32),
        pltpu.VMEM((N_TRIG, BLK), f32),
        pltpu.VMEM((C_ROWS[2], 2 * BLK), f32),
        pltpu.VMEM((256, BLK), f32),
    ]
    return pl.pallas_call(
        grid_kernel,
        out_shape=jax.ShapeDtypeStruct((8, TILE, TILE), f32),
        in_specs=[smem, smem, vmem, vmem],
        out_specs=vmem,
        scratch_shapes=[
            pltpu.SMEM((OWNED,), jnp.int32),
            pltpu.SMEM((MAX_GROUPS + 2,), jnp.int32),
            pltpu.VMEM((MAX_GROUPS, 16, BLK), f32),
            pltpu.VMEM((N_PHASE, BLK), f32),
            *factors,
            *factors,
            pltpu.VMEM((OWNED + 1, 2, SUB, BLK), f32),
            pltpu.VMEM((4, OWNED * SUB, 2 * BLK), f32),
        ],
        compiler_params=pltpu.CompilerParams(vmem_limit_bytes=62 * 1024 * 1024),
        name="grid_tile",
    )(info, offset, taper, got)


FAR_FIRST = (6, 5, 7, 2, 4, 1, 3)


def near(me, k, sign):
    return (me // 4 + k // 4) % 2 * 4 + (me + 4 + sign * (k % 4)) % 4


def gather_kernel(tile, recv, send_sem, recv_sem):
    me = lax.axis_index("freq")
    own = pltpu.make_async_copy(
        tile.at[:, pl.ds(pl.multiple_of(me * (TILE // GROUPS), 8), TILE // GROUPS)],
        recv.at[0],
        recv_sem.at[0],
    )
    own.start()
    barrier = pltpu.get_barrier_semaphore()
    for k in FAR_FIRST:
        pl.semaphore_signal(
            barrier,
            inc=1,
            device_id={"freq": near(me, k, 1)},
            device_id_type=pl.DeviceIdType.MESH,
        )
    pl.semaphore_wait(barrier, GROUPS - 1)
    strip = TILE // GROUPS
    copies = []
    for k in FAR_FIRST:
        peer = near(me, k, 1)
        copy = pltpu.make_async_remote_copy(
            src_ref=tile.at[:, pl.ds(pl.multiple_of(peer * strip, 8), strip)],
            dst_ref=recv.at[k],
            send_sem=send_sem.at[k],
            recv_sem=recv_sem.at[k],
            device_id={"freq": peer},
            device_id_type=pl.DeviceIdType.MESH,
        )
        copy.start()
        copies.append(copy)
    own.wait()
    for copy in copies:
        copy.wait_recv()
    for copy in copies:
        copy.wait_send()


def sum_kernel(parts, out):
    value = parts[0]
    for k in range(1, GROUPS):
        value = value + parts[k]
    for c in range(8):
        out[:, c, :] = value[c]


def sum_over_freq(tile):
    strip = TILE // GROUPS
    anywhere = pl.BlockSpec(memory_space=pl.ANY)
    vmem = pl.BlockSpec(memory_space=pltpu.VMEM)
    parts = pl.pallas_call(
        gather_kernel,
        out_shape=jax.ShapeDtypeStruct((GROUPS, 8, strip, TILE), jnp.float32),
        in_specs=[anywhere],
        out_specs=anywhere,
        scratch_shapes=[
            pltpu.SemaphoreType.DMA((GROUPS,)),
            pltpu.SemaphoreType.DMA((GROUPS,)),
        ],
        compiler_params=pltpu.CompilerParams(
            collective_id=1, has_side_effects=True, vmem_limit_bytes=62 * 1024 * 1024
        ),
        name="gather_over_freq",
    )(tile)
    return pl.pallas_call(
        sum_kernel,
        out_shape=jax.ShapeDtypeStruct((strip, 8, TILE), jnp.float32),
        in_specs=[vmem],
        out_specs=vmem,
        compiler_params=pltpu.CompilerParams(vmem_limit_bytes=62 * 1024 * 1024),
        name="sum_over_freq",
    )(parts)


def shards(
    visibility, uv_offset, w_offset, taper, row_count, block_owner, block_slot, subgrid_offset
):
    got, info = exchange(
        block_owner[:, :, 0], block_slot, row_count, visibility[0], uv_offset[0], w_offset[0]
    )
    return sum_over_freq(grid_tile(info, subgrid_offset.T, taper, got))


def solution(mesh):
    placed = (
        P("freq", "uv", None, None),
        P("freq", "uv", None, None),
        P("freq", "uv", None),
        P(),
        P("freq", "uv"),
        P("freq", "uv", None),
        P("freq", "uv"),
        P("uv", None),
    )
    return jax.shard_map(
        shards, mesh=mesh, in_specs=placed, out_specs=P(("uv", "freq"), None, None), check_vma=False
    )
```

```python
import functools
import math

import jax
import jax.numpy as jnp
from jax import lax
from jax.experimental import pallas as pl
from jax.experimental.pallas import tpu as pltpu
from jax.sharding import PartitionSpec as P

SUB = 32
BLK = 128
TILE = 128
OWNERS = 32
GROUPS = 8
OWNED = 16
SLOTS = 64
ROWS = 24
SENT = 23
MAX_GROUPS = 82

SIN_POLY = (
    4.442882919124345,
    -7.308245686509104,
    3.6063542184332804,
    -0.8461116503752865,
    0.10982451642699691,
)
COS_POLY = (
    1.4142134962552289,
    -6.978850948563853,
    5.7394603769076955,
    -1.8835579059892091,
    0.31068802753070307,
)


def horner(z, coefficients):
    value = z * coefficients[-1] + coefficients[-2]
    for c in coefficients[-3::-1]:
        value = value * z + c
    return value


def sincos_turns(turns):
    f = turns - jnp.round(turns)
    z = f * f
    s = horner(z, SIN_POLY) * f
    c = horner(z, COS_POLY)
    return s * c, 1.0 - s * s


def split(x):
    hi = x.astype(jnp.bfloat16)
    lo = (x - hi.astype(jnp.float32)).astype(jnp.bfloat16)
    return hi, lo


def dot_nt(a, b):
    return lax.dot_general(a, b, (((1,), (1,)), ((), ())), preferred_element_type=jnp.float32)


def dot_nn(a, b):
    return lax.dot_general(a, b, (((1,), (0,)), ((), ())), preferred_element_type=jnp.float32)


def iota(shape, axis):
    return lax.broadcasted_iota(jnp.int32, shape, axis)


def partner(me, i, sign):
    j = i // 4
    dz = jnp.where(j % 2 == 0, 4 + j // 2, 4 - (j + 1) // 2)
    dy = 1 - (i % 4) // 2
    dc = 1 - i % 2
    y = (me // 16 + dy) % 2
    z = (me // 2 + 8 + sign * dz) % 8
    return y * 16 + z * 2 + (me + dc) % 2


def exchange_kernel(
    owner, slot, count, vis, uvo, wo, got, info, send, recv, send_sem, recv_sem
):
    me = lax.axis_index("uv")
    barrier = pltpu.get_barrier_semaphore()

    def greet(k, carry):
        peer = partner(me, k, 1)
        pl.semaphore_signal(
            barrier, inc=1, device_id={"uv": peer}, device_id_type=pl.DeviceIdType.MESH
        )
        return carry

    lax.fori_loop(0, OWNERS - 1, greet, 0)

    size = vis.shape[0]
    mine = owner[...].astype(jnp.float32)
    across = jnp.broadcast_to(mine, (size, size))
    row, col = iota((size, size), 0), iota((size, size), 1)
    down = jnp.sum(jnp.where(row == col, across, 0.0), axis=1, keepdims=True)
    earlier = jnp.where((down == across) & (row < col), 1.0, 0.0)
    target = mine + OWNERS * jnp.sum(earlier, axis=0, keepdims=True)
    pick = jnp.where(iota((SLOTS, size), 0).astype(jnp.float32) == target, 1.0, 0.0)
    slots = jnp.sum(pick * slot[...].astype(jnp.float32), axis=1, keepdims=True)
    counts = jnp.sum(pick * count[...].astype(jnp.float32), axis=1, keepdims=True)
    lane = iota((OWNERS, BLK), 1)
    facts = jnp.zeros((OWNERS, BLK), jnp.float32)
    for k, value in enumerate((slots[:OWNERS], counts[:OWNERS], slots[OWNERS:], counts[OWNERS:])):
        facts = jnp.where(lane == k, value, facts)
    send[pl.ds(22, OWNERS, stride=ROWS), :] = facts
    data = jnp.concatenate(
        [vis[:, c, :] for c in range(8)] + [uvo[:, 0, :], uvo[:, 1, :], wo[...]], 1
    )
    hi = data.astype(jnp.bfloat16)
    rest = data - hi.astype(jnp.float32)
    mid, lo = split(rest)
    pick = pick.astype(jnp.bfloat16)
    moved = dot_nn(jnp.concatenate([pick] * 3, 1), jnp.concatenate([hi, mid, lo], 0))
    for rank in range(2):
        part = slice(rank * OWNERS, rank * OWNERS + OWNERS)
        for c in range(11):
            at = 8 * rank + c if c < 8 else 16 + 3 * rank + c - 8
            send[pl.ds(at, OWNERS, stride=ROWS), :] = moved[part, c * BLK : c * BLK + BLK]

    pl.semaphore_wait(barrier, OWNERS - 1)

    def copy_to(k):
        peer = partner(me, k, 1)
        return pltpu.make_async_remote_copy(
            src_ref=send.at[pl.ds(pl.multiple_of(peer * ROWS, 8), SENT)],
            dst_ref=recv.at[pl.ds(pl.multiple_of(me * ROWS, 8), SENT)],
            send_sem=send_sem.at[k],
            recv_sem=recv_sem.at[k],
            device_id={"uv": peer},
            device_id_type=pl.DeviceIdType.MESH,
        )

    def start(k, carry):
        copy_to(k).start()
        return carry

    lax.fori_loop(0, OWNERS - 1, start, 0)
    own = pl.ds(pl.multiple_of(me * ROWS, 8), ROWS)
    recv[own, :] = send[own, :]

    def finish(k, carry):
        source = partner(me, k, -1)
        pltpu.make_async_remote_copy(
            src_ref=send.at[pl.ds(pl.multiple_of(source * ROWS, 8), SENT)],
            dst_ref=recv.at[pl.ds(pl.multiple_of(source * ROWS, 8), SENT)],
            send_sem=send_sem.at[k],
            recv_sem=recv_sem.at[k],
            device_id={"uv": source},
            device_id_type=pl.DeviceIdType.MESH,
        ).wait_recv()
        return carry

    lax.fori_loop(0, OWNERS - 1, finish, 0)
    got[...] = recv[...]
    known = recv[pl.ds(22, OWNERS, stride=ROWS), :]
    totals = jnp.zeros((1, BLK), jnp.float32)
    for k in (0, 2):
        here = iota((OWNERS, BLK), 1).astype(jnp.float32) == known[:, k : k + 1]
        totals += jnp.sum(jnp.where(here, known[:, k + 1 : k + 2], 0.0), axis=0, keepdims=True)
    known = jnp.concatenate([known, jnp.zeros((BLK - OWNERS, BLK), jnp.float32)], 0)
    listed = jnp.transpose(known)[0:8, :]
    info[...] = jnp.where(iota((8, BLK), 0) == 4, totals, listed).astype(jnp.int32)

    def drain(k, carry):
        copy_to(k).wait_send()
        return carry

    lax.fori_loop(0, OWNERS - 1, drain, 0)


def exchange(owner, slot, count, vis, uvo, wo):
    vmem = pl.BlockSpec(memory_space=pltpu.VMEM)
    return pl.pallas_call(
        exchange_kernel,
        out_shape=(
            jax.ShapeDtypeStruct((OWNERS * ROWS, BLK), jnp.float32),
            jax.ShapeDtypeStruct((8, BLK), jnp.int32),
        ),
        in_specs=[vmem] * 6,
        out_specs=(vmem, vmem),
        scratch_shapes=[
            pltpu.VMEM((OWNERS * ROWS, BLK), jnp.float32),
            pltpu.VMEM((OWNERS * ROWS, BLK), jnp.float32),
            pltpu.SemaphoreType.DMA((OWNERS,)),
            pltpu.SemaphoreType.DMA((OWNERS,)),
        ],
        compiler_params=pltpu.CompilerParams(
            collective_id=0, has_side_effects=True, vmem_limit_bytes=62 * 1024 * 1024
        ),
        name="exchange",
    )(owner, slot, count, vis, uvo, wo)


ROW_L = 0
ROW_B = 64
ROW_H = 128
ROW_C = 192
ROW_M = 208
ROW_U = 216
ROW_V = 232
ROW_E = 248
N_TRIG = 272
N_ONCE = 72
N_PHASE = 160


def once(k):
    if k < 6:
        base, k = (ROW_L, ROW_H)[k // 3], k % 3 + 1
        return ((0, 8 - k, base, 8 - k, 0), (8 - k, k, base, k, 0))
    if k == 6:
        return ((0, 4, ROW_L, 4, 0), (4, 4, ROW_H, 4, 0))
    return ((0, 8, (ROW_L, ROW_H)[k - 7], 0, 1),)


STEP = 8
TILE_A = (tuple(range(8)) + (16,), tuple(range(8, 16)))
C_ROWS = (0, 9 * 32, 17 * 32)


def phases(g, buf, ntab, sines, cosines, c_part, d_part):
    u = buf[g, 8:9, :]
    v = buf[g, 9:10, :]
    w = buf[g, 10:11, :]
    sub = iota((8, BLK), 0)
    row = sub.astype(jnp.float32)
    first_row = sub == 0
    halves = jnp.where(sub < 4, 1.0, -1.0)
    step0 = row * (0.5 / SUB)
    step1 = (row + 8.0) * (0.5 / SUB)

    def keep(at, turns):
        s, c = sincos_turns(turns)
        sines[at : at + 8, :] = s
        cosines[at : at + 8, :] = c

    keep(ROW_M, jnp.where(sub == 0, u, jnp.where(sub == 1, v, w)) * ntab[152:160, :])
    keep(ROW_U, u * step0)
    keep(ROW_U + 8, u * step1)
    keep(ROW_V, v * step0)
    keep(ROW_V + 8, v * step1)
    for k in range(N_ONCE // 8):
        s, c = sincos_turns(w * ntab[8 * k : 8 * k + 8, :])
        for first, size, base, a, diagonal in once(k):
            for table, value in ((sines, s), (cosines, c)):
                part = value[first : first + size, :]
                if diagonal:
                    table[pl.ds(base, size, stride=9), :] = part
                else:
                    table[base + a * 8 : base + a * 8 + size, :] = part
                    table[pl.ds(base + a, size, stride=8), :] = part
    for k in range(8):
        keep(ROW_B + 8 * k, w * ntab[N_ONCE + 8 * k : N_ONCE + 8 * k + 8, :])
    keep(ROW_C, w * ntab[136:144, :])
    keep(ROW_C + 8, w * ntab[144:152, :])

    vis = buf[g, 0:8, :]
    swapped = pltpu.roll(vis, 4, 0) * halves
    for t in range(2):
        cv = cosines[ROW_V + 8 * t : ROW_V + 8 * t + 8, :]
        sv = sines[ROW_V + 8 * t : ROW_V + 8 * t + 8, :]
        if t == 0:
            c16 = jnp.where(first_row, cosines[ROW_M + 1 : ROW_M + 2, :], 0.0)
            sv = jnp.where(first_row, -sines[ROW_M + 1 : ROW_M + 2, :], sv)
        for c in range(8):
            one = jnp.broadcast_to(vis[c : c + 1, :], (8, BLK))
            two = jnp.broadcast_to(swapped[c : c + 1, :], (8, BLK))
            at = t * 128 + c * 16
            odd = two * sv
            if t == 0:
                odd = odd + one * c16
            d_part[at : at + 8, :] = one * cv
            d_part[at + 8 : at + 16, :] = odd

    cu0 = cosines[ROW_U : ROW_U + 8, :]
    cu1 = cosines[ROW_U + 8 : ROW_U + 16, :]
    su0 = sines[ROW_U : ROW_U + 8, :]
    su1 = sines[ROW_U + 8 : ROW_U + 16, :]
    c16 = cosines[ROW_M : ROW_M + 1, :]
    s16 = sines[ROW_M : ROW_M + 1, :]
    for at, to in ((ROW_C, ROW_E), (ROW_C + 8, ROW_E + 8), (ROW_M, ROW_E + 16)):
        c, s = cosines[at : at + 8, :], sines[at : at + 8, :]
        cosines[to : to + 8, :] = c * c16 + s * s16
        sines[to : to + 8, :] = s * c16 - c * s16
    for t in range(2):
        for i, a in enumerate(TILE_A[t]):
            edge = slice(ROW_E + a, ROW_E + a + 1)
            if a < 8:
                p0 = slice(ROW_L + a * 8, ROW_L + a * 8 + 8)
                p1 = pl.ds(ROW_B + a, 8, stride=8)
            elif a < 16:
                p0 = slice(ROW_B + (a - 8) * 8, ROW_B + (a - 8) * 8 + 8)
                p1 = slice(ROW_H + (a - 8) * 8, ROW_H + (a - 8) * 8 + 8)
            else:
                p0 = slice(ROW_C, ROW_C + 8)
                p1 = slice(ROW_C + 8, ROW_C + 16)
                edge = slice(ROW_E + 18, ROW_E + 19)
            cw0, sw0 = cosines[p0, :], sines[p0, :]
            cw1, sw1 = cosines[p1, :], sines[p1, :]
            cos_2 = jnp.where(first_row, cosines[edge, :], cw0 * su0)
            sin_2 = jnp.where(first_row, sines[edge, :], sw0 * su0)
            cos_rows = [cw0 * cu0, cw1 * cu1, cos_2, cw1 * su1]
            sin_rows = [sw0 * cu0, sw1 * cu1, sin_2, sw1 * su1]
            at = C_ROWS[t] + i * 32
            for part, rows in enumerate((cos_rows, sin_rows)):
                for k in range(4):
                    c_part[at + 8 * k : at + 8 * k + 8, part * BLK : part * BLK + BLK] = rows[k]


def add_images(s, c_part, d_part, acc):
    lane = iota((SUB, BLK), 1)
    for t in range(2):
        d_both = jnp.concatenate(
            [
                jnp.concatenate([d, jnp.concatenate([d[64:, :], -d[:64, :]], 0)], 1)
                for d in split(d_part[t * 128 : t * 128 + 128, :])
            ],
            0,
        )
        c_hi, c_lo = split(c_part[C_ROWS[t] : C_ROWS[t + 1], :])
        o_hi = dot_nt(c_hi, d_both)
        o_lo = dot_nt(c_lo, d_both)
        total = None
        for i, a in enumerate(TILE_A[t]):
            hi = o_hi[i * 32 : i * 32 + 32, :]
            lo = o_lo[i * 32 : i * 32 + 32, 0:BLK]
            value = hi[:, 0:BLK] + hi[:, BLK:] + lo
            if total is None:
                total = value
            elif a == 16:
                total = jnp.where((lane & 15) == 8, value, total)
            else:
                total = jnp.where((lane & 7) == i, value, total)
        acc[s, t] += total


def grid_kernel(
    info,
    offset,
    taper,
    got,
    tile,
    base,
    slot_of,
    buf,
    ntab,
    sines_0,
    cosines_0,
    c_0,
    d_0,
    sines_1,
    cosines_1,
    c_1,
    d_1,
    acc,
    spread,
):
    slot_of[0] = OWNED

    def place_slot(s, first):
        number = lax.shift_right_logical(info[4, s] + (BLK - 1), 7)
        base[s] = first * BLK

        def name_group(i, carry):
            slot_of[first + i + 1] = s
            return carry

        lax.fori_loop(0, number, name_group, 0)
        return first + number

    groups = lax.fori_loop(0, OWNED, place_slot, 0)
    slot_of[groups + 1] = OWNED

    def clear_group(g, carry):
        buf[g] = jnp.zeros((16, BLK), jnp.float32)
        return carry

    lax.fori_loop(0, groups + 2, clear_group, 0)
    lane8 = iota((8, BLK), 1)

    def compact(k, carry):
        moved = []
        for i4 in range(4):
            i = k * 4 + i4
            others = got[pl.ds(i * ROWS + 16, 8), :]
            for rank in range(2):
                s = info[2 * rank, i]
                n = info[2 * rank + 1, i]
                at = base[s]
                base[s] = at + n
                g = lax.shift_right_logical(at, 7)
                shift = at & (BLK - 1)
                vis = pltpu.roll(got[pl.ds(i * ROWS + 8 * rank, 8), :], shift, 1)
                rest = pltpu.roll(others if rank == 0 else pltpu.roll(others, 5, 0), shift, 1)
                here = (lane8 >= shift) & (lane8 < shift + n)
                after = lane8 < shift + n - BLK
                moved.append((g, vis, rest, here, after))
        for g, vis, rest, here, after in moved:
            pltpu.store(buf.at[g, 0:8, :], vis, mask=here)
            pltpu.store(buf.at[g, 8:16, :], rest, mask=here)
            pltpu.store(buf.at[g + 1, 0:8, :], vis, mask=after)
            pltpu.store(buf.at[g + 1, 8:16, :], rest, mask=after)
        return carry

    lax.fori_loop(0, OWNERS // 4, compact, 0)

    def n_of(a, b):
        l = b * (0.5 / SUB)
        m = a * (0.5 / SUB)
        return 1.0 - jnp.sqrt(1.0 - l * l - m * m)

    row = iota((8, BLK), 0).astype(jnp.float32)
    for k in range(N_ONCE // 8):
        a, b = row, row
        for first, size, base, y, diagonal in once(k):
            shift = 0.0 if base == ROW_L else 8.0
            here = row >= float(first)
            a = jnp.where(here, row + shift if diagonal else float(y) + shift, a)
            b = jnp.where(here, row - float(first) + shift, b)
        ntab[8 * k : 8 * k + 8, :] = n_of(a, b)
    for k in range(8):
        ntab[N_ONCE + 8 * k : N_ONCE + 8 * k + 8, :] = n_of(float(8 + k), row)
    ntab[136:144, :] = n_of(16.0, row)
    ntab[144:152, :] = n_of(16.0, row + 8.0)
    ntab[152:160, :] = jnp.where(
        row < 2.0, 16 * 0.5 / SUB, n_of(16.0, jnp.full((8, BLK), 16.0, jnp.float32))
    )

    for s in range(OWNED):
        acc[s] = jnp.zeros((2, SUB, BLK), jnp.float32)

    def two_groups(g):
        phases(g, buf, ntab, sines_0, cosines_0, c_0, d_0)
        add_images(slot_of[g], c_1, d_1, acc)
        phases(g + 1, buf, ntab, sines_1, cosines_1, c_1, d_1)
        add_images(slot_of[g + 1], c_0, d_0, acc)

    def more_groups(i, carry):
        for k in range(0, STEP, 2):
            two_groups(STEP * i + k)
        return carry

    def rest(i, carry):
        two_groups(2 * i)
        return carry

    whole = lax.div(groups, STEP)
    steps = lax.div(groups + 1, 2)
    lax.fori_loop(0, whole, more_groups, 0)
    lax.fori_loop(STEP // 2 * whole, steps, rest, 0)
    add_images(slot_of[2 * steps], c_1, d_1, acc)

    def y_of(high, sign, low):
        i = high * 8 + low
        return jnp.where(sign == 0, 16 + i, jnp.where(i == 0, 0, 16 - i))

    def x_of(j):
        return jnp.where(j < 16, j + 16, jnp.where(j == 16, 0, 32 - j))

    def exact(a, b, dims):
        return lax.dot_general(
            a, b, (dims, ((), ())), precision=lax.Precision.HIGHEST,
            preferred_element_type=jnp.float32,
        )

    pick_x = (x_of(iota((SUB, SUB), 0)) == iota((SUB, SUB), 1)).astype(jnp.float32)
    place = iota((SUB, 2 * BLK), 1)
    pick_y = (
        y_of(lax.shift_right_logical(place, 7), lax.shift_right_logical(place, 3) & 1, place & 7)
        == iota((SUB, 2 * BLK), 0)
    ).astype(jnp.float32)
    weight = exact(exact(pick_x, taper[...], ((1,), (1,))), pick_y, ((1,), (0,))) * (
        1.0 / math.sqrt(BLK)
    )

    row, col = iota((BLK, BLK), 0), iota((BLK, BLK), 1)
    turn = (x_of(row & (SUB - 1)) * (col & (SUB - 1))) & (SUB - 1)
    sx, cx = sincos_turns(turn.astype(jnp.float32) * (1.0 / SUB))
    same = lax.shift_right_logical(row, 5) == lax.shift_right_logical(col, 5)
    w_hi, w_lo = split(
        jnp.concatenate(
            [jnp.where(same, cx * (1.0 / SUB), 0.0), jnp.where(same, sx * (-1.0 / SUB), 0.0)], 1
        )
    )
    w_all = jnp.concatenate([w_hi, w_hi, w_lo], 0)
    lane = iota((SUB, BLK), 1)
    even_lane = (lane & 8) == 0
    lane16 = iota((16, BLK), 1)
    first_row = iota((8, BLK), 0) == 0
    turn_sign = jnp.where(lane16 < BLK // 2, 1.0, -1.0)
    edge = iota((16, BLK), 0) == 0

    for q in range(OWNED // 4):
        rows = []
        for s in range(4 * q, 4 * q + 4):
            both = []
            for t in range(2):
                a = acc[s, t]
                y = jnp.where(even_lane, a + pltpu.roll(a, BLK - 8, 1), pltpu.roll(a, 8, 1) - a)
                if t == 0:
                    y = jnp.where((lane & 7) == 0, a, y)
                cos_x, sin_x = y[0:16, :], y[16:32, :]
                turned = pltpu.roll(sin_x, BLK // 2, 1) * turn_sign
                plus = jnp.where(edge, cos_x, cos_x + turned)
                minus = jnp.where(edge, sin_x, cos_x - turned)
                both.append(jnp.concatenate([plus, minus], 0))
            rows.append(jnp.concatenate(both, 1) * weight)
        x_hi, x_lo = split(jnp.transpose(jnp.concatenate(rows, 0)))
        z = dot_nn(jnp.concatenate([x_hi, x_lo, x_hi], 1), w_all)
        rights = [offset[1, 4 * q + j] for j in range(4)]
        inside = [(lane16 >= right) & (lane16 < right + SUB) for right in rights]
        for t in range(2):
            for p in range(4):
                re = z[t * 128 + p * 16 : t * 128 + p * 16 + 16, :]
                im = z[t * 128 + p * 16 + 64 : t * 128 + p * 16 + 80, :]
                re, im = re[:, 0:BLK] - im[:, BLK:], re[:, BLK:] + im[:, 0:BLK]
                up, down = (re[:8], im[:8]), (re[8:], im[8:])
                tops = [up[0] + down[0], up[1] + down[1]]
                lows = [up[1] - down[1], down[0] - up[0]]
                if t == 0:
                    tops = [jnp.where(first_row, x, y) for x, y in zip(up, tops)]
                    lows = [jnp.where(first_row, x, y) for x, y in zip(down, lows)]
                joined = [jnp.concatenate(pair, 0) for pair in zip(tops, lows)]
                for j in range(4):
                    at = (4 * q + j) * SUB + t * 16
                    shift = (rights[j] + (BLK - SUB * j)) & (BLK - 1)
                    for part in range(2):
                        spread[p, at : at + 16, part * BLK : part * BLK + BLK] = jnp.where(
                            inside[j], pltpu.roll(joined[part], shift, 1), 0.0
                        )

    lane = iota((1, OWNED * SUB), 1)
    corner = jnp.zeros((1, OWNED * SUB), jnp.int32)
    for s in range(OWNED):
        corner = jnp.where(lax.shift_right_logical(lane, 5) == s, offset[0, s], corner)
    high = (lax.shift_right_logical(lane, 4) & 1) * 8 + (lane & 7)
    low_half = (lane & 8) == 0
    yy = jnp.where(low_half | (high > 0), 16 + high, 0)
    use_cos = low_half | (high == 0)

    def turned(at, y):
        return sincos_turns(((at * y) & (SUB - 1)).astype(jnp.float32) * (1.0 / SUB))

    s_at, c_at = turned(iota((TILE, BLK), 0), jnp.broadcast_to(yy[:, 0:BLK], (TILE, BLK)))
    use_cos = jnp.broadcast_to(use_cos[:, 0:BLK], (TILE, BLK))
    first = jnp.concatenate([jnp.where(use_cos, c_at, s_at)] * 4, 1)
    second = jnp.concatenate([jnp.where(use_cos, s_at, -c_at)] * 4, 1)
    s_corner, c_corner = turned(corner, yy)
    ky = iota((TILE, OWNED * SUB), 0) - corner
    inside = (ky >= 0) & (ky < SUB)
    h_hi, h_lo = split(jnp.where(inside, first * c_corner + second * s_corner, 0.0))
    h_both = jnp.concatenate([h_hi, h_lo], 0)
    for p in range(4):
        b_hi, b_lo = split(spread[p])
        o = dot_nn(h_both, b_hi)
        o = o[0:TILE, :] + o[TILE:, :] + dot_nn(h_hi, b_lo)
        tile[p] = o[:, 0:BLK]
        tile[p + 4] = o[:, BLK:]


def grid_tile(info, offset, taper, got):
    smem = pl.BlockSpec(memory_space=pltpu.SMEM)
    vmem = pl.BlockSpec(memory_space=pltpu.VMEM)
    f32 = jnp.float32
    factors = [
        pltpu.VMEM((N_TRIG, BLK), f32),
        pltpu.VMEM((N_TRIG, BLK), f32),
        pltpu.VMEM((C_ROWS[2], 2 * BLK), f32),
        pltpu.VMEM((256, BLK), f32),
    ]
    return pl.pallas_call(
        grid_kernel,
        out_shape=jax.ShapeDtypeStruct((8, TILE, TILE), f32),
        in_specs=[smem, smem, vmem, vmem],
        out_specs=vmem,
        scratch_shapes=[
            pltpu.SMEM((OWNED,), jnp.int32),
            pltpu.SMEM((MAX_GROUPS + 2,), jnp.int32),
            pltpu.VMEM((MAX_GROUPS, 16, BLK), f32),
            pltpu.VMEM((N_PHASE, BLK), f32),
            *factors,
            *factors,
            pltpu.VMEM((OWNED + 1, 2, SUB, BLK), f32),
            pltpu.VMEM((4, OWNED * SUB, 2 * BLK), f32),
        ],
        compiler_params=pltpu.CompilerParams(vmem_limit_bytes=62 * 1024 * 1024),
        name="grid_tile",
    )(info, offset, taper, got)


FAR_FIRST = (6, 5, 7, 2, 4, 1, 3)


def near(me, k, sign):
    return (me // 4 + k // 4) % 2 * 4 + (me + 4 + sign * (k % 4)) % 4


def gather_kernel(tile, recv, send_sem, recv_sem):
    me = lax.axis_index("freq")
    own = pltpu.make_async_copy(
        tile.at[:, pl.ds(pl.multiple_of(me * (TILE // GROUPS), 8), TILE // GROUPS)],
        recv.at[0],
        recv_sem.at[0],
    )
    own.start()
    barrier = pltpu.get_barrier_semaphore()
    for k in FAR_FIRST:
        pl.semaphore_signal(
            barrier,
            inc=1,
            device_id={"freq": near(me, k, 1)},
            device_id_type=pl.DeviceIdType.MESH,
        )
    pl.semaphore_wait(barrier, GROUPS - 1)
    strip = TILE // GROUPS
    copies = []
    for k in FAR_FIRST:
        peer = near(me, k, 1)
        copy = pltpu.make_async_remote_copy(
            src_ref=tile.at[:, pl.ds(pl.multiple_of(peer * strip, 8), strip)],
            dst_ref=recv.at[k],
            send_sem=send_sem.at[k],
            recv_sem=recv_sem.at[k],
            device_id={"freq": peer},
            device_id_type=pl.DeviceIdType.MESH,
        )
        copy.start()
        copies.append(copy)
    own.wait()
    for copy in copies:
        copy.wait_recv()
    for copy in copies:
        copy.wait_send()


def sum_kernel(parts, out):
    value = parts[0]
    for k in range(1, GROUPS):
        value = value + parts[k]
    for c in range(8):
        out[:, c, :] = value[c]


def sum_over_freq(tile):
    strip = TILE // GROUPS
    anywhere = pl.BlockSpec(memory_space=pl.ANY)
    vmem = pl.BlockSpec(memory_space=pltpu.VMEM)
    parts = pl.pallas_call(
        gather_kernel,
        out_shape=jax.ShapeDtypeStruct((GROUPS, 8, strip, TILE), jnp.float32),
        in_specs=[anywhere],
        out_specs=anywhere,
        scratch_shapes=[
            pltpu.SemaphoreType.DMA((GROUPS,)),
            pltpu.SemaphoreType.DMA((GROUPS,)),
        ],
        compiler_params=pltpu.CompilerParams(
            collective_id=1, has_side_effects=True, vmem_limit_bytes=62 * 1024 * 1024
        ),
        name="gather_over_freq",
    )(tile)
    return pl.pallas_call(
        sum_kernel,
        out_shape=jax.ShapeDtypeStruct((strip, 8, TILE), jnp.float32),
        in_specs=[vmem],
        out_specs=vmem,
        compiler_params=pltpu.CompilerParams(vmem_limit_bytes=62 * 1024 * 1024),
        name="sum_over_freq",
    )(parts)


def shards(
    visibility, uv_offset, w_offset, taper, row_count, block_owner, block_slot, subgrid_offset
):
    got, info = exchange(
        block_owner[:, :, 0], block_slot, row_count, visibility[0], uv_offset[0], w_offset[0]
    )
    return sum_over_freq(grid_tile(info, subgrid_offset.T, taper, got))


def solution(mesh):
    placed = (
        P("freq", "uv", None, None),
        P("freq", "uv", None, None),
        P("freq", "uv", None),
        P(),
        P("freq", "uv"),
        P("freq", "uv", None),
        P("freq", "uv"),
        P("uv", None),
    )
    return jax.shard_map(
        shards, mesh=mesh, in_specs=placed, out_specs=P(("uv", "freq"), None, None), check_vma=False
    )
```

```python
import functools
import math

import jax
import jax.numpy as jnp
from jax import lax
from jax.experimental import pallas as pl
from jax.experimental.pallas import tpu as pltpu
from jax.sharding import PartitionSpec as P

SUB = 32
BLK = 128
TILE = 128
OWNERS = 32
GROUPS = 8
OWNED = 16
SLOTS = 64
ROWS = 24
SENT = 23
MAX_GROUPS = 82

SIN_POLY = (
    4.442882919124345,
    -7.308245686509104,
    3.6063542184332804,
    -0.8461116503752865,
    0.10982451642699691,
)
COS_POLY = (
    1.4142134962552289,
    -6.978850948563853,
    5.7394603769076955,
    -1.8835579059892091,
    0.31068802753070307,
)


def horner(z, coefficients):
    value = z * coefficients[-1] + coefficients[-2]
    for c in coefficients[-3::-1]:
        value = value * z + c
    return value


def sincos_turns(turns):
    f = turns - jnp.round(turns)
    z = f * f
    s = horner(z, SIN_POLY) * f
    c = horner(z, COS_POLY)
    return s * c, 1.0 - s * s


def split(x):
    hi = x.astype(jnp.bfloat16)
    lo = (x - hi.astype(jnp.float32)).astype(jnp.bfloat16)
    return hi, lo


def dot_nt(a, b):
    return lax.dot_general(a, b, (((1,), (1,)), ((), ())), preferred_element_type=jnp.float32)


def dot_nn(a, b):
    return lax.dot_general(a, b, (((1,), (0,)), ((), ())), preferred_element_type=jnp.float32)


def iota(shape, axis):
    return lax.broadcasted_iota(jnp.int32, shape, axis)


def partner(me, i, sign):
    j = i // 4
    dz = jnp.where(j % 2 == 0, 4 + j // 2, 4 - (j + 1) // 2)
    dy = 1 - (i % 4) // 2
    dc = 1 - i % 2
    y = (me // 16 + dy) % 2
    z = (me // 2 + 8 + sign * dz) % 8
    return y * 16 + z * 2 + (me + dc) % 2


def exchange_kernel(
    owner, slot, count, vis, uvo, wo, got, info, send, recv, send_sem, recv_sem
):
    me = lax.axis_index("uv")
    barrier = pltpu.get_barrier_semaphore()

    def greet(k, carry):
        peer = partner(me, k, 1)
        pl.semaphore_signal(
            barrier, inc=1, device_id={"uv": peer}, device_id_type=pl.DeviceIdType.MESH
        )
        return carry

    lax.fori_loop(0, OWNERS - 1, greet, 0)

    size = vis.shape[0]
    mine = owner[...].astype(jnp.float32)
    across = jnp.broadcast_to(mine, (size, size))
    row, col = iota((size, size), 0), iota((size, size), 1)
    down = jnp.sum(jnp.where(row == col, across, 0.0), axis=1, keepdims=True)
    earlier = jnp.where((down == across) & (row < col), 1.0, 0.0)
    target = mine + OWNERS * jnp.sum(earlier, axis=0, keepdims=True)
    pick = jnp.where(iota((SLOTS, size), 0).astype(jnp.float32) == target, 1.0, 0.0)
    slots = jnp.sum(pick * slot[...].astype(jnp.float32), axis=1, keepdims=True)
    counts = jnp.sum(pick * count[...].astype(jnp.float32), axis=1, keepdims=True)
    lane = iota((OWNERS, BLK), 1)
    facts = jnp.zeros((OWNERS, BLK), jnp.float32)
    for k, value in enumerate((slots[:OWNERS], counts[:OWNERS], slots[OWNERS:], counts[OWNERS:])):
        facts = jnp.where(lane == k, value, facts)
    send[pl.ds(22, OWNERS, stride=ROWS), :] = facts
    data = jnp.concatenate(
        [vis[:, c, :] for c in range(8)] + [uvo[:, 0, :], uvo[:, 1, :], wo[...]], 1
    )
    hi = data.astype(jnp.bfloat16)
    rest = data - hi.astype(jnp.float32)
    mid, lo = split(rest)
    pick = pick.astype(jnp.bfloat16)
    moved = dot_nn(jnp.concatenate([pick] * 3, 1), jnp.concatenate([hi, mid, lo], 0))
    for rank in range(2):
        part = slice(rank * OWNERS, rank * OWNERS + OWNERS)
        for c in range(11):
            at = 8 * rank + c if c < 8 else 16 + 3 * rank + c - 8
            send[pl.ds(at, OWNERS, stride=ROWS), :] = moved[part, c * BLK : c * BLK + BLK]

    pl.semaphore_wait(barrier, OWNERS - 1)

    def copy_to(k):
        peer = partner(me, k, 1)
        return pltpu.make_async_remote_copy(
            src_ref=send.at[pl.ds(pl.multiple_of(peer * ROWS, 8), SENT)],
            dst_ref=recv.at[pl.ds(pl.multiple_of(me * ROWS, 8), SENT)],
            send_sem=send_sem.at[k],
            recv_sem=recv_sem.at[k],
            device_id={"uv": peer},
            device_id_type=pl.DeviceIdType.MESH,
        )

    def start(k, carry):
        copy_to(k).start()
        return carry

    lax.fori_loop(0, OWNERS - 1, start, 0)
    own = pl.ds(pl.multiple_of(me * ROWS, 8), ROWS)
    recv[own, :] = send[own, :]

    def finish(k, carry):
        source = partner(me, k, -1)
        pltpu.make_async_remote_copy(
            src_ref=send.at[pl.ds(pl.multiple_of(source * ROWS, 8), SENT)],
            dst_ref=recv.at[pl.ds(pl.multiple_of(source * ROWS, 8), SENT)],
            send_sem=send_sem.at[k],
            recv_sem=recv_sem.at[k],
            device_id={"uv": source},
            device_id_type=pl.DeviceIdType.MESH,
        ).wait_recv()
        return carry

    lax.fori_loop(0, OWNERS - 1, finish, 0)
    got[...] = recv[...]
    known = recv[pl.ds(22, OWNERS, stride=ROWS), :]
    totals = jnp.zeros((1, BLK), jnp.float32)
    for k in (0, 2):
        here = iota((OWNERS, BLK), 1).astype(jnp.float32) == known[:, k : k + 1]
        totals += jnp.sum(jnp.where(here, known[:, k + 1 : k + 2], 0.0), axis=0, keepdims=True)
    known = jnp.concatenate([known, jnp.zeros((BLK - OWNERS, BLK), jnp.float32)], 0)
    listed = jnp.transpose(known)[0:8, :]
    info[...] = jnp.where(iota((8, BLK), 0) == 4, totals, listed).astype(jnp.int32)

    def drain(k, carry):
        copy_to(k).wait_send()
        return carry

    lax.fori_loop(0, OWNERS - 1, drain, 0)


def exchange(owner, slot, count, vis, uvo, wo):
    vmem = pl.BlockSpec(memory_space=pltpu.VMEM)
    return pl.pallas_call(
        exchange_kernel,
        out_shape=(
            jax.ShapeDtypeStruct((OWNERS * ROWS, BLK), jnp.float32),
            jax.ShapeDtypeStruct((8, BLK), jnp.int32),
        ),
        in_specs=[vmem] * 6,
        out_specs=(vmem, vmem),
        scratch_shapes=[
            pltpu.VMEM((OWNERS * ROWS, BLK), jnp.float32),
            pltpu.VMEM((OWNERS * ROWS, BLK), jnp.float32),
            pltpu.SemaphoreType.DMA((OWNERS,)),
            pltpu.SemaphoreType.DMA((OWNERS,)),
        ],
        compiler_params=pltpu.CompilerParams(
            collective_id=0, has_side_effects=True, vmem_limit_bytes=62 * 1024 * 1024
        ),
        name="exchange",
    )(owner, slot, count, vis, uvo, wo)


ROW_L = 0
ROW_B = 64
ROW_H = 128
ROW_C = 192
ROW_M = 208
ROW_U = 216
ROW_V = 232
ROW_E = 248
N_TRIG = 272
N_ONCE = 72
N_PHASE = 160


def once(k):
    if k < 6:
        base, k = (ROW_L, ROW_H)[k // 3], k % 3 + 1
        return ((0, 8 - k, base, 8 - k, 0), (8 - k, k, base, k, 0))
    if k == 6:
        return ((0, 4, ROW_L, 4, 0), (4, 4, ROW_H, 4, 0))
    return ((0, 8, (ROW_L, ROW_H)[k - 7], 0, 1),)


STEP = 12
TILE_A = (tuple(range(8)) + (16,), tuple(range(8, 16)))
C_ROWS = (0, 9 * 32, 17 * 32)


def phases(g, buf, ntab, sines, cosines, c_part, d_part):
    u = buf[g, 8:9, :]
    v = buf[g, 9:10, :]
    w = buf[g, 10:11, :]
    sub = iota((8, BLK), 0)
    row = sub.astype(jnp.float32)
    first_row = sub == 0
    halves = jnp.where(sub < 4, 1.0, -1.0)
    step0 = row * (0.5 / SUB)
    step1 = (row + 8.0) * (0.5 / SUB)

    def keep(at, turns):
        s, c = sincos_turns(turns)
        sines[at : at + 8, :] = s
        cosines[at : at + 8, :] = c

    keep(ROW_M, jnp.where(sub == 0, u, jnp.where(sub == 1, v, w)) * ntab[152:160, :])
    keep(ROW_U, u * step0)
    keep(ROW_U + 8, u * step1)
    keep(ROW_V, v * step0)
    keep(ROW_V + 8, v * step1)
    for k in range(N_ONCE // 8):
        s, c = sincos_turns(w * ntab[8 * k : 8 * k + 8, :])
        for first, size, base, a, diagonal in once(k):
            for table, value in ((sines, s), (cosines, c)):
                part = value[first : first + size, :]
                if diagonal:
                    table[pl.ds(base, size, stride=9), :] = part
                else:
                    table[base + a * 8 : base + a * 8 + size, :] = part
                    table[pl.ds(base + a, size, stride=8), :] = part
    for k in range(8):
        keep(ROW_B + 8 * k, w * ntab[N_ONCE + 8 * k : N_ONCE + 8 * k + 8, :])
    keep(ROW_C, w * ntab[136:144, :])
    keep(ROW_C + 8, w * ntab[144:152, :])

    vis = buf[g, 0:8, :]
    swapped = pltpu.roll(vis, 4, 0) * halves
    for t in range(2):
        cv = cosines[ROW_V + 8 * t : ROW_V + 8 * t + 8, :]
        sv = sines[ROW_V + 8 * t : ROW_V + 8 * t + 8, :]
        if t == 0:
            c16 = jnp.where(first_row, cosines[ROW_M + 1 : ROW_M + 2, :], 0.0)
            sv = jnp.where(first_row, -sines[ROW_M + 1 : ROW_M + 2, :], sv)
        for c in range(8):
            one = jnp.broadcast_to(vis[c : c + 1, :], (8, BLK))
            two = jnp.broadcast_to(swapped[c : c + 1, :], (8, BLK))
            at = t * 128 + c * 16
            odd = two * sv
            if t == 0:
                odd = odd + one * c16
            d_part[at : at + 8, :] = one * cv
            d_part[at + 8 : at + 16, :] = odd

    cu0 = cosines[ROW_U : ROW_U + 8, :]
    cu1 = cosines[ROW_U + 8 : ROW_U + 16, :]
    su0 = sines[ROW_U : ROW_U + 8, :]
    su1 = sines[ROW_U + 8 : ROW_U + 16, :]
    c16 = cosines[ROW_M : ROW_M + 1, :]
    s16 = sines[ROW_M : ROW_M + 1, :]
    for at, to in ((ROW_C, ROW_E), (ROW_C + 8, ROW_E + 8), (ROW_M, ROW_E + 16)):
        c, s = cosines[at : at + 8, :], sines[at : at + 8, :]
        cosines[to : to + 8, :] = c * c16 + s * s16
        sines[to : to + 8, :] = s * c16 - c * s16
    for t in range(2):
        for i, a in enumerate(TILE_A[t]):
            edge = slice(ROW_E + a, ROW_E + a + 1)
            if a < 8:
                p0 = slice(ROW_L + a * 8, ROW_L + a * 8 + 8)
                p1 = pl.ds(ROW_B + a, 8, stride=8)
            elif a < 16:
                p0 = slice(ROW_B + (a - 8) * 8, ROW_B + (a - 8) * 8 + 8)
                p1 = slice(ROW_H + (a - 8) * 8, ROW_H + (a - 8) * 8 + 8)
            else:
                p0 = slice(ROW_C, ROW_C + 8)
                p1 = slice(ROW_C + 8, ROW_C + 16)
                edge = slice(ROW_E + 18, ROW_E + 19)
            cw0, sw0 = cosines[p0, :], sines[p0, :]
            cw1, sw1 = cosines[p1, :], sines[p1, :]
            cos_2 = jnp.where(first_row, cosines[edge, :], cw0 * su0)
            sin_2 = jnp.where(first_row, sines[edge, :], sw0 * su0)
            cos_rows = [cw0 * cu0, cw1 * cu1, cos_2, cw1 * su1]
            sin_rows = [sw0 * cu0, sw1 * cu1, sin_2, sw1 * su1]
            at = C_ROWS[t] + i * 32
            for part, rows in enumerate((cos_rows, sin_rows)):
                for k in range(4):
                    c_part[at + 8 * k : at + 8 * k + 8, part * BLK : part * BLK + BLK] = rows[k]


def add_images(s, c_part, d_part, acc):
    lane = iota((SUB, BLK), 1)
    for t in range(2):
        d_both = jnp.concatenate(
            [
                jnp.concatenate([d, jnp.concatenate([d[64:, :], -d[:64, :]], 0)], 1)
                for d in split(d_part[t * 128 : t * 128 + 128, :])
            ],
            0,
        )
        c_hi, c_lo = split(c_part[C_ROWS[t] : C_ROWS[t + 1], :])
        o_hi = dot_nt(c_hi, d_both)
        o_lo = dot_nt(c_lo, d_both)
        total = None
        for i, a in enumerate(TILE_A[t]):
            hi = o_hi[i * 32 : i * 32 + 32, :]
            lo = o_lo[i * 32 : i * 32 + 32, 0:BLK]
            value = hi[:, 0:BLK] + hi[:, BLK:] + lo
            if total is None:
                total = value
            elif a == 16:
                total = jnp.where((lane & 15) == 8, value, total)
            else:
                total = jnp.where((lane & 7) == i, value, total)
        acc[s, t] += total


def grid_kernel(
    info,
    offset,
    taper,
    got,
    tile,
    base,
    slot_of,
    buf,
    ntab,
    sines_0,
    cosines_0,
    c_0,
    d_0,
    sines_1,
    cosines_1,
    c_1,
    d_1,
    acc,
    spread,
):
    slot_of[0] = OWNED

    def place_slot(s, first):
        number = lax.shift_right_logical(info[4, s] + (BLK - 1), 7)
        base[s] = first * BLK

        def name_group(i, carry):
            slot_of[first + i + 1] = s
            return carry

        lax.fori_loop(0, number, name_group, 0)
        return first + number

    groups = lax.fori_loop(0, OWNED, place_slot, 0)
    slot_of[groups + 1] = OWNED

    def clear_group(g, carry):
        buf[g] = jnp.zeros((16, BLK), jnp.float32)
        return carry

    lax.fori_loop(0, groups + 2, clear_group, 0)
    lane8 = iota((8, BLK), 1)

    def compact(k, carry):
        moved = []
        for i4 in range(8):
            i = k * 8 + i4
            others = got[pl.ds(i * ROWS + 16, 8), :]
            for rank in range(2):
                s = info[2 * rank, i]
                n = info[2 * rank + 1, i]
                at = base[s]
                base[s] = at + n
                g = lax.shift_right_logical(at, 7)
                shift = at & (BLK - 1)
                vis = pltpu.roll(got[pl.ds(i * ROWS + 8 * rank, 8), :], shift, 1)
                rest = pltpu.roll(others if rank == 0 else pltpu.roll(others, 5, 0), shift, 1)
                here = (lane8 >= shift) & (lane8 < shift + n)
                after = lane8 < shift + n - BLK
                moved.append((g, vis, rest, here, after))
        for g, vis, rest, here, after in moved:
            pltpu.store(buf.at[g, 0:8, :], vis, mask=here)
            pltpu.store(buf.at[g, 8:16, :], rest, mask=here)
            pltpu.store(buf.at[g + 1, 0:8, :], vis, mask=after)
            pltpu.store(buf.at[g + 1, 8:16, :], rest, mask=after)
        return carry

    lax.fori_loop(0, OWNERS // 8, compact, 0)

    def n_of(a, b):
        l = b * (0.5 / SUB)
        m = a * (0.5 / SUB)
        return 1.0 - jnp.sqrt(1.0 - l * l - m * m)

    row = iota((8, BLK), 0).astype(jnp.float32)
    for k in range(N_ONCE // 8):
        a, b = row, row
        for first, size, base, y, diagonal in once(k):
            shift = 0.0 if base == ROW_L else 8.0
            here = row >= float(first)
            a = jnp.where(here, row + shift if diagonal else float(y) + shift, a)
            b = jnp.where(here, row - float(first) + shift, b)
        ntab[8 * k : 8 * k + 8, :] = n_of(a, b)
    for k in range(8):
        ntab[N_ONCE + 8 * k : N_ONCE + 8 * k + 8, :] = n_of(float(8 + k), row)
    ntab[136:144, :] = n_of(16.0, row)
    ntab[144:152, :] = n_of(16.0, row + 8.0)
    ntab[152:160, :] = jnp.where(
        row < 2.0, 16 * 0.5 / SUB, n_of(16.0, jnp.full((8, BLK), 16.0, jnp.float32))
    )

    for s in range(OWNED):
        acc[s] = jnp.zeros((2, SUB, BLK), jnp.float32)

    def two_groups(g):
        phases(g, buf, ntab, sines_0, cosines_0, c_0, d_0)
        add_images(slot_of[g], c_1, d_1, acc)
        phases(g + 1, buf, ntab, sines_1, cosines_1, c_1, d_1)
        add_images(slot_of[g + 1], c_0, d_0, acc)

    def more_groups(i, carry):
        for k in range(0, STEP, 2):
            two_groups(STEP * i + k)
        return carry

    def rest(i, carry):
        two_groups(2 * i)
        return carry

    whole = lax.div(groups, STEP)
    steps = lax.div(groups + 1, 2)
    lax.fori_loop(0, whole, more_groups, 0)
    lax.fori_loop(STEP // 2 * whole, steps, rest, 0)
    add_images(slot_of[2 * steps], c_1, d_1, acc)

    def y_of(high, sign, low):
        i = high * 8 + low
        return jnp.where(sign == 0, 16 + i, jnp.where(i == 0, 0, 16 - i))

    def x_of(j):
        return jnp.where(j < 16, j + 16, jnp.where(j == 16, 0, 32 - j))

    def exact(a, b, dims):
        return lax.dot_general(
            a, b, (dims, ((), ())), precision=lax.Precision.HIGHEST,
            preferred_element_type=jnp.float32,
        )

    pick_x = (x_of(iota((SUB, SUB), 0)) == iota((SUB, SUB), 1)).astype(jnp.float32)
    place = iota((SUB, 2 * BLK), 1)
    pick_y = (
        y_of(lax.shift_right_logical(place, 7), lax.shift_right_logical(place, 3) & 1, place & 7)
        == iota((SUB, 2 * BLK), 0)
    ).astype(jnp.float32)
    weight = exact(exact(pick_x, taper[...], ((1,), (1,))), pick_y, ((1,), (0,))) * (
        1.0 / math.sqrt(BLK)
    )

    row, col = iota((BLK, BLK), 0), iota((BLK, BLK), 1)
    turn = (x_of(row & (SUB - 1)) * (col & (SUB - 1))) & (SUB - 1)
    sx, cx = sincos_turns(turn.astype(jnp.float32) * (1.0 / SUB))
    same = lax.shift_right_logical(row, 5) == lax.shift_right_logical(col, 5)
    w_hi, w_lo = split(
        jnp.concatenate(
            [jnp.where(same, cx * (1.0 / SUB), 0.0), jnp.where(same, sx * (-1.0 / SUB), 0.0)], 1
        )
    )
    w_all = jnp.concatenate([w_hi, w_hi, w_lo], 0)
    lane = iota((SUB, BLK), 1)
    even_lane = (lane & 8) == 0
    lane16 = iota((16, BLK), 1)
    first_row = iota((8, BLK), 0) == 0
    turn_sign = jnp.where(lane16 < BLK // 2, 1.0, -1.0)
    edge = iota((16, BLK), 0) == 0

    for q in range(OWNED // 4):
        rows = []
        for s in range(4 * q, 4 * q + 4):
            both = []
            for t in range(2):
                a = acc[s, t]
                y = jnp.where(even_lane, a + pltpu.roll(a, BLK - 8, 1), pltpu.roll(a, 8, 1) - a)
                if t == 0:
                    y = jnp.where((lane & 7) == 0, a, y)
                cos_x, sin_x = y[0:16, :], y[16:32, :]
                turned = pltpu.roll(sin_x, BLK // 2, 1) * turn_sign
                plus = jnp.where(edge, cos_x, cos_x + turned)
                minus = jnp.where(edge, sin_x, cos_x - turned)
                both.append(jnp.concatenate([plus, minus], 0))
            rows.append(jnp.concatenate(both, 1) * weight)
        x_hi, x_lo = split(jnp.transpose(jnp.concatenate(rows, 0)))
        z = dot_nn(jnp.concatenate([x_hi, x_lo, x_hi], 1), w_all)
        rights = [offset[1, 4 * q + j] for j in range(4)]
        inside = [(lane16 >= right) & (lane16 < right + SUB) for right in rights]
        for t in range(2):
            for p in range(4):
                re = z[t * 128 + p * 16 : t * 128 + p * 16 + 16, :]
                im = z[t * 128 + p * 16 + 64 : t * 128 + p * 16 + 80, :]
                re, im = re[:, 0:BLK] - im[:, BLK:], re[:, BLK:] + im[:, 0:BLK]
                up, down = (re[:8], im[:8]), (re[8:], im[8:])
                tops = [up[0] + down[0], up[1] + down[1]]
                lows = [up[1] - down[1], down[0] - up[0]]
                if t == 0:
                    tops = [jnp.where(first_row, x, y) for x, y in zip(up, tops)]
                    lows = [jnp.where(first_row, x, y) for x, y in zip(down, lows)]
                joined = [jnp.concatenate(pair, 0) for pair in zip(tops, lows)]
                for j in range(4):
                    at = (4 * q + j) * SUB + t * 16
                    shift = (rights[j] + (BLK - SUB * j)) & (BLK - 1)
                    for part in range(2):
                        spread[p, at : at + 16, part * BLK : part * BLK + BLK] = jnp.where(
                            inside[j], pltpu.roll(joined[part], shift, 1), 0.0
                        )

    lane = iota((1, OWNED * SUB), 1)
    corner = jnp.zeros((1, OWNED * SUB), jnp.int32)
    for s in range(OWNED):
        corner = jnp.where(lax.shift_right_logical(lane, 5) == s, offset[0, s], corner)
    high = (lax.shift_right_logical(lane, 4) & 1) * 8 + (lane & 7)
    low_half = (lane & 8) == 0
    yy = jnp.where(low_half | (high > 0), 16 + high, 0)
    use_cos = low_half | (high == 0)

    def turned(at, y):
        return sincos_turns(((at * y) & (SUB - 1)).astype(jnp.float32) * (1.0 / SUB))

    s_at, c_at = turned(iota((TILE, BLK), 0), jnp.broadcast_to(yy[:, 0:BLK], (TILE, BLK)))
    use_cos = jnp.broadcast_to(use_cos[:, 0:BLK], (TILE, BLK))
    first = jnp.concatenate([jnp.where(use_cos, c_at, s_at)] * 4, 1)
    second = jnp.concatenate([jnp.where(use_cos, s_at, -c_at)] * 4, 1)
    s_corner, c_corner = turned(corner, yy)
    ky = iota((TILE, OWNED * SUB), 0) - corner
    inside = (ky >= 0) & (ky < SUB)
    h_hi, h_lo = split(jnp.where(inside, first * c_corner + second * s_corner, 0.0))
    h_both = jnp.concatenate([h_hi, h_lo], 0)
    for p in range(4):
        b_hi, b_lo = split(spread[p])
        o = dot_nn(h_both, b_hi)
        o = o[0:TILE, :] + o[TILE:, :] + dot_nn(h_hi, b_lo)
        tile[p] = o[:, 0:BLK]
        tile[p + 4] = o[:, BLK:]


def grid_tile(info, offset, taper, got):
    smem = pl.BlockSpec(memory_space=pltpu.SMEM)
    vmem = pl.BlockSpec(memory_space=pltpu.VMEM)
    f32 = jnp.float32
    factors = [
        pltpu.VMEM((N_TRIG, BLK), f32),
        pltpu.VMEM((N_TRIG, BLK), f32),
        pltpu.VMEM((C_ROWS[2], 2 * BLK), f32),
        pltpu.VMEM((256, BLK), f32),
    ]
    return pl.pallas_call(
        grid_kernel,
        out_shape=jax.ShapeDtypeStruct((8, TILE, TILE), f32),
        in_specs=[smem, smem, vmem, vmem],
        out_specs=vmem,
        scratch_shapes=[
            pltpu.SMEM((OWNED,), jnp.int32),
            pltpu.SMEM((MAX_GROUPS + 2,), jnp.int32),
            pltpu.VMEM((MAX_GROUPS, 16, BLK), f32),
            pltpu.VMEM((N_PHASE, BLK), f32),
            *factors,
            *factors,
            pltpu.VMEM((OWNED + 1, 2, SUB, BLK), f32),
            pltpu.VMEM((4, OWNED * SUB, 2 * BLK), f32),
        ],
        compiler_params=pltpu.CompilerParams(vmem_limit_bytes=62 * 1024 * 1024),
        name="grid_tile",
    )(info, offset, taper, got)


FAR_FIRST = (6, 5, 7, 2, 4, 1, 3)


def near(me, k, sign):
    return (me // 4 + k // 4) % 2 * 4 + (me + 4 + sign * (k % 4)) % 4


def gather_kernel(tile, recv, send_sem, recv_sem):
    me = lax.axis_index("freq")
    own = pltpu.make_async_copy(
        tile.at[:, pl.ds(pl.multiple_of(me * (TILE // GROUPS), 8), TILE // GROUPS)],
        recv.at[0],
        recv_sem.at[0],
    )
    own.start()
    barrier = pltpu.get_barrier_semaphore()
    for k in FAR_FIRST:
        pl.semaphore_signal(
            barrier,
            inc=1,
            device_id={"freq": near(me, k, 1)},
            device_id_type=pl.DeviceIdType.MESH,
        )
    pl.semaphore_wait(barrier, GROUPS - 1)
    strip = TILE // GROUPS
    copies = []
    for k in FAR_FIRST:
        peer = near(me, k, 1)
        copy = pltpu.make_async_remote_copy(
            src_ref=tile.at[:, pl.ds(pl.multiple_of(peer * strip, 8), strip)],
            dst_ref=recv.at[k],
            send_sem=send_sem.at[k],
            recv_sem=recv_sem.at[k],
            device_id={"freq": peer},
            device_id_type=pl.DeviceIdType.MESH,
        )
        copy.start()
        copies.append(copy)
    own.wait()
    for copy in copies:
        copy.wait_recv()
    for copy in copies:
        copy.wait_send()


def sum_kernel(parts, out):
    value = parts[0]
    for k in range(1, GROUPS):
        value = value + parts[k]
    for c in range(8):
        out[:, c, :] = value[c]


def sum_over_freq(tile):
    strip = TILE // GROUPS
    anywhere = pl.BlockSpec(memory_space=pl.ANY)
    vmem = pl.BlockSpec(memory_space=pltpu.VMEM)
    parts = pl.pallas_call(
        gather_kernel,
        out_shape=jax.ShapeDtypeStruct((GROUPS, 8, strip, TILE), jnp.float32),
        in_specs=[anywhere],
        out_specs=anywhere,
        scratch_shapes=[
            pltpu.SemaphoreType.DMA((GROUPS,)),
            pltpu.SemaphoreType.DMA((GROUPS,)),
        ],
        compiler_params=pltpu.CompilerParams(
            collective_id=1, has_side_effects=True, vmem_limit_bytes=62 * 1024 * 1024
        ),
        name="gather_over_freq",
    )(tile)
    return pl.pallas_call(
        sum_kernel,
        out_shape=jax.ShapeDtypeStruct((strip, 8, TILE), jnp.float32),
        in_specs=[vmem],
        out_specs=vmem,
        compiler_params=pltpu.CompilerParams(vmem_limit_bytes=62 * 1024 * 1024),
        name="sum_over_freq",
    )(parts)


def shards(
    visibility, uv_offset, w_offset, taper, row_count, block_owner, block_slot, subgrid_offset
):
    got, info = exchange(
        block_owner[:, :, 0], block_slot, row_count, visibility[0], uv_offset[0], w_offset[0]
    )
    return sum_over_freq(grid_tile(info, subgrid_offset.T, taper, got))


def solution(mesh):
    placed = (
        P("freq", "uv", None, None),
        P("freq", "uv", None, None),
        P("freq", "uv", None),
        P(),
        P("freq", "uv"),
        P("freq", "uv", None),
        P("freq", "uv"),
        P("uv", None),
    )
    return jax.shard_map(
        shards, mesh=mesh, in_specs=placed, out_specs=P(("uv", "freq"), None, None), check_vma=False
    )
```
